256 devices in a mesh: lon: 16 (over x_lo, z), lat: 8 (over y, core), ens: 2 (over x_hi).
Axes of the slice: x: 4 (x_hi: 2, x_lo: 2; x = x_hi * 2 + x_lo), y: 4, z: 8, core: 2. Of those that a mesh axis runs over, the one named last changes fastest.
Arguments:
- temp: float32 [2, 12, 128, 2048], P('ens', None, 'lat', 'lon'), may hold values from -6 to 6
- height: float32 [2, 128, 2048], P('ens', 'lat', 'lon'), may hold values from -6 to 6
- flow: float32 [2, 2, 128, 2048], P('ens', None, 'lat', 'lon'), may hold values from -6 to 6
- land_sea: int32 [128, 2048], P('lat', 'lon'), may hold values 0 or 1
- fold: int32 [2048], replicated, may hold values from 0 to 2047, as said below
- w_first: bfloat16 [16, 99], replicated, may hold values from -0.625 to 0.625
- w_second: bfloat16 [16, 144], replicated, may hold values from -0.5 to 0.5
- w_third: bfloat16 [10, 144], replicated, may hold values from -0.5 to 0.5
- temp_bar: float32 [2, 12, 128, 2048], P('ens', None, 'lat', 'lon'), may hold values from -6 to 6
- height_bar: float32 [2, 128, 2048], P('ens', 'lat', 'lon'), may hold values from -6 to 6
- flow_bar: float32 [2, 2, 128, 2048], P('ens', None, 'lat', 'lon'), may hold values from -6 to 6
Outputs:
- temp_grad: float32 [2, 12, 128, 2048], P('ens', None, 'lat', 'lon')
- height_grad: float32 [2, 128, 2048], P('ens', 'lat', 'lon')
- flow_grad: float32 [2, 2, 128, 2048], P('ens', None, 'lat', 'lon')
- first_grad: float32 [16, 99], replicated
- second_grad: float32 [16, 144], replicated
- third_grad: float32 [10, 144], replicated
The draws below stay inside these ranges and needn't reach their ends.
Inputs may be any that keep to these rules, and one draw needn't show every extreme that they name: fold[i] = (s - 1 - i) mod 2048 for one s of each draw, so that fold[fold[i]] = i.
All inputs are finite; a program needn't handle non-finite values. No bound on the sum of `land_sea` on one device may be relied on, other than what follows from the above.
Results may differ from the reference program's by a relative error of at most 0.008.
Values sent between devices are 32-bit elements; how exact they have to be, the bound alone decides.
A program may use at most 128 MiB of HBM per device.

```python
import math
import jax
import jax.numpy as jnp
from jax import lax

LEV = 12
CL = 10
CH = 16
SUB = 4
LAYERS = 3
MEMBERS = 2
NLAT = 128
NLON = 2048


def draw_fold(key, part):
    key = jax.random.fold_in(key, 11)
    shift = jax.random.randint(key, (), 0, NLON, dtype=jnp.int32)
    columns = jnp.arange(NLON, dtype=jnp.int32)
    return (shift - 1 - columns) % NLON


def with_ends(array, rng, smallest, high):
    spot = [jax.random.randint(jax.random.fold_in(rng, axis), (), 0, length) for axis, length in enumerate(array.shape)]
    main_axis = array.shape.index(max(array.shape))
    neighbour = spot[:main_axis] + [(spot[main_axis] + 1) % array.shape[main_axis]] + spot[main_axis + 1:]
    return array.at[tuple(spot)].set(smallest).at[tuple(neighbour)].set(high)


def block_levels(own_key, dims, pieces, least, largest):
    def one(axis_at, blocks):
        heights = jax.random.uniform(jax.random.fold_in(jax.random.fold_in(own_key, 6), axis_at), (blocks,), jnp.float32, least / len(pieces), largest / len(pieces))
        return jnp.repeat(jnp.exp(heights), dims[axis_at] // blocks).reshape((-1,) + (1,) * (len(dims) - axis_at - 1))

    gain = one(*pieces[0])
    for cut in pieces[1:]:
        gain = gain * one(*cut)
    return gain


def noise(own_key, shape, scale, most, cuts=(), kind=jnp.bfloat16):
    result = jax.random.normal(own_key, shape, jnp.float32) * scale
    if len(cuts) > 0:
        result = block_levels(own_key, shape, cuts, -0.22, 0.18) * result
    return jnp.clip(result, min=-most, max=most).astype(kind)


def setup_inputs(seed: int = 0) -> dict:
    key_list = jax.random.split(jax.random.key(seed), 12)
    temp = noise(key_list[0], (MEMBERS, LEV, NLAT, NLON), 1.0, 6.0, ((0, 2), (2, 8), (3, 16)), jnp.float32)
    height = noise(key_list[1], (MEMBERS, NLAT, NLON), 1.0, 6.0, ((0, 2), (1, 8), (2, 16)), jnp.float32)
    flow = noise(key_list[2], (MEMBERS, 2, NLAT, NLON), 1.0, 6.0, ((0, 2), (2, 8), (3, 16)), jnp.float32)
    land_sea = with_ends((jax.random.randint(key_list[3], (NLAT, NLON), 0, 5) < 4).astype(jnp.int32), jax.random.fold_in(key_list[3], 1), 0, 1)
    fold = draw_fold(jax.random.fold_in(key_list[11], 71), 0)
    w_first = noise(key_list[5], (CH, 9 * (CL + 1)), (9 * (CL + 1)) ** -0.5, 0.625)
    w_second = noise(key_list[6], (CH, 9 * CH), (9 * CH) ** -0.5, 0.5)
    w_third = noise(key_list[7], (CL, 9 * CH), (9 * CH) ** -0.5, 0.5)
    temp_bar = noise(key_list[8], (MEMBERS, LEV, NLAT, NLON), 1.0, 6.0, ((0, 2), (2, 8), (3, 16)), jnp.float32)
    height_bar = noise(key_list[9], (MEMBERS, NLAT, NLON), 1.0, 6.0, ((0, 2), (1, 8), (2, 16)), jnp.float32)
    flow_bar = noise(key_list[10], (MEMBERS, 2, NLAT, NLON), 1.0, 6.0, ((0, 2), (2, 8), (3, 16)), jnp.float32)
    return {"temp": temp, "height": height, "flow": flow, "land_sea": land_sea, "fold": fold, "w_first": w_first, "w_second": w_second, "w_third": w_third, "temp_bar": temp_bar, "height_bar": height_bar, "flow_bar": flow_bar}


gravity = 0.3
drag_rate = 0.05
coriolis = 0.2
diffusion = 0.1
advection = 0.1
closure_gain = 0.5

def crop(field, width):
    if width == 0:
        return field
    return field[..., width:field.shape[-2] - width, width:field.shape[-1] - width]

def physics(tracer_ext, height, east, north, wet):
    for index in range(SUB):
        wet = crop(wet, 1)
        spread = 0.5 * (east[1:-1, 2:] - east[1:-1, :-2]) + 0.5 * (north[2:, 1:-1] - north[:-2, 1:-1])
        height = wet * (crop(height, 1) - gravity * spread)
        wet = crop(wet, 1)
        east_old = crop(east, 2)
        north_old = crop(north, 2)
        slope_east = 0.5 * (height[1:-1, 2:] - height[1:-1, :-2])
        slope_north = 0.5 * (height[2:, 1:-1] - height[:-2, 1:-1])
        east = wet * ((1.0 - drag_rate) * east_old - gravity * slope_east + coriolis * north_old)
        north = wet * ((1.0 - drag_rate) * north_old - gravity * slope_north - coriolis * east_old)
        height = crop(height, 1)
    near = crop(tracer_ext, LAYERS - 1)
    centre = near[:, 1:-1, 1:-1]
    laplace = near[:, 2:, 1:-1] + near[:, :-2, 1:-1] + near[:, 1:-1, 2:] + near[:, 1:-1, :-2] - 4.0 * centre
    slope_east = 0.5 * (near[:, 1:-1, 2:] - near[:, 1:-1, :-2])
    slope_north = 0.5 * (near[:, 2:, 1:-1] - near[:, :-2, 1:-1])
    east_inner = crop(east, LAYERS)
    north_inner = crop(north, LAYERS)
    wet_inner = crop(wet, LAYERS)
    moved = centre + wet_inner * (diffusion * laplace - advection * (east_inner * slope_east + north_inner * slope_north))
    return (moved, height, east_inner, north_inner)

def patches(field):
    channels = field.shape[0]
    row_count = field.shape[1] - 2
    column_count = field.shape[2] - 2
    parts = [field[:, down:down + row_count, across:across + column_count] for down in range(3) for across in range(3)]
    return (jnp.concatenate(parts, axis=0).reshape(9 * channels, row_count * column_count), row_count, column_count)

def unpatch(grads, channels, row_count, column_count):
    grads = grads.reshape(9, channels, row_count, column_count)
    total = jnp.zeros((channels, row_count + 2, column_count + 2), jnp.float32)
    for down in range(3):
        for across in range(3):
            total = total + jnp.pad(grads[3 * down + across], ((0, 0), (down, 2 - down), (across, 2 - across)))
    return total

def contract_last(left, right):
    return lax.dot_general(left, right, (((1,), (1,)), ((), ())), preferred_element_type=jnp.float32)

def contract_first(left, right):
    return lax.dot_general(left, right, (((0,), (0,)), ((), ())), preferred_element_type=jnp.float32)

def closure_forward(inputs, weights):
    w_first, w_second, w_third = weights
    first, rows_one, columns_one = patches(inputs)
    act_one = jnp.tanh(jnp.dot(w_first, first, preferred_element_type=jnp.float32))
    hidden_one = act_one.astype(jnp.bfloat16).reshape(act_one.shape[0], rows_one, columns_one)
    second, rows_two, columns_two = patches(hidden_one)
    act_two = jnp.tanh(jnp.dot(w_second, second, preferred_element_type=jnp.float32))
    hidden_two = act_two.astype(jnp.bfloat16).reshape(act_two.shape[0], rows_two, columns_two)
    third, rows_three, columns_three = patches(hidden_two)
    extents = (rows_one, columns_one, rows_two, columns_two, rows_three, columns_three)
    return (first, act_one, second, act_two, third, extents)

def closure_backward(grad_tendency, saved, weights):
    w_first, w_second, w_third = weights
    first, act_one, second, act_two, third, extents = saved
    rows_one, columns_one, rows_two, columns_two, rows_three, columns_three = extents
    grad_three = grad_tendency.astype(jnp.bfloat16)
    weight_three = contract_last(grad_three, third)
    back_three = unpatch(contract_first(w_third, grad_three), act_two.shape[0], rows_three, columns_three)
    grad_two = (back_three.reshape(act_two.shape) * (1.0 - act_two * act_two)).astype(jnp.bfloat16)
    weight_two = contract_last(grad_two, second)
    back_two = unpatch(contract_first(w_second, grad_two), act_one.shape[0], rows_two, columns_two)
    grad_one = (back_two.reshape(act_one.shape) * (1.0 - act_one * act_one)).astype(jnp.bfloat16)
    weight_one = contract_last(grad_one, first)
    back_one = unpatch(contract_first(w_first, grad_one), first.shape[0] // 9, rows_one, columns_one)
    return (back_one, (weight_one, weight_two, weight_three))

def local_adjoint(tracer_ext, height, east, north, wet, weights, temp_bar, height_bar, east_bar, north_bar):
    levels = temp_bar.shape[0]
    closed = weights[2].shape[0]

    def advance(tracer_in, height_in, east_in, north_in):
        return physics(tracer_in, height_in, east_in, north_in, wet)
    outputs, pull = jax.vjp(advance, tracer_ext, height, east, north)
    height_rim = outputs[1]
    inputs = jnp.concatenate([tracer_ext[:closed], height_rim[None]], axis=0).astype(jnp.bfloat16)
    saved = closure_forward(inputs, weights)
    wet_inner = crop(wet, (wet.shape[-1] - temp_bar.shape[-1]) // 2)
    grad_tendency = (closure_gain * wet_inner * temp_bar[:closed]).reshape(closed, -1)
    back_inputs, weight_grads = closure_backward(grad_tendency, saved, weights)
    height_rim_grad = back_inputs[closed] + jnp.pad(height_bar, LAYERS)
    tracer_grad, height_ext, east_ext, north_ext = pull((temp_bar, height_rim_grad, east_bar, north_bar))
    tracer_grad = tracer_grad + jnp.pad(back_inputs[:closed], ((0, levels - closed), (0, 0), (0, 0)))
    return (tracer_grad, height_ext, east_ext, north_ext, weight_grads)

def extend(field, width, sign, fold):
    lat_cells = field.shape[-2]
    lon_cells = field.shape[-1]
    span = jnp.arange(-width, lon_cells + width, dtype=jnp.int32) % lon_cells
    wide = jnp.take(field, span, axis=-1)
    top = jnp.flip(field[..., lat_cells - width:, :], axis=-2)
    north = sign * jnp.take(top, jnp.take(fold, span), axis=-1)
    return jnp.concatenate([jnp.zeros_like(north), wide, north], axis=-2)

def retract(grad_ext, field, width, sign, fold):
    unused, pull = jax.vjp(lambda source: extend(source, width, sign, fold), field)
    return pull(grad_ext)[0]

def reference(temp, height, flow, land_sea, fold, w_first, w_second, w_third, temp_bar, height_bar, flow_bar):
    rim = 2 * SUB + LAYERS
    weights = (w_first, w_second, w_third)
    wet = extend(land_sea.astype(jnp.float32), rim, 1.0, fold)
    temp_grads = []
    height_grads = []
    flow_grads = []
    weight_total = tuple((jnp.zeros(matrix.shape, jnp.float32) for matrix in weights))
    for member in range(MEMBERS):
        tracer_ext = extend(temp[member], LAYERS, 1.0, fold)
        height_ext = extend(height[member], rim, 1.0, fold)
        east_ext = extend(flow[member, 0], rim, -1.0, fold)
        north_ext = extend(flow[member, 1], rim, -1.0, fold)
        tracer_grad, height_back, east_back, north_back, weight_grads = local_adjoint(tracer_ext, height_ext, east_ext, north_ext, wet, weights, temp_bar[member], height_bar[member], flow_bar[member, 0], flow_bar[member, 1])
        temp_grads.append(retract(tracer_grad, temp[member], LAYERS, 1.0, fold))
        height_grads.append(retract(height_back, height[member], rim, 1.0, fold))
        flow_grads.append(jnp.stack([retract(east_back, flow[member, 0], rim, -1.0, fold), retract(north_back, flow[member, 1], rim, -1.0, fold)]))
        weight_total = jax.tree.map(jnp.add, weight_total, weight_grads)
    scale = 1.0 / math.sqrt(MEMBERS * NLAT * NLON)
    return (jnp.stack(temp_grads), jnp.stack(height_grads), jnp.stack(flow_grads), weight_total[0] * scale, weight_total[1] * scale, weight_total[2] * scale)
```

```python
import functools
import math

import jax
import jax.numpy as jnp
from jax import lax
from jax.experimental import pallas as pl
from jax.experimental.pallas import tpu as pltpu
from jax.sharding import PartitionSpec as P

MESH = pl.DeviceIdType.MESH
F32 = jnp.float32
BF16 = jnp.bfloat16

SUB = 4
LEV = 12
CL = 10
RIM = 11
TRIM = 3
HCH = 12
LANES = 128

gravity = 0.3
drag_rate = 0.05
coriolis = 0.2
diffusion = 0.1
advection = 0.1
closure_gain = 0.5


def lane_iota(rows):
    return lax.broadcasted_iota(jnp.int32, (rows, LANES), 1)


def east_of(x):
    a, b = (pltpu.roll(v, LANES - 1, 1) for v in x)
    edge = lane_iota(a.shape[0]) == LANES - 1
    return (jnp.where(edge, b, a), jnp.where(edge, a, b))


def west_of(x):
    a, b = (pltpu.roll(v, 1, 1) for v in x)
    edge = lane_iota(a.shape[0]) == 0
    return (jnp.where(edge, b, a), jnp.where(edge, a, b))


def north_of(x):
    return tuple(pltpu.roll(v, v.shape[0] - 1, 0) for v in x)


def south_of(x):
    return tuple(pltpu.roll(v, 1, 0) for v in x)


def lift(fn):
    return lambda *pairs: tuple(fn(*vs) for vs in zip(*pairs))


sub2 = lift(lambda u, v: u - v)


def step_forward(h, e, n, w):
    de = sub2(east_of(e), west_of(e))
    dn = sub2(north_of(n), south_of(n))
    h = lift(lambda w_, h_, a, b: w_ * (h_ - (0.5 * gravity) * (a + b)))(w, h, de, dn)
    se = sub2(east_of(h), west_of(h))
    sn = sub2(north_of(h), south_of(h))
    keep = 1.0 - drag_rate
    e_new = lift(lambda w_, e_, n_, s: w_ * (keep * e_ - (0.5 * gravity) * s + coriolis * n_))(w, e, n, se)
    n_new = lift(lambda w_, e_, n_, s: w_ * (keep * n_ - (0.5 * gravity) * s - coriolis * e_))(w, e, n, sn)
    return h, e_new, n_new


def step_adjoint(h, e, n, w):
    we = lift(lambda a, b: a * b)(w, e)
    wn = lift(lambda a, b: a * b)(w, n)
    de = sub2(east_of(we), west_of(we))
    dn = sub2(north_of(wn), south_of(wn))
    hw = lift(lambda w_, h_, a, b: w_ * (h_ + (0.5 * gravity) * (a + b)))(w, h, de, dn)
    se = sub2(east_of(hw), west_of(hw))
    sn = sub2(north_of(hw), south_of(hw))
    keep = 1.0 - drag_rate
    e_new = lift(lambda a, b, s: keep * a - coriolis * b + (0.5 * gravity) * s)(we, wn, se)
    n_new = lift(lambda a, b, s: keep * b + coriolis * a + (0.5 * gravity) * s)(we, wn, sn)
    return hw, e_new, n_new


def slot_mask(rows, width, count, offset):
    lane = lane_iota(rows)
    mask = None
    for slot in range(count):
        start = 2 * width * slot + offset
        here = (lane >= start) & (lane < start + width)
        mask = here if mask is None else mask | here
    return mask


def pack_edges(fields, width):
    lane = lane_iota(fields[0].shape[0])
    out = jnp.zeros_like(fields[0])
    for slot, field in enumerate(fields):
        start = 2 * width * slot
        rolled = pltpu.roll(field, (start + width) % LANES, 1)
        out = jnp.where((lane >= start) & (lane < start + 2 * width), rolled, out)
    return out


def unpack_edge(packed, width, slot):
    lane = lane_iota(packed.shape[0])
    rolled = pltpu.roll(packed, (-width - 2 * width * slot) % LANES, 1)
    return jnp.where((lane < width) | (lane >= LANES - width), rolled, 0.0)


def split_bf16(x):
    high = x.astype(BF16)
    rest = x - high.astype(F32)
    middle = rest.astype(BF16)
    low = (rest - middle.astype(F32)).astype(BF16)
    return jnp.concatenate([high, middle, low], axis=0)


def permute_columns(x, select):
    rows = x.shape[0]
    y = jnp.dot(split_bf16(x), select, preferred_element_type=F32)
    return (y[2 * rows :] + y[rows : 2 * rows]) + y[:rows]


def store_shifted(ref, row, pair):
    for dx, shifted in enumerate((west_of(pair), pair, east_of(pair))):
        for tile in range(2):
            ref[tile, row, 16 * dx : 16 * dx + 16, :] = shifted[tile].astype(BF16)


def patch(ref, row):
    return jnp.concatenate([ref[tile, row : row + 3].reshape(144, LANES) for tile in range(2)], axis=1)


def conv_row(weight, ref, row):
    y = jnp.dot(weight, patch(ref, row), preferred_element_type=F32)
    return (y[:, :LANES], y[:, LANES:])


def contract(left, right):
    return lax.dot_general(left, right, (((1,), (1,)), ((), ())), preferred_element_type=F32)


def kernel(
    sizes,
    temp,
    height,
    flow,
    land_sea,
    fold,
    w_first,
    w_second,
    w_third,
    temp_bar,
    height_bar,
    flow_bar,
    temp_out,
    height_out,
    flow_out,
    first_out,
    second_out,
    third_out,
    surf,
    trac,
    inputs,
    wet_i,
    bar_t,
    bar_h,
    bar_f,
    fold_s,
    w1_raw,
    w2_raw,
    w3_raw,
    w_rows,
    w_flip,
    msg_out,
    msg_in,
    fold_surf,
    fold_trac,
    g3_rows,
    xs1,
    xs2,
    xs3,
    gs1,
    gs2,
    gs3,
    act1,
    act2,
    back,
    sg,
    tg,
    back_out,
    back_in,
    back_surf,
    back_trac,
    unfold_surf,
    unfold_trac,
    wsum,
    rs_in,
    part_in,
    full,
    load_sem,
    f_send,
    f_recv,
    m_send,
    m_recv,
    fold_send,
    fold_recv,
    b_send,
    b_recv,
    bm_send,
    bm_recv,
    unfold_send,
    unfold_recv,
    ar_send,
    ar_recv,
):
    nlon, nlat, nens = sizes
    lon, lat, ens = lax.axis_index("lon"), lax.axis_index("lat"), lax.axis_index("ens")
    top = nlat - 1
    left, right = lax.rem(lon + nlon - 1, nlon), lax.rem(lon + 1, nlon)
    group = nlat * nens
    place = ens * nlat + lat
    chunk = 64 // nlon

    def remote(src, dst, send, recv, **device):
        return pltpu.make_async_remote_copy(
            src_ref=src, dst_ref=dst, send_sem=send, recv_sem=recv, device_id=device, device_id_type=MESH
        )

    barrier = pltpu.get_barrier_semaphore()

    def greet(**device):
        pl.semaphore_signal(barrier, inc=1, device_id=device, device_id_type=MESH)

    for k in range(1, nlon):
        greet(lon=lax.rem(lon + k, nlon))
    for k in range(1, group):
        other = lax.rem(place + k, group)
        greet(lat=lax.rem(other, nlat), ens=other // nlat)

    @pl.when(lat > 0)
    def _():
        greet(lon=left, lat=lat - 1)
        greet(lon=right, lat=lat - 1)

    @pl.when(lat < top)
    def _():
        greet(lon=left, lat=lat + 1)
        greet(lon=right, lat=lat + 1)

    loads = [
        (temp.at[0], trac.at[0, :, 8:24, :]),
        (height.at[0], surf.at[0, 0, 16:32, :]),
        (flow.at[0], surf.at[0, 1:3, 16:32, :]),
        (land_sea, wet_i),
        (fold, fold_s),
        (w_first, w1_raw),
        (w_second, w2_raw),
        (w_third, w3_raw),
        (temp_bar.at[0], bar_t),
        (height_bar.at[0], bar_h),
        (flow_bar.at[0], bar_f),
    ]
    loads = [pltpu.make_async_copy(src, dst, load_sem.at[k]) for k, (src, dst) in enumerate(loads)]
    for load in loads:
        load.start()

    inputs[:, 32 * (HCH + 1) :, :] = jnp.zeros((2, 32 * (15 - HCH), LANES), F32)
    for ref, rows in ((gs3, 20), (gs2, 22), (gs1, 24)):
        for tile in range(2):
            for row in (0, 1, rows - 2, rows - 1):
                ref[tile, row] = jnp.zeros((48, LANES), BF16)
    back[...] = jnp.zeros_like(back)
    fold_surf[lon, 40:48, :] = jnp.zeros((8, LANES), F32)
    fold_trac[lon, 32:40, :] = jnp.zeros((8, LANES), F32)
    unfold_surf[lon, 32:40, :] = jnp.zeros((8, LANES), F32)
    unfold_trac[lon, 32:40, :] = jnp.zeros((8, LANES), F32)

    @pl.when(lat == 0)
    def _():
        surf[:, :, 0:16, :] = jnp.zeros((2, 4, 16, LANES), F32)
        trac[:, :, 0:8, :] = jnp.zeros((2, LEV, 8, LANES), F32)
        back_in[:, 0] = jnp.zeros((2, 2, 16, LANES), F32)
        back_surf[0] = jnp.zeros((3, 16, LANES), F32)
        back_trac[0] = jnp.zeros((LEV, 8, LANES), F32)

    @pl.when(lat == top)
    def _():
        surf[:, :, 32:48, :] = jnp.zeros((2, 4, 16, LANES), F32)
        trac[:, :, 24:32, :] = jnp.zeros((2, LEV, 8, LANES), F32)
        back_in[:, 2] = jnp.zeros((2, 2, 16, LANES), F32)
        back_surf[1] = jnp.zeros((3, 16, LANES), F32)
        back_trac[1] = jnp.zeros((LEV, 8, LANES), F32)

    for k in (1, 2, 3, 0):
        loads[k].wait()
    surf[0, 3, 16:32, :] = wet_i[...].astype(F32)
    msg_out[0] = pack_edges([surf[0, f, 16:32, :] for f in range(4)], RIM)
    msg_out[1] = pack_edges([trac[0, c, 8:24, :] for c in range(LEV)], TRIM)

    def lat_copies(up):
        to = 1 if up else -1
        rows_s = slice(0, 16) if up else slice(32, 48)
        rows_t = (slice(16, 24), slice(0, 8)) if up else (slice(8, 16), slice(24, 32))
        slot = 0 if up else 2
        return (
            remote(surf.at[0, :, 16:32, :], surf.at[0, :, rows_s, :], f_send.at[slot], f_recv.at[slot], lat=lat + to),
            remote(
                trac.at[0, :, rows_t[0], :],
                trac.at[0, :, rows_t[1], :],
                f_send.at[slot + 1],
                f_recv.at[slot + 1],
                lat=lat + to,
            ),
        )

    def edge_copy(side, shift):
        slot = 3 * side + 1 - shift
        return remote(
            msg_out, msg_in.at[side, 1 - shift], m_send.at[slot], m_recv.at[slot], lon=(right, left)[side], lat=lat + shift
        )

    def fold_copies(k):
        peer = lax.rem(lon + k, nlon)
        return (
            remote(fold_surf.at[lon], fold_surf.at[lon], fold_send.at[0, k], fold_recv.at[0, k], lon=peer),
            remote(fold_trac.at[lon], fold_trac.at[lon], fold_send.at[1, k], fold_recv.at[1, k], lon=peer),
        )

    def fold_arrivals(k):
        source = lax.rem(lon + nlon - k, nlon)
        return (
            remote(fold_surf.at[lon], fold_surf.at[source], fold_send.at[0, k], fold_recv.at[0, k], lon=source),
            remote(fold_trac.at[lon], fold_trac.at[source], fold_send.at[1, k], fold_recv.at[1, k], lon=source),
        )

    @pl.when(lat == top)
    def _():
        for f in range(4):
            for m in range(RIM):
                row = RIM * f + m
                fold_surf[lon, row : row + 1, :] = surf[0, f, 31 - m : 32 - m, :]
        for c in range(LEV):
            for m in range(TRIM):
                row = TRIM * c + m
                fold_trac[lon, row : row + 1, :] = trac[0, c, 23 - m : 24 - m, :]

    pl.semaphore_wait(
        barrier, (nlon - 1) + (group - 1) + 2 * (lat > 0).astype(jnp.int32) + 2 * (lat < top).astype(jnp.int32)
    )

    def for_lat(fn):
        pl.when(lat > 0)(functools.partial(fn, -1))
        fn(0)
        pl.when(lat < top)(functools.partial(fn, 1))

    @pl.when(lat == top)
    def _():
        for k in range(1, nlon):
            fold_copies(k)[0].start()

    def start_forward(shift):
        if shift:
            for copy in lat_copies(shift > 0):
                copy.start()
        for side in range(2):
            edge_copy(side, shift).start()

    for_lat(start_forward)

    @pl.when(lat == top)
    def _():
        for k in range(1, nlon):
            fold_copies(k)[1].start()

    for k in range(4, 11):
        loads[k].wait()
    raw1 = w1_raw[...].astype(F32)
    w_rows[...] = jnp.zeros_like(w_rows)
    for tap in range(9):
        w_rows[0, :, 16 * tap : 16 * tap + CL] = raw1[:, 11 * tap : 11 * tap + CL]
        w_rows[0, :, 16 * tap + HCH : 16 * tap + HCH + 1] = raw1[:, 11 * tap + CL : 11 * tap + CL + 1]
    w_rows[1, :, 0:144] = w2_raw[...].astype(F32)
    w_rows[2, 0:CL, 0:144] = w3_raw[...].astype(F32)
    for layer in range(3):
        first = jnp.transpose(w_rows[layer, :, 0:128])
        second = jnp.transpose(w_rows[layer, :, 128:256])
        for tap in range(9):
            block = second[0:16, :] if tap == 8 else first[16 * tap : 16 * tap + 16, :]
            w_flip[layer, :, 16 * (8 - tap) : 16 * (8 - tap) + 16] = block
    weight1 = w_rows[0, :, 0:144].astype(BF16)
    weight2 = w_rows[1, :, 0:144].astype(BF16)
    flip1, flip2, flip3 = (w_flip[layer].astype(BF16) for layer in range(3))

    wet_own = surf[0, 3, 16:32, :]
    g3_rows[16 * CL :, :] = jnp.zeros((16 * (16 - CL), LANES), F32)
    for c in range(CL):
        g3_rows[16 * c : 16 * c + 16, :] = closure_gain * wet_own * bar_t[c]
    for row in range(16):
        own = g3_rows[pl.ds(row, 16, stride=16), :]
        store_shifted(gs3, row + 2, (own, jnp.zeros_like(own)))

    shift_s = fold_s[0] + 1
    base = shift_s - 139 - LANES * lon + LANES * (2 * nlon)
    tile0 = base // LANES
    offset = shift_s - 1 - LANES * lon + LANES * (2 * nlon) - LANES * tile0

    def mirrored(ref):
        return jnp.concatenate([ref[lax.rem(tile0 + j, nlon)] for j in range(3)], axis=1)

    def mirror_matrix():
        source = lax.broadcasted_iota(jnp.int32, (3 * LANES, 2 * LANES), 0)
        column = lax.broadcasted_iota(jnp.int32, (3 * LANES, 2 * LANES), 1)
        column = jnp.where(column < LANES + LANES // 2, column, column - 2 * LANES)
        return jnp.where(source + column == offset, 1.0, 0.0).astype(BF16)

    left_s = slot_mask(16, RIM, 4, 0)
    left_t = slot_mask(16, TRIM, LEV, 0)

    def wait_forward(shift):
        k = shift + 1
        if shift:
            for copy in lat_copies(shift < 0):
                copy.wait_recv()
        for side in range(2):
            edge_copy(side, -shift).wait_recv()
        packed = jnp.where(left_s, msg_in[0, k, 0], msg_in[1, k, 0])
        for f in range(4):
            surf[1, f, 16 * k : 16 * k + 16, :] = unpack_edge(packed, RIM, f)
        packed = jnp.where(left_t, msg_in[0, k, 1], msg_in[1, k, 1])
        rows, at = ((slice(8, 16), 0), (slice(0, 16), 8), (slice(0, 8), 24))[k]
        packed = packed[rows]
        for c in range(LEV):
            trac[1, c, at : at + packed.shape[0], :] = unpack_edge(packed, TRIM, c)

    for_lat(wait_forward)

    @pl.when(lat == top)
    def _():
        select = mirror_matrix()
        for k in range(1, nlon):
            fold_arrivals(k)[0].wait_recv()
        ghost = permute_columns(mirrored(fold_surf), select)
        for f in range(4):
            rows = ghost[RIM * f : RIM * f + RIM]
            rows = -rows if f in (1, 2) else rows
            for tile in range(2):
                surf[tile, f, 32 : 32 + RIM, :] = rows[:, LANES * tile : LANES * tile + LANES]
        for k in range(1, nlon):
            fold_arrivals(k)[1].wait_recv()
        ghost = permute_columns(mirrored(fold_trac), select)
        for c in range(LEV):
            rows = ghost[TRIM * c : TRIM * c + TRIM]
            for tile in range(2):
                trac[tile, c, 24 : 24 + TRIM, :] = rows[:, LANES * tile : LANES * tile + LANES]

    h, e, n, wet = (tuple(surf[tile, f] for tile in range(2)) for f in range(4))
    for _ in range(SUB):
        h, e, n = step_forward(h, e, n, wet)
    new_e, new_n = e[0][16:32], n[0][16:32]

    for tile in range(2):
        for c in range(LEV):
            inputs[tile, 32 * c : 32 * c + 32, :] = trac[tile, c]
        inputs[tile, 32 * HCH : 32 * HCH + 32, :] = h[tile][8:40]
    for row in range(22):
        store_shifted(xs1, row, tuple(inputs[tile, pl.ds(5 + row, 16, stride=32), :] for tile in range(2)))
    for row in range(20):
        act = lift(jnp.tanh)(conv_row(weight1, xs1, row))
        for tile in range(2):
            act1[tile, row] = act[tile]
        store_shifted(xs2, row, act)
    for row in range(18):
        act = lift(jnp.tanh)(conv_row(weight2, xs2, row))
        for tile in range(2):
            act2[tile, row] = act[tile]
        store_shifted(xs3, row, act)

    def weight_sum(gs, xs, rows):
        total = jnp.zeros((16, 144), F32)
        for row in range(rows):
            grad = jnp.concatenate([gs[tile, row + 2, 16:32, :] for tile in range(2)], axis=1)
            total = total + contract(grad, patch(xs, row))
        return total

    def back_layer(weight, gs, act_ref, out, rows):
        for row in range(rows):
            grad = conv_row(weight, gs, row)
            act = tuple(act_ref[tile, row] for tile in range(2))
            store_shifted(out, row + 2, lift(lambda g, a: g * (1.0 - a * a))(grad, act))

    sum3 = weight_sum(gs3, xs3, 16)
    back_layer(flip3, gs3, act2, gs2, 18)
    sum2 = weight_sum(gs2, xs2, 18)
    back_layer(flip2, gs2, act1, gs1, 20)
    sum1 = weight_sum(gs1, xs1, 20)

    tail = jnp.concatenate([sum1[:, 128:144], sum2[:, 128:144], sum3[:, 128:144], jnp.zeros((16, 80), F32)], axis=1)
    rows = jnp.concatenate([sum1[:, :128], sum2[:, :128], sum3[:, :128], tail], axis=0)
    for k in range(nlon):
        wsum[k] = rows[chunk * k : chunk * k + chunk]

    def scatter_copy(k):
        peer = lax.rem(lon + k, nlon)
        return remote(wsum.at[peer], rs_in.at[k], ar_send.at[0, k], ar_recv.at[0, k], lon=peer)

    def part_copy(k):
        other = lax.rem(place + k, group)
        return remote(
            part_in.at[place],
            part_in.at[place],
            ar_send.at[1, k],
            ar_recv.at[1, k],
            lat=lax.rem(other, nlat),
            ens=other // nlat,
        )

    def part_arrival(k):
        other = lax.rem(place + group - k, group)
        return remote(
            part_in.at[place],
            part_in.at[other],
            ar_send.at[1, k],
            ar_recv.at[1, k],
            lat=lax.rem(other, nlat),
            ens=other // nlat,
        )

    def full_copy(k):
        peer = lax.rem(lon + k, nlon)
        return remote(full.at[lon], full.at[lon], ar_send.at[2, k], ar_recv.at[2, k], lon=peer)

    def full_arrival(k):
        source = lax.rem(lon + nlon - k, nlon)
        return remote(full.at[lon], full.at[source], ar_send.at[2, k], ar_recv.at[2, k], lon=source)

    for k in range(1, nlon):
        scatter_copy(k).start()

    for row in range(22):
        grad = conv_row(flip1, gs1, row)
        for tile in range(2):
            back[tile, pl.ds(5 + row, 16, stride=32), :] = grad[tile]

    lane16 = lane_iota(16)
    zero8 = jnp.zeros((8, LANES), F32)
    sum_e = jnp.zeros((16, LANES), F32)
    sum_n = jnp.zeros((16, LANES), F32)
    for c in range(LEV):
        bar = bar_t[c]
        wb = wet_own * bar
        own, halo = trac[0, c, 8:24, :], trac[1, c, 8:24, :]
        ahead = jnp.where(lane16 == LANES - 1, pltpu.roll(halo, LANES - 1, 1), pltpu.roll(own, LANES - 1, 1))
        behind = jnp.where(lane16 == 0, pltpu.roll(halo, 1, 1), pltpu.roll(own, 1, 1))
        sum_e = sum_e + wb * (ahead - behind)
        sum_n = sum_n + wb * (trac[0, c, 9:25, :] - trac[0, c, 7:23, :])
        qe = (0.5 * advection) * new_e * wb
        qn = (0.5 * advection) * new_n * wb
        wd = diffusion * wb
        up = pltpu.roll(wd + qe, LANES - 1, 1)
        down = pltpu.roll(wd - qe, 1, 1)
        middle = (
            bar - 4.0 * wd + jnp.where(lane16 < LANES - 1, up, 0.0) + jnp.where(lane16 > 0, down, 0.0)
        )
        side = jnp.where(lane16 == LANES - 1, up, jnp.where(lane16 == 0, down, 0.0))
        above = pltpu.roll(jnp.concatenate([zero8, wd + qn, zero8], axis=0), 31, 0)
        below = pltpu.roll(jnp.concatenate([zero8, wd - qn, zero8], axis=0), 1, 0)
        main = jnp.concatenate([zero8, middle, zero8], axis=0) + above + below
        side = jnp.concatenate([zero8, side, zero8], axis=0)
        if c < CL:
            main = main + back[0, 32 * c : 32 * c + 32, :]
            side = side + back[1, 32 * c : 32 * c + 32, :]
        tg[0, c] = main
        tg[1, c] = side

    def own_rows(x):
        zero16 = jnp.zeros((16, LANES), F32)
        return (jnp.concatenate([zero16, x, zero16], axis=0), jnp.zeros((48, LANES), F32))

    e = own_rows(bar_f[0] - (0.5 * advection) * sum_e)
    n = own_rows(bar_f[1] - (0.5 * advection) * sum_n)
    rim = tuple(jnp.concatenate([zero8, back[tile, 32 * HCH : 32 * HCH + 32, :], zero8], axis=0) for tile in range(2))
    h = lift(lambda a, b: a + b)(rim, own_rows(bar_h[...]))
    wet = tuple(surf[tile, 3] for tile in range(2))
    for index in range(SUB):
        h, e, n = step_adjoint(h, e, n, wet)
        if index == 1:
            for k in range(1, nlon):
                scatter_copy(k).wait_recv()
            part = wsum[lon]
            for k in range(1, nlon):
                part = part + rs_in[k]
            part_in[place] = part
            for k in range(1, group):
                part_copy(k).start()
    for f, pair in enumerate((h, e, n)):
        for tile in range(2):
            sg[tile, f] = pair[tile]

    for block in range(3):
        back_out[block, 0] = pack_edges([sg[1, f, 16 * block : 16 * block + 16, :] for f in range(3)], RIM)
        if block == 1:
            fields = [tg[1, c, 8:24, :] for c in range(LEV)]
        elif block == 0:
            fields = [jnp.concatenate([zero8, tg[1, c, 0:8, :]], axis=0) for c in range(LEV)]
        else:
            fields = [jnp.concatenate([tg[1, c, 24:32, :], zero8], axis=0) for c in range(LEV)]
        back_out[block, 1] = pack_edges(fields, TRIM)

    def lat_back(up):
        to = 1 if up else -1
        rows_s = slice(32, 48) if up else slice(0, 16)
        rows_t = slice(24, 32) if up else slice(0, 8)
        slot = 0 if up else 1
        return (
            remote(sg.at[0, :, rows_s, :], back_surf.at[slot], b_send.at[0, slot], b_recv.at[0, slot], lat=lat + to),
            remote(tg.at[0, :, rows_t, :], back_trac.at[slot], b_send.at[1, slot], b_recv.at[1, slot], lat=lat + to),
        )

    def edge_back(side, block, same=False):
        slot = 3 if same else 2 - block
        to = lat if same else lat + block - 1
        return remote(
            back_out.at[block],
            back_in.at[side, slot],
            bm_send.at[side, slot],
            bm_recv.at[side, slot],
            lon=(right, left)[side],
            lat=to,
        )

    @pl.when(lat == top)
    def _():
        for side in range(2):
            edge_back(side, 2, True).start()

    def start_back(shift):
        if shift:
            for copy in lat_back(shift > 0):
                copy.start()
        for side in range(2):
            edge_back(side, shift + 1).start()

    for_lat(start_back)

    right_s = slot_mask(16, RIM, 3, RIM)
    right_t = slot_mask(16, TRIM, LEV, TRIM)

    def unfold_copies(k):
        peer = lax.rem(lon + k, nlon)
        return (
            remote(unfold_surf.at[lon], unfold_surf.at[lon], unfold_send.at[0, k], unfold_recv.at[0, k], lon=peer),
            remote(unfold_trac.at[lon], unfold_trac.at[lon], unfold_send.at[1, k], unfold_recv.at[1, k], lon=peer),
        )

    def unfold_arrivals(k):
        source = lax.rem(lon + nlon - k, nlon)
        return (
            remote(unfold_surf.at[lon], unfold_surf.at[source], unfold_send.at[0, k], unfold_recv.at[0, k], lon=source),
            remote(unfold_trac.at[lon], unfold_trac.at[source], unfold_send.at[1, k], unfold_recv.at[1, k], lon=source),
        )

    @pl.when(lat == top)
    def _():
        for side in range(2):
            edge_back(side, 2, True).wait_recv()
        packed = jnp.where(right_s, back_in[0, 3, 0], back_in[1, 3, 0])
        for f in range(3):
            sg[0, f, 32:48, :] = sg[0, f, 32:48, :] + unpack_edge(packed, RIM, f)
            for j in range(RIM):
                row = RIM * f + j
                unfold_surf[lon, row : row + 1, :] = sg[0, f, 42 - j : 43 - j, :]
        packed = jnp.where(right_t, back_in[0, 3, 1], back_in[1, 3, 1])[0:8]
        for c in range(LEV):
            tg[0, c, 24:32, :] = tg[0, c, 24:32, :] + unpack_edge(packed, TRIM, c)
            for j in range(TRIM):
                row = TRIM * c + j
                unfold_trac[lon, row : row + 1, :] = tg[0, c, 26 - j : 27 - j, :]
        for k in range(1, nlon):
            for copy in unfold_copies(k):
                copy.start()

    for k in range(1, group):
        part_arrival(k).wait_recv()
    total = part_in[0]
    for k in range(1, group):
        total = total + part_in[k]
    full[lon] = total
    for k in range(1, nlon):
        full_copy(k).start()

    def wait_back(shift):
        if shift:
            for copy in lat_back(shift < 0):
                copy.wait_recv()
        for side in range(2):
            edge_back(side, 1 - shift).wait_recv()

    for_lat(wait_back)

    from_left = back_in[0, 0] + back_in[0, 1] + back_in[0, 2]
    from_right = back_in[1, 0] + back_in[1, 1] + back_in[1, 2]
    packed = jnp.where(right_s, from_left[0], from_right[0])
    for f in range(3):
        total = sg[0, f, 16:32, :] + back_surf[0, f] + back_surf[1, f] + unpack_edge(packed, RIM, f)
        if f == 0:
            height_out[0] = total
        else:
            flow_out[0, f - 1] = total
    packed = jnp.where(right_t, from_left[1], from_right[1])
    for c in range(LEV):
        ghosts = jnp.concatenate([back_trac[0, c], back_trac[1, c]], axis=0)
        temp_out[0, c] = tg[0, c, 8:24, :] + ghosts + unpack_edge(packed, TRIM, c)

    for k in range(1, nlon):
        full_arrival(k).wait_recv()
    scale = 1.0 / math.sqrt(nens * nlat * 16 * nlon * LANES)
    rows = jnp.concatenate([full[k] for k in range(nlon)], axis=0) * scale
    for layer, out in ((1, second_out), (2, third_out)):
        count = out.shape[0]
        out[:, 0:128] = rows[16 * layer : 16 * layer + count]
        out[:, 128:144] = rows[48 : 48 + count, 16 * layer : 16 * layer + 16]
    for tap in range(9):
        block = rows[48:64, 0:16] if tap == 8 else rows[0:16, 16 * tap : 16 * tap + 16]
        first_out[:, 11 * tap : 11 * tap + CL] = block[:, 0:CL]
        first_out[:, 11 * tap + CL : 11 * tap + CL + 1] = block[:, HCH : HCH + 1]

    @pl.when(lat == top)
    def _():
        for k in range(1, nlon):
            for copy in unfold_arrivals(k):
                copy.wait_recv()
        source = lax.broadcasted_iota(jnp.int32, (3 * LANES, LANES), 0)
        column = lax.broadcasted_iota(jnp.int32, (3 * LANES, LANES), 1)
        select = jnp.where(source + column == offset, 1.0, 0.0).astype(BF16)
        ghost = permute_columns(mirrored(unfold_surf), select)
        height_out[0, 16 - RIM : 16, :] = height_out[0, 16 - RIM : 16, :] + ghost[0:RIM]
        for f in (1, 2):
            flow_out[0, f - 1, 16 - RIM : 16, :] = (
                flow_out[0, f - 1, 16 - RIM : 16, :] - ghost[RIM * f : RIM * f + RIM]
            )
        ghost = permute_columns(mirrored(unfold_trac), select)
        for c in range(LEV):
            temp_out[0, c, 16 - TRIM : 16, :] = (
                temp_out[0, c, 16 - TRIM : 16, :] + ghost[TRIM * c : TRIM * c + TRIM]
            )

    def sent_forward(shift):
        if shift:
            for copy in lat_copies(shift > 0):
                copy.wait_send()
            for copy in lat_back(shift > 0):
                copy.wait_send()
        for side in range(2):
            edge_copy(side, shift).wait_send()
            edge_back(side, shift + 1).wait_send()

    for_lat(sent_forward)
    for k in range(1, nlon):
        scatter_copy(k).wait_send()
        full_copy(k).wait_send()
    for k in range(1, group):
        part_copy(k).wait_send()

    @pl.when(lat == top)
    def _():
        for side in range(2):
            edge_back(side, 2, True).wait_send()
        for k in range(1, nlon):
            for copy in fold_copies(k) + unfold_copies(k):
                copy.wait_send()


def solution(mesh):
    nlon, nlat, nens = (mesh.shape[axis] for axis in ("lon", "lat", "ens"))
    group = nlat * nens

    def local(temp, height, flow, land_sea, fold, w_first, w_second, w_third, temp_bar, height_bar, flow_bar):
        vmem = pltpu.VMEM
        dma = pltpu.SemaphoreType.DMA
        chunk = 64 // nlon
        scratch = [
            vmem((2, 4, 48, LANES), F32),
            vmem((2, LEV, 32, LANES), F32),
            vmem((2, 16 * 32, LANES), F32),
            vmem((16, LANES), jnp.int32),
            vmem((LEV, 16, LANES), F32),
            vmem((16, LANES), F32),
            vmem((2, 16, LANES), F32),
            pltpu.SMEM(fold.shape, jnp.int32),
            vmem(w_first.shape, BF16),
            vmem(w_second.shape, BF16),
            vmem(w_third.shape, BF16),
            vmem((3, 16, 256), F32),
            vmem((3, 16, 144), F32),
            vmem((2, 16, LANES), F32),
            vmem((2, 3, 2, 16, LANES), F32),
            vmem((nlon, 48, LANES), F32),
            vmem((nlon, 40, LANES), F32),
            vmem((16 * 16, LANES), F32),
            vmem((2, 22, 48, LANES), BF16),
            vmem((2, 20, 48, LANES), BF16),
            vmem((2, 18, 48, LANES), BF16),
            vmem((2, 24, 48, LANES), BF16),
            vmem((2, 22, 48, LANES), BF16),
            vmem((2, 20, 48, LANES), BF16),
            vmem((2, 20, 16, LANES), F32),
            vmem((2, 18, 16, LANES), F32),
            vmem((2, 16 * 32, LANES), F32),
            vmem((2, 3, 48, LANES), F32),
            vmem((2, LEV, 32, LANES), F32),
            vmem((3, 2, 16, LANES), F32),
            vmem((2, 4, 2, 16, LANES), F32),
            vmem((2, 3, 16, LANES), F32),
            vmem((2, LEV, 8, LANES), F32),
            vmem((nlon, 40, LANES), F32),
            vmem((nlon, 40, LANES), F32),
            vmem((nlon, chunk, LANES), F32),
            vmem((nlon, chunk, LANES), F32),
            vmem((group, chunk, LANES), F32),
            vmem((nlon, chunk, LANES), F32),
            dma((11,)),
            dma((4,)),
            dma((4,)),
            dma((6,)),
            dma((6,)),
            dma((2, nlon)),
            dma((2, nlon)),
            dma((2, 2)),
            dma((2, 2)),
            dma((2, 4)),
            dma((2, 4)),
            dma((2, nlon)),
            dma((2, nlon)),
            dma((3, max(nlon, group))),
            dma((3, max(nlon, group))),
        ]
        out_shape = (
            jax.ShapeDtypeStruct(temp.shape, F32),
            jax.ShapeDtypeStruct(height.shape, F32),
            jax.ShapeDtypeStruct(flow.shape, F32),
            jax.ShapeDtypeStruct(w_first.shape, F32),
            jax.ShapeDtypeStruct(w_second.shape, F32),
            jax.ShapeDtypeStruct(w_third.shape, F32),
        )
        return pl.pallas_call(
            functools.partial(kernel, (nlon, nlat, nens)),
            out_shape=out_shape,
            in_specs=[pl.BlockSpec(memory_space=pl.ANY)] * 11,
            out_specs=[pl.BlockSpec(memory_space=pltpu.VMEM)] * 6,
            scratch_shapes=scratch,
            compiler_params=pltpu.CompilerParams(
                collective_id=0, has_side_effects=True, vmem_limit_bytes=32 * 1024 * 1024
            ),
        )(temp, height, flow, land_sea, fold, w_first, w_second, w_third, temp_bar, height_bar, flow_bar)

    field = P("ens", None, "lat", "lon")
    plane = P("ens", "lat", "lon")
    return jax.shard_map(
        local,
        mesh=mesh,
        in_specs=(field, plane, field, P("lat", "lon"), P(), P(), P(), P(), field, plane, field),
        out_specs=(field, plane, field, P(), P(), P()),
        check_vma=False,
    )
```

```python
import functools
import math

import jax
import jax.numpy as jnp
from jax import lax
from jax.experimental import pallas as pl
from jax.experimental.pallas import tpu as pltpu
from jax.sharding import PartitionSpec as P

MESH = pl.DeviceIdType.MESH
F32 = jnp.float32
BF16 = jnp.bfloat16

SUB = 4
LEV = 12
CL = 10
RIM = 11
TRIM = 3
HCH = 12
LANES = 128

gravity = 0.3
drag_rate = 0.05
coriolis = 0.2
diffusion = 0.1
advection = 0.1
closure_gain = 0.5


def lane_iota(rows):
    return lax.broadcasted_iota(jnp.int32, (rows, LANES), 1)


def east_of(x):
    a, b = (pltpu.roll(v, LANES - 1, 1) for v in x)
    edge = lane_iota(a.shape[0]) == LANES - 1
    return (jnp.where(edge, b, a), jnp.where(edge, a, b))


def west_of(x):
    a, b = (pltpu.roll(v, 1, 1) for v in x)
    edge = lane_iota(a.shape[0]) == 0
    return (jnp.where(edge, b, a), jnp.where(edge, a, b))


def north_of(x):
    return tuple(pltpu.roll(v, v.shape[0] - 1, 0) for v in x)


def south_of(x):
    return tuple(pltpu.roll(v, 1, 0) for v in x)


def lift(fn):
    return lambda *pairs: tuple(fn(*vs) for vs in zip(*pairs))


sub2 = lift(lambda u, v: u - v)


def step_forward(h, e, n, w):
    de = sub2(east_of(e), west_of(e))
    dn = sub2(north_of(n), south_of(n))
    h = lift(lambda w_, h_, a, b: w_ * (h_ - (0.5 * gravity) * (a + b)))(w, h, de, dn)
    se = sub2(east_of(h), west_of(h))
    sn = sub2(north_of(h), south_of(h))
    keep = 1.0 - drag_rate
    e_new = lift(lambda w_, e_, n_, s: w_ * (keep * e_ - (0.5 * gravity) * s + coriolis * n_))(w, e, n, se)
    n_new = lift(lambda w_, e_, n_, s: w_ * (keep * n_ - (0.5 * gravity) * s - coriolis * e_))(w, e, n, sn)
    return h, e_new, n_new


def step_adjoint(h, e, n, w):
    we = lift(lambda a, b: a * b)(w, e)
    wn = lift(lambda a, b: a * b)(w, n)
    de = sub2(east_of(we), west_of(we))
    dn = sub2(north_of(wn), south_of(wn))
    hw = lift(lambda w_, h_, a, b: w_ * (h_ + (0.5 * gravity) * (a + b)))(w, h, de, dn)
    se = sub2(east_of(hw), west_of(hw))
    sn = sub2(north_of(hw), south_of(hw))
    keep = 1.0 - drag_rate
    e_new = lift(lambda a, b, s: keep * a - coriolis * b + (0.5 * gravity) * s)(we, wn, se)
    n_new = lift(lambda a, b, s: keep * b + coriolis * a + (0.5 * gravity) * s)(we, wn, sn)
    return hw, e_new, n_new


def slot_mask(rows, width, count, offset):
    lane = lane_iota(rows)
    mask = None
    for slot in range(count):
        start = 2 * width * slot + offset
        here = (lane >= start) & (lane < start + width)
        mask = here if mask is None else mask | here
    return mask


def pack_edges(fields, width):
    lane = lane_iota(fields[0].shape[0])
    out = jnp.zeros_like(fields[0])
    for slot, field in enumerate(fields):
        start = 2 * width * slot
        rolled = pltpu.roll(field, (start + width) % LANES, 1)
        out = jnp.where((lane >= start) & (lane < start + 2 * width), rolled, out)
    return out


def unpack_edge(packed, width, slot):
    lane = lane_iota(packed.shape[0])
    rolled = pltpu.roll(packed, (-width - 2 * width * slot) % LANES, 1)
    return jnp.where((lane < width) | (lane >= LANES - width), rolled, 0.0)


def split_bf16(x):
    high = x.astype(BF16)
    rest = x - high.astype(F32)
    middle = rest.astype(BF16)
    low = (rest - middle.astype(F32)).astype(BF16)
    return jnp.concatenate([high, middle, low], axis=0)


def permute_columns(x, select):
    rows = x.shape[0]
    y = jnp.dot(split_bf16(x), select, preferred_element_type=F32)
    return (y[2 * rows :] + y[rows : 2 * rows]) + y[:rows]


def store_shifted(ref, row, pair):
    for dx, shifted in enumerate((west_of(pair), pair, east_of(pair))):
        for tile in range(2):
            ref[tile, row, 16 * dx : 16 * dx + 16, :] = shifted[tile].astype(BF16)


def patch(ref, row):
    return jnp.concatenate([ref[tile, row : row + 3].reshape(144, LANES) for tile in range(2)], axis=1)


def conv_row(weight, ref, row):
    y = jnp.dot(weight, patch(ref, row), preferred_element_type=F32)
    return (y[:, :LANES], y[:, LANES:])


def contract(left, right):
    return lax.dot_general(left, right, (((1,), (1,)), ((), ())), preferred_element_type=F32)


def kernel(
    sizes,
    temp,
    height,
    flow,
    land_sea,
    fold,
    w_first,
    w_second,
    w_third,
    temp_bar,
    height_bar,
    flow_bar,
    temp_out,
    height_out,
    flow_out,
    first_out,
    second_out,
    third_out,
    surf,
    trac,
    inputs,
    wet_i,
    bar_t,
    bar_h,
    bar_f,
    fold_s,
    w1_raw,
    w2_raw,
    w3_raw,
    w_rows,
    w_flip,
    msg_out,
    msg_in,
    fold_surf,
    fold_trac,
    g3_rows,
    xs1,
    xs2,
    xs3,
    gs1,
    gs2,
    gs3,
    act1,
    act2,
    back,
    sg,
    tg,
    back_out,
    back_in,
    back_surf,
    back_trac,
    unfold_surf,
    unfold_trac,
    unfold_edge,
    halves,
    half_in,
    plane_in,
    column_in,
    totals,
    load_sem,
    f_send,
    f_recv,
    m_send,
    m_recv,
    fold_send,
    fold_recv,
    b_send,
    b_recv,
    bm_send,
    bm_recv,
    unfold_send,
    unfold_recv,
    pair_send,
    pair_recv,
    plane_send,
    plane_recv,
    column_send,
    column_recv,
):
    nlon, nlat, nens = sizes
    lon, lat, ens = lax.axis_index("lon"), lax.axis_index("lat"), lax.axis_index("ens")
    top = nlat - 1
    left, right = lax.rem(lon + nlon - 1, nlon), lax.rem(lon + 1, nlon)
    nz, ny = nlon // 2, nlat // 2
    core, z = lax.rem(lat, 2), lax.rem(lon, nz)
    plane = 2 * ny * nens
    place = (ens * 2 + lon // nz) * ny + lat // 2

    def remote(src, dst, send, recv, **device):
        return pltpu.make_async_remote_copy(
            src_ref=src, dst_ref=dst, send_sem=send, recv_sem=recv, device_id=device, device_id_type=MESH
        )

    barrier = pltpu.get_barrier_semaphore()

    def greet(**device):
        pl.semaphore_signal(barrier, inc=1, device_id=device, device_id_type=MESH)

    def plane_device(index):
        return dict(lon=lax.rem(index // ny, 2) * nz + z, lat=lax.rem(index, ny) * 2 + core, ens=index // (2 * ny))

    def column_device(index):
        return dict(lon=(lon // nz) * nz + index)

    for k in range(1, plane):
        greet(**plane_device(lax.rem(place + k, plane)))
    for k in range(1, nz):
        greet(**column_device(lax.rem(z + k, nz)))
    greet(lon=left)
    greet(lon=right)

    @pl.when(lat > 0)
    def _():
        greet(lat=lat - 1)
        greet(lon=left, lat=lat - 1)
        greet(lon=right, lat=lat - 1)

    @pl.when(lat < top)
    def _():
        greet(lat=lat + 1)
        greet(lon=left, lat=lat + 1)
        greet(lon=right, lat=lat + 1)

    @pl.when(lat == top)
    def _():
        for k in range(1, nlon):
            greet(lon=lax.rem(lon + k, nlon))

    loads = [
        (temp.at[0], trac.at[0, :, 8:24, :]),
        (height.at[0], surf.at[0, 0, 16:32, :]),
        (flow.at[0], surf.at[0, 1:3, 16:32, :]),
        (land_sea, wet_i),
        (fold, fold_s),
        (w_first, w1_raw),
        (w_second, w2_raw),
        (w_third, w3_raw),
        (temp_bar.at[0], bar_t),
        (height_bar.at[0], bar_h),
        (flow_bar.at[0], bar_f),
    ]
    loads = [pltpu.make_async_copy(src, dst, load_sem.at[k]) for k, (src, dst) in enumerate(loads)]
    for load in loads:
        load.start()

    inputs[:, 32 * (HCH + 1) :, :] = jnp.zeros((2, 32 * (15 - HCH), LANES), F32)
    for ref, rows in ((gs3, 20), (gs2, 22), (gs1, 24)):
        for tile in range(2):
            for row in (0, 1, rows - 2, rows - 1):
                ref[tile, row] = jnp.zeros((48, LANES), BF16)
    back[...] = jnp.zeros_like(back)
    fold_surf[lon, 40:48, :] = jnp.zeros((8, LANES), F32)
    fold_trac[lon, 32:40, :] = jnp.zeros((8, LANES), F32)
    for ref in (unfold_surf, unfold_trac):
        ref[lon, 32:40, :] = jnp.zeros((8, LANES), F32)
    unfold_edge[:, 32:40, :] = jnp.zeros((2, 8, LANES), F32)

    @pl.when(lat == 0)
    def _():
        surf[:, :, 0:16, :] = jnp.zeros((2, 4, 16, LANES), F32)
        trac[:, :, 0:8, :] = jnp.zeros((2, LEV, 8, LANES), F32)
        back_in[:, 0] = jnp.zeros((2, 2, 16, LANES), F32)
        back_surf[0] = jnp.zeros((3, 16, LANES), F32)
        back_trac[0] = jnp.zeros((LEV, 8, LANES), F32)

    @pl.when(lat == top)
    def _():
        surf[:, :, 32:48, :] = jnp.zeros((2, 4, 16, LANES), F32)
        trac[:, :, 24:32, :] = jnp.zeros((2, LEV, 8, LANES), F32)
        back_in[:, 2] = jnp.zeros((2, 2, 16, LANES), F32)
        back_surf[1] = jnp.zeros((3, 16, LANES), F32)
        back_trac[1] = jnp.zeros((LEV, 8, LANES), F32)

    for k in (1, 2, 3, 0):
        loads[k].wait()
    surf[0, 3, 16:32, :] = wet_i[...].astype(F32)
    msg_out[0] = pack_edges([surf[0, f, 16:32, :] for f in range(4)], RIM)
    msg_out[1] = pack_edges([trac[0, c, 8:24, :] for c in range(LEV)], TRIM)

    def lat_copies(up):
        to = 1 if up else -1
        rows_s = slice(0, 16) if up else slice(32, 48)
        rows_t = (slice(16, 24), slice(0, 8)) if up else (slice(8, 16), slice(24, 32))
        slot = 0 if up else 2
        return (
            remote(surf.at[0, :, 16:32, :], surf.at[0, :, rows_s, :], f_send.at[slot], f_recv.at[slot], lat=lat + to),
            remote(
                trac.at[0, :, rows_t[0], :],
                trac.at[0, :, rows_t[1], :],
                f_send.at[slot + 1],
                f_recv.at[slot + 1],
                lat=lat + to,
            ),
        )

    def edge_copy(side, shift):
        slot = 3 * side + 1 - shift
        return remote(
            msg_out, msg_in.at[side, 1 - shift], m_send.at[slot], m_recv.at[slot], lon=(right, left)[side], lat=lat + shift
        )

    def fold_copies(k):
        peer = lax.rem(lon + k, nlon)
        return (
            remote(fold_surf.at[lon], fold_surf.at[lon], fold_send.at[0, k], fold_recv.at[0, k], lon=peer),
            remote(fold_trac.at[lon], fold_trac.at[lon], fold_send.at[1, k], fold_recv.at[1, k], lon=peer),
        )

    def fold_arrivals(k):
        source = lax.rem(lon + nlon - k, nlon)
        return (
            remote(fold_surf.at[lon], fold_surf.at[source], fold_send.at[0, k], fold_recv.at[0, k], lon=source),
            remote(fold_trac.at[lon], fold_trac.at[source], fold_send.at[1, k], fold_recv.at[1, k], lon=source),
        )

    @pl.when(lat == top)
    def _():
        for f in range(4):
            for m in range(RIM):
                row = RIM * f + m
                fold_surf[lon, row : row + 1, :] = surf[0, f, 31 - m : 32 - m, :]
        for c in range(LEV):
            for m in range(TRIM):
                row = TRIM * c + m
                fold_trac[lon, row : row + 1, :] = trac[0, c, 23 - m : 24 - m, :]

    pl.semaphore_wait(
        barrier,
        (plane - 1)
        + (nz - 1)
        + 2
        + 3 * (lat > 0).astype(jnp.int32)
        + 3 * (lat < top).astype(jnp.int32)
        + (nlon - 1) * (lat == top).astype(jnp.int32),
    )

    def for_lat(fn):
        pl.when(lat > 0)(functools.partial(fn, -1))
        fn(0)
        pl.when(lat < top)(functools.partial(fn, 1))

    @pl.when(lat == top)
    def _():
        for k in range(1, nlon):
            fold_copies(k)[0].start()

    def start_forward(shift):
        if shift:
            for copy in lat_copies(shift > 0):
                copy.start()
        for side in range(2):
            edge_copy(side, shift).start()

    for_lat(start_forward)

    @pl.when(lat == top)
    def _():
        for k in range(1, nlon):
            fold_copies(k)[1].start()

    for k in range(4, 11):
        loads[k].wait()
    raw1 = w1_raw[...].astype(F32)
    w_rows[...] = jnp.zeros_like(w_rows)
    for tap in range(9):
        w_rows[0, :, 16 * tap : 16 * tap + CL] = raw1[:, 11 * tap : 11 * tap + CL]
        w_rows[0, :, 16 * tap + HCH : 16 * tap + HCH + 1] = raw1[:, 11 * tap + CL : 11 * tap + CL + 1]
    w_rows[1, :, 0:144] = w2_raw[...].astype(F32)
    w_rows[2, 0:CL, 0:144] = w3_raw[...].astype(F32)
    for layer in range(3):
        first = jnp.transpose(w_rows[layer, :, 0:128])
        second = jnp.transpose(w_rows[layer, :, 128:256])
        for tap in range(9):
            block = second[0:16, :] if tap == 8 else first[16 * tap : 16 * tap + 16, :]
            w_flip[layer, :, 16 * (8 - tap) : 16 * (8 - tap) + 16] = block
    weight1 = w_rows[0, :, 0:144].astype(BF16)
    weight2 = w_rows[1, :, 0:144].astype(BF16)
    flip1, flip2, flip3 = (w_flip[layer].astype(BF16) for layer in range(3))

    wet_own = surf[0, 3, 16:32, :]
    g3_rows[16 * CL :, :] = jnp.zeros((16 * (16 - CL), LANES), F32)
    for c in range(CL):
        g3_rows[16 * c : 16 * c + 16, :] = closure_gain * wet_own * bar_t[c]
    for row in range(16):
        own = g3_rows[pl.ds(row, 16, stride=16), :]
        store_shifted(gs3, row + 2, (own, jnp.zeros_like(own)))

    shift_s = fold_s[0] + 1
    base = shift_s - 139 - LANES * lon + LANES * (2 * nlon)
    tile0 = base // LANES
    offset = shift_s - 1 - LANES * lon + LANES * (2 * nlon) - LANES * tile0

    def mirrored(ref):
        return jnp.concatenate([ref[lax.rem(tile0 + j, nlon)] for j in range(3)], axis=1)

    def mirror_matrix():
        source = lax.broadcasted_iota(jnp.int32, (3 * LANES, 2 * LANES), 0)
        column = lax.broadcasted_iota(jnp.int32, (3 * LANES, 2 * LANES), 1)
        column = jnp.where(column < LANES + LANES // 2, column, column - 2 * LANES)
        return jnp.where(source + column == offset, 1.0, 0.0).astype(BF16)

    left_s = slot_mask(16, RIM, 4, 0)
    left_t = slot_mask(16, TRIM, LEV, 0)

    def wait_forward(shift):
        k = shift + 1
        if shift:
            for copy in lat_copies(shift < 0):
                copy.wait_recv()
        for side in range(2):
            edge_copy(side, -shift).wait_recv()
        packed = jnp.where(left_s, msg_in[0, k, 0], msg_in[1, k, 0])
        for f in range(4):
            surf[1, f, 16 * k : 16 * k + 16, :] = unpack_edge(packed, RIM, f)
        packed = jnp.where(left_t, msg_in[0, k, 1], msg_in[1, k, 1])
        rows, at = ((slice(8, 16), 0), (slice(0, 16), 8), (slice(0, 8), 24))[k]
        packed = packed[rows]
        for c in range(LEV):
            trac[1, c, at : at + packed.shape[0], :] = unpack_edge(packed, TRIM, c)

    for_lat(wait_forward)

    @pl.when(lat == top)
    def _():
        select = mirror_matrix()
        for k in range(1, nlon):
            fold_arrivals(k)[0].wait_recv()
        ghost = permute_columns(mirrored(fold_surf), select)
        for f in range(4):
            rows = ghost[RIM * f : RIM * f + RIM]
            rows = -rows if f in (1, 2) else rows
            for tile in range(2):
                surf[tile, f, 32 : 32 + RIM, :] = rows[:, LANES * tile : LANES * tile + LANES]

    h, e, n, wet = (tuple(surf[tile, f] for tile in range(2)) for f in range(4))
    for _ in range(SUB):
        h, e, n = step_forward(h, e, n, wet)
    new_e, new_n = e[0][16:32], n[0][16:32]

    @pl.when(lat == top)
    def _():
        select = mirror_matrix()
        for k in range(1, nlon):
            fold_arrivals(k)[1].wait_recv()
        ghost = permute_columns(mirrored(fold_trac), select)
        for c in range(LEV):
            rows = ghost[TRIM * c : TRIM * c + TRIM]
            for tile in range(2):
                trac[tile, c, 24 : 24 + TRIM, :] = rows[:, LANES * tile : LANES * tile + LANES]


    for tile in range(2):
        for c in range(LEV):
            inputs[tile, 32 * c : 32 * c + 32, :] = trac[tile, c]
        inputs[tile, 32 * HCH : 32 * HCH + 32, :] = h[tile][8:40]
    for row in range(22):
        store_shifted(xs1, row, tuple(inputs[tile, pl.ds(5 + row, 16, stride=32), :] for tile in range(2)))
    for row in range(20):
        act = lift(jnp.tanh)(conv_row(weight1, xs1, row))
        for tile in range(2):
            act1[tile, row] = act[tile]
        store_shifted(xs2, row, act)
    for row in range(18):
        act = lift(jnp.tanh)(conv_row(weight2, xs2, row))
        for tile in range(2):
            act2[tile, row] = act[tile]
        store_shifted(xs3, row, act)

    def weight_sum(gs, xs, rows):
        total = jnp.zeros((16, 144), F32)
        for row in range(rows):
            grad = jnp.concatenate([gs[tile, row + 2, 16:32, :] for tile in range(2)], axis=1)
            total = total + contract(grad, patch(xs, row))
        return total

    def back_layer(weight, gs, act_ref, out, rows):
        for row in range(rows):
            grad = conv_row(weight, gs, row)
            act = tuple(act_ref[tile, row] for tile in range(2))
            store_shifted(out, row + 2, lift(lambda g, a: g * (1.0 - a * a))(grad, act))

    sum3 = weight_sum(gs3, xs3, 16)
    back_layer(flip3, gs3, act2, gs2, 18)
    sum2 = weight_sum(gs2, xs2, 18)
    back_layer(flip2, gs2, act1, gs1, 20)
    sum1 = weight_sum(gs1, xs1, 20)

    tail = jnp.concatenate([sum1[:, 128:144], sum2[:, 128:144], sum3[:, 128:144], jnp.zeros((16, 80), F32)], axis=1)
    tail = jnp.concatenate([tail[0:6, 0:48], tail[6:12, 0:48], tail[10:16, 0:32]], axis=1)
    rows = jnp.concatenate([sum1[:, :128], sum2[:, :128], sum3[0:CL, :128], tail], axis=0)
    halves[0] = rows[0:24]
    halves[1] = rows[24:48]

    def half_copy():
        return remote(halves.at[1 - core], half_in, pair_send.at[0], pair_recv.at[0], lat=lat + 1 - 2 * core)

    def plane_copy(k, arrival=False):
        other = lax.rem(place + (plane - k if arrival else k), plane)
        slot = other if arrival else place
        return remote(
            plane_in.at[place], plane_in.at[slot], plane_send.at[k], plane_recv.at[k], **plane_device(other)
        )

    def column_copy(k, arrival=False):
        other = lax.rem(z + (nz - k if arrival else k), nz)
        slot = other if arrival else z
        return remote(
            column_in.at[z], column_in.at[slot], column_send.at[k], column_recv.at[k], **column_device(other)
        )

    def total_copy(arrival=False):
        slot = 1 - core if arrival else core
        return remote(totals.at[core], totals.at[slot], pair_send.at[1], pair_recv.at[1], lat=lat + 1 - 2 * core)

    def sum_slots(ref, count):
        total = ref[0]
        for k in range(1, count):
            total = total + ref[k]
        return total

    half_copy().start()

    for row in range(22):
        grad = conv_row(flip1, gs1, row)
        for tile in range(2):
            back[tile, pl.ds(5 + row, 16, stride=32), :] = grad[tile]

    lane16 = lane_iota(16)
    zero8 = jnp.zeros((8, LANES), F32)
    sum_e = jnp.zeros((16, LANES), F32)
    sum_n = jnp.zeros((16, LANES), F32)
    for c in range(LEV):
        bar = bar_t[c]
        wb = wet_own * bar
        own, halo = trac[0, c, 8:24, :], trac[1, c, 8:24, :]
        ahead = jnp.where(lane16 == LANES - 1, pltpu.roll(halo, LANES - 1, 1), pltpu.roll(own, LANES - 1, 1))
        behind = jnp.where(lane16 == 0, pltpu.roll(halo, 1, 1), pltpu.roll(own, 1, 1))
        sum_e = sum_e + wb * (ahead - behind)
        sum_n = sum_n + wb * (trac[0, c, 9:25, :] - trac[0, c, 7:23, :])
        qe = (0.5 * advection) * new_e * wb
        qn = (0.5 * advection) * new_n * wb
        wd = diffusion * wb
        up = pltpu.roll(wd + qe, LANES - 1, 1)
        down = pltpu.roll(wd - qe, 1, 1)
        middle = (
            bar - 4.0 * wd + jnp.where(lane16 < LANES - 1, up, 0.0) + jnp.where(lane16 > 0, down, 0.0)
        )
        side = jnp.where(lane16 == LANES - 1, up, jnp.where(lane16 == 0, down, 0.0))
        above = pltpu.roll(jnp.concatenate([zero8, wd + qn, zero8], axis=0), 31, 0)
        below = pltpu.roll(jnp.concatenate([zero8, wd - qn, zero8], axis=0), 1, 0)
        main = jnp.concatenate([zero8, middle, zero8], axis=0) + above + below
        side = jnp.concatenate([zero8, side, zero8], axis=0)
        if c < CL:
            main = main + back[0, 32 * c : 32 * c + 32, :]
            side = side + back[1, 32 * c : 32 * c + 32, :]
        tg[0, c] = main
        tg[1, c] = side

    def lat_back(up):
        to = 1 if up else -1
        rows_s = slice(32, 48) if up else slice(0, 16)
        rows_t = slice(24, 32) if up else slice(0, 8)
        slot = 0 if up else 1
        return (
            remote(sg.at[0, :, rows_s, :], back_surf.at[slot], b_send.at[0, slot], b_recv.at[0, slot], lat=lat + to),
            remote(tg.at[0, :, rows_t, :], back_trac.at[slot], b_send.at[1, slot], b_recv.at[1, slot], lat=lat + to),
        )

    def unfold_copies(k):
        peer = lax.rem(lon + k, nlon)
        return (
            remote(unfold_surf.at[lon], unfold_surf.at[lon], unfold_send.at[0, k], unfold_recv.at[0, k], lon=peer),
            remote(unfold_trac.at[lon], unfold_trac.at[lon], unfold_send.at[1, k], unfold_recv.at[1, k], lon=peer),
        )

    def unfold_arrivals(k):
        source = lax.rem(lon + nlon - k, nlon)
        return (
            remote(unfold_surf.at[lon], unfold_surf.at[source], unfold_send.at[0, k], unfold_recv.at[0, k], lon=source),
            remote(unfold_trac.at[lon], unfold_trac.at[source], unfold_send.at[1, k], unfold_recv.at[1, k], lon=source),
        )

    def pack_ghosts(grads, first, count, width, out, edge):
        for f in range(count):
            for j in range(width):
                row, ghost = width * f + j, first + width - 1 - j
                out[lon, row : row + 1, :] = grads[0, f, ghost : ghost + 1, :]
                edge[row : row + 1, :] = grads[1, f, ghost : ghost + 1, :]
        out[lon, 40:48, :] = pack_edges([edge[8 * g : 8 * g + 8, :] for g in range(5)], width)

    @pl.when(lat == top)
    def _():
        pack_ghosts(tg, 24, LEV, TRIM, unfold_trac, unfold_edge.at[0])
        for k in range(1, nlon):
            unfold_copies(k)[1].start()

    pl.when(lat > 0)(lambda: lat_back(False)[1].start())
    pl.when(lat < top)(lambda: lat_back(True)[1].start())

    half_copy().wait_recv()
    plane_in[place] = halves[core] + half_in[...]
    for k in range(1, plane):
        plane_copy(k).start()

    def own_rows(x):
        zero16 = jnp.zeros((16, LANES), F32)
        return (jnp.concatenate([zero16, x, zero16], axis=0), jnp.zeros((48, LANES), F32))

    e = own_rows(bar_f[0] - (0.5 * advection) * sum_e)
    n = own_rows(bar_f[1] - (0.5 * advection) * sum_n)
    rim = tuple(jnp.concatenate([zero8, back[tile, 32 * HCH : 32 * HCH + 32, :], zero8], axis=0) for tile in range(2))
    h = lift(lambda a, b: a + b)(rim, own_rows(bar_h[...]))
    wet = tuple(surf[tile, 3] for tile in range(2))
    for index in range(SUB):
        h, e, n = step_adjoint(h, e, n, wet)
    for f, pair in enumerate((h, e, n)):
        for tile in range(2):
            sg[tile, f] = pair[tile]

    for block in range(3):
        back_out[block, 0] = pack_edges([sg[1, f, 16 * block : 16 * block + 16, :] for f in range(3)], RIM)
        if block == 1:
            fields = [tg[1, c, 8:24, :] for c in range(LEV)]
        elif block == 0:
            fields = [jnp.concatenate([zero8, tg[1, c, 0:8, :]], axis=0) for c in range(LEV)]
        else:
            fields = [jnp.concatenate([tg[1, c, 24:32, :], zero8], axis=0) for c in range(LEV)]
        back_out[block, 1] = pack_edges(fields, TRIM)

    def edge_back(side, block):
        return remote(
            back_out.at[block],
            back_in.at[side, 2 - block],
            bm_send.at[side, 2 - block],
            bm_recv.at[side, 2 - block],
            lon=(right, left)[side],
            lat=lat + block - 1,
        )

    @pl.when(lat == top)
    def _():
        pack_ghosts(sg, 32, 3, RIM, unfold_surf, unfold_edge.at[1])
        for k in range(1, nlon):
            unfold_copies(k)[0].start()

    def start_back(shift):
        if shift:
            lat_back(shift > 0)[0].start()
        for side in range(2):
            edge_back(side, shift + 1).start()

    for_lat(start_back)

    right_s = slot_mask(16, RIM, 3, RIM)
    right_t = slot_mask(16, TRIM, LEV, TRIM)

    for k in range(1, plane):
        plane_copy(k, True).wait_recv()
    column_in[z] = sum_slots(plane_in, plane)
    for k in range(1, nz):
        column_copy(k).start()

    def wait_back(shift):
        if shift:
            for copy in lat_back(shift < 0):
                copy.wait_recv()
        for side in range(2):
            edge_back(side, 1 - shift).wait_recv()

    for_lat(wait_back)

    from_left = back_in[0, 0] + back_in[0, 1] + back_in[0, 2]
    from_right = back_in[1, 0] + back_in[1, 1] + back_in[1, 2]
    packed = jnp.where(right_s, from_left[0], from_right[0])
    for f in range(3):
        total = sg[0, f, 16:32, :] + back_surf[0, f] + back_surf[1, f] + unpack_edge(packed, RIM, f)
        if f == 0:
            height_out[0] = total
        else:
            flow_out[0, f - 1] = total
    packed = jnp.where(right_t, from_left[1], from_right[1])
    for c in range(LEV):
        ghosts = jnp.concatenate([back_trac[0, c], back_trac[1, c]], axis=0)
        temp_out[0, c] = tg[0, c, 8:24, :] + ghosts + unpack_edge(packed, TRIM, c)

    for k in range(1, nz):
        column_copy(k, True).wait_recv()
    totals[core] = sum_slots(column_in, nz)
    total_copy().start()

    @pl.when(lat == top)
    def _():
        lane = lax.broadcasted_iota(jnp.int32, (LANES, LANES), 0)
        column = lax.broadcasted_iota(jnp.int32, (LANES, LANES), 1)
        halo = jnp.where(lane < LANES // 2, lane + LANES, lane - LANES)
        select = jnp.concatenate(
            [jnp.where(at + LANES * j + column == offset, 1.0, 0.0) for at in (lane, halo) for j in range(3)], axis=0
        ).astype(BF16)

        def unfold(ref, width):
            tiles = [ref[lax.rem(tile0 + j, nlon)] for j in range(3)]
            edges = [
                jnp.concatenate([unpack_edge(tile[40:48], width, g) for g in range(5)], axis=0) for tile in tiles
            ]
            return permute_columns(jnp.concatenate([tile[0:40] for tile in tiles] + edges, axis=1), select)

        for k in range(1, nlon):
            unfold_arrivals(k)[1].wait_recv()
        ghost = unfold(unfold_trac, TRIM)
        for c in range(LEV):
            temp_out[0, c, 16 - TRIM : 16, :] = (
                temp_out[0, c, 16 - TRIM : 16, :] + ghost[TRIM * c : TRIM * c + TRIM]
            )
        for k in range(1, nlon):
            unfold_arrivals(k)[0].wait_recv()
        ghost = unfold(unfold_surf, RIM)
        height_out[0, 16 - RIM : 16, :] = height_out[0, 16 - RIM : 16, :] + ghost[0:RIM]
        for f in (1, 2):
            flow_out[0, f - 1, 16 - RIM : 16, :] = (
                flow_out[0, f - 1, 16 - RIM : 16, :] - ghost[RIM * f : RIM * f + RIM]
            )

    total_copy(True).wait_recv()
    scale = 1.0 / math.sqrt(nens * nlat * 16 * nlon * LANES)
    rows = jnp.concatenate([totals[0], totals[1]], axis=0) * scale
    tail = rows[32 + CL : 48]
    tail = jnp.concatenate(
        [tail[:, 0:48], tail[:, 48:96], jnp.concatenate([tail[2:6, 96:128], jnp.zeros((4, 16), F32)], axis=1)], axis=0
    )
    for layer, out in ((1, second_out), (2, third_out)):
        count = out.shape[0]
        out[:, 0:128] = rows[16 * layer : 16 * layer + count]
        out[:, 128:144] = tail[0:count, 16 * layer : 16 * layer + 16]
    for tap in range(9):
        block = tail[:, 0:16] if tap == 8 else rows[0:16, 16 * tap : 16 * tap + 16]
        first_out[:, 11 * tap : 11 * tap + CL] = block[:, 0:CL]
        first_out[:, 11 * tap + CL : 11 * tap + CL + 1] = block[:, HCH : HCH + 1]

    def sent_forward(shift):
        if shift:
            for copy in lat_copies(shift > 0):
                copy.wait_send()
            for copy in lat_back(shift > 0):
                copy.wait_send()
        for side in range(2):
            edge_copy(side, shift).wait_send()
            edge_back(side, shift + 1).wait_send()

    for_lat(sent_forward)
    half_copy().wait_send()
    total_copy().wait_send()
    for k in range(1, plane):
        plane_copy(k).wait_send()
    for k in range(1, nz):
        column_copy(k).wait_send()

    @pl.when(lat == top)
    def _():
        for k in range(1, nlon):
            for copy in fold_copies(k) + unfold_copies(k):
                copy.wait_send()


def hand_over(*refs):
    sources, targets, sem = refs[:6], refs[6:12], refs[12]
    copies = [pltpu.make_async_copy(src, dst, sem.at[k]) for k, (src, dst) in enumerate(zip(sources, targets))]
    for copy in copies:
        copy.start()
    for copy in copies:
        copy.wait()


def solution(mesh):
    nlon, nlat, nens = (mesh.shape[axis] for axis in ("lon", "lat", "ens"))
    plane = nlat * nens

    def local(temp, height, flow, land_sea, fold, w_first, w_second, w_third, temp_bar, height_bar, flow_bar):
        vmem = pltpu.VMEM
        dma = pltpu.SemaphoreType.DMA
        scratch = [
            vmem((2, 4, 48, LANES), F32),
            vmem((2, LEV, 32, LANES), F32),
            vmem((2, 16 * 32, LANES), F32),
            vmem((16, LANES), jnp.int32),
            vmem((LEV, 16, LANES), F32),
            vmem((16, LANES), F32),
            vmem((2, 16, LANES), F32),
            pltpu.SMEM(fold.shape, jnp.int32),
            vmem(w_first.shape, BF16),
            vmem(w_second.shape, BF16),
            vmem(w_third.shape, BF16),
            vmem((3, 16, 256), F32),
            vmem((3, 16, 144), F32),
            vmem((2, 16, LANES), F32),
            vmem((2, 3, 2, 16, LANES), F32),
            vmem((nlon, 48, LANES), F32),
            vmem((nlon, 40, LANES), F32),
            vmem((16 * 16, LANES), F32),
            vmem((2, 22, 48, LANES), BF16),
            vmem((2, 20, 48, LANES), BF16),
            vmem((2, 18, 48, LANES), BF16),
            vmem((2, 24, 48, LANES), BF16),
            vmem((2, 22, 48, LANES), BF16),
            vmem((2, 20, 48, LANES), BF16),
            vmem((2, 20, 16, LANES), F32),
            vmem((2, 18, 16, LANES), F32),
            vmem((2, 16 * 32, LANES), F32),
            vmem((2, 3, 48, LANES), F32),
            vmem((2, LEV, 32, LANES), F32),
            vmem((3, 2, 16, LANES), F32),
            vmem((2, 3, 2, 16, LANES), F32),
            vmem((2, 3, 16, LANES), F32),
            vmem((2, LEV, 8, LANES), F32),
            vmem((nlon, 48, LANES), F32),
            vmem((nlon, 48, LANES), F32),
            vmem((2, 40, LANES), F32),
            vmem((2, 24, LANES), F32),
            vmem((24, LANES), F32),
            vmem((plane, 24, LANES), F32),
            vmem((nlon // 2, 24, LANES), F32),
            vmem((2, 24, LANES), F32),
            dma((11,)),
            dma((4,)),
            dma((4,)),
            dma((6,)),
            dma((6,)),
            dma((2, nlon)),
            dma((2, nlon)),
            dma((2, 2)),
            dma((2, 2)),
            dma((2, 4)),
            dma((2, 4)),
            dma((2, nlon)),
            dma((2, nlon)),
            dma((2,)),
            dma((2,)),
            dma((plane,)),
            dma((plane,)),
            dma((nlon // 2,)),
            dma((nlon // 2,)),
        ]
        out_shape = (
            jax.ShapeDtypeStruct(temp.shape, F32),
            jax.ShapeDtypeStruct(height.shape, F32),
            jax.ShapeDtypeStruct(flow.shape, F32),
            jax.ShapeDtypeStruct(w_first.shape, F32),
            jax.ShapeDtypeStruct(w_second.shape, F32),
            jax.ShapeDtypeStruct(w_third.shape, F32),
        )
        results = pl.pallas_call(
            functools.partial(kernel, (nlon, nlat, nens)),
            out_shape=out_shape,
            in_specs=[pl.BlockSpec(memory_space=pltpu.HBM)] * 11,
            out_specs=[pl.BlockSpec(memory_space=pltpu.VMEM)] * 6,
            scratch_shapes=scratch,
            compiler_params=pltpu.CompilerParams(
                collective_id=0, has_side_effects=True, vmem_limit_bytes=60 * 1024 * 1024
            ),
        )(temp, height, flow, land_sea, fold, w_first, w_second, w_third, temp_bar, height_bar, flow_bar)
        return pl.pallas_call(
            hand_over,
            out_shape=out_shape,
            in_specs=[pl.BlockSpec(memory_space=pltpu.VMEM)] * 6,
            out_specs=[pl.BlockSpec(memory_space=pltpu.HBM)] * 6,
            scratch_shapes=[dma((6,))],
        )(*results)

    field = P("ens", None, "lat", "lon")
    surface = P("ens", "lat", "lon")
    return jax.shard_map(
        local,
        mesh=mesh,
        in_specs=(field, surface, field, P("lat", "lon"), P(), P(), P(), P(), field, surface, field),
        out_specs=(field, surface, field, P(), P(), P()),
        check_vma=False,
    )
```

```python
import functools
import math

import jax
import jax.numpy as jnp
from jax import lax
from jax.experimental import pallas as pl
from jax.experimental.pallas import tpu as pltpu
from jax.sharding import PartitionSpec as P

MESH = pl.DeviceIdType.MESH
F32 = jnp.float32
BF16 = jnp.bfloat16

SUB = 4
LEV = 12
CL = 10
RIM = 10
TRIM = 3
HCH = 12
LANES = 128

gravity = 0.3
drag_rate = 0.05
coriolis = 0.2
diffusion = 0.1
advection = 0.1
closure_gain = 0.5


def lane_iota(rows):
    return lax.broadcasted_iota(jnp.int32, (rows, LANES), 1)


def east_of(x):
    a, b = (pltpu.roll(v, LANES - 1, 1) for v in x)
    edge = lane_iota(a.shape[0]) == LANES - 1
    return (jnp.where(edge, b, a), jnp.where(edge, a, b))


def west_of(x):
    a, b = (pltpu.roll(v, 1, 1) for v in x)
    edge = lane_iota(a.shape[0]) == 0
    return (jnp.where(edge, b, a), jnp.where(edge, a, b))


def north_of(x):
    return tuple(pltpu.roll(v, v.shape[0] - 1, 0) for v in x)


def south_of(x):
    return tuple(pltpu.roll(v, 1, 0) for v in x)


def lift(fn):
    return lambda *pairs: tuple(fn(*vs) for vs in zip(*pairs))


sub2 = lift(lambda u, v: u - v)


def step_forward(h, e, n, w):
    de = sub2(east_of(e), west_of(e))
    dn = sub2(north_of(n), south_of(n))
    h = lift(lambda w_, h_, a, b: w_ * (h_ - (0.5 * gravity) * (a + b)))(w, h, de, dn)
    se = sub2(east_of(h), west_of(h))
    sn = sub2(north_of(h), south_of(h))
    keep = 1.0 - drag_rate
    e_new = lift(lambda w_, e_, n_, s: w_ * (keep * e_ - (0.5 * gravity) * s + coriolis * n_))(w, e, n, se)
    n_new = lift(lambda w_, e_, n_, s: w_ * (keep * n_ - (0.5 * gravity) * s - coriolis * e_))(w, e, n, sn)
    return h, e_new, n_new


def step_adjoint(h, e, n, w):
    we = lift(lambda a, b: a * b)(w, e)
    wn = lift(lambda a, b: a * b)(w, n)
    de = sub2(east_of(we), west_of(we))
    dn = sub2(north_of(wn), south_of(wn))
    hw = lift(lambda w_, h_, a, b: w_ * (h_ + (0.5 * gravity) * (a + b)))(w, h, de, dn)
    se = sub2(east_of(hw), west_of(hw))
    sn = sub2(north_of(hw), south_of(hw))
    keep = 1.0 - drag_rate
    e_new = lift(lambda a, b, s: keep * a - coriolis * b + (0.5 * gravity) * s)(we, wn, se)
    n_new = lift(lambda a, b, s: keep * b + coriolis * a + (0.5 * gravity) * s)(we, wn, sn)
    return hw, e_new, n_new


def slot_mask(rows, width, count, offset):
    lane = lane_iota(rows)
    mask = None
    for slot in range(count):
        start = 2 * width * slot + offset
        here = (lane >= start) & (lane < start + width)
        mask = here if mask is None else mask | here
    return mask


def pack_edges(fields, width):
    lane = lane_iota(fields[0].shape[0])
    out = jnp.zeros_like(fields[0])
    for slot, field in enumerate(fields):
        start = 2 * width * slot
        rolled = pltpu.roll(field, (start + width) % LANES, 1)
        out = jnp.where((lane >= start) & (lane < start + 2 * width), rolled, out)
    return out


def unpack_edge(packed, width, slot):
    lane = lane_iota(packed.shape[0])
    rolled = pltpu.roll(packed, (-width - 2 * width * slot) % LANES, 1)
    return jnp.where((lane < width) | (lane >= LANES - width), rolled, 0.0)


def split_bf16(x):
    high = x.astype(BF16)
    rest = x - high.astype(F32)
    middle = rest.astype(BF16)
    low = (rest - middle.astype(F32)).astype(BF16)
    return jnp.concatenate([high, middle, low], axis=0)


def permute_columns(x, select):
    rows = x.shape[0]
    y = jnp.dot(split_bf16(x), select, preferred_element_type=F32)
    return (y[2 * rows :] + y[rows : 2 * rows]) + y[:rows]


def store_shifted(ref, row, pair):
    for dx, shifted in enumerate((west_of(pair), pair, east_of(pair))):
        for tile in range(2):
            ref[tile, row, 16 * dx : 16 * dx + 16, :] = shifted[tile].astype(BF16)


def patch(ref, row):
    return jnp.concatenate([ref[tile, row : row + 3].reshape(144, LANES) for tile in range(2)], axis=1)


def conv_row(weight, ref, row):
    y = jnp.dot(weight, patch(ref, row), preferred_element_type=F32)
    return (y[:, :LANES], y[:, LANES:])


def contract(left, right):
    return lax.dot_general(left, right, (((1,), (1,)), ((), ())), preferred_element_type=F32)


def kernel(
    sizes,
    temp,
    height,
    flow,
    land_sea,
    fold,
    w_first,
    w_second,
    w_third,
    temp_bar,
    height_bar,
    flow_bar,
    temp_out,
    height_out,
    flow_out,
    first_out,
    second_out,
    third_out,
    surf,
    trac,
    inputs,
    wet_i,
    bar_t,
    bar_h,
    bar_f,
    fold_s,
    w1_raw,
    w2_raw,
    w3_raw,
    w_rows,
    w_flip,
    msg_out,
    msg_in,
    fold_surf,
    fold_trac,
    select_in,
    select_out,
    g3_rows,
    xs1,
    xs2,
    xs3,
    gs1,
    gs2,
    gs3,
    act1,
    act2,
    back,
    sg,
    tg,
    back_out,
    back_in,
    back_surf,
    back_trac,
    unfold_surf,
    unfold_trac,
    unfold_edge,
    halves,
    half_in,
    plane_in,
    column_in,
    totals,
    load_sem,
    f_send,
    f_recv,
    m_send,
    m_recv,
    fold_send,
    fold_recv,
    b_send,
    b_recv,
    bm_send,
    bm_recv,
    unfold_send,
    unfold_recv,
    pair_send,
    pair_recv,
    plane_send,
    plane_recv,
    column_send,
    column_recv,
):
    nlon, nlat, nens = sizes
    lon, lat, ens = lax.axis_index("lon"), lax.axis_index("lat"), lax.axis_index("ens")
    top = nlat - 1
    left, right = lax.rem(lon + nlon - 1, nlon), lax.rem(lon + 1, nlon)
    nz, ny = nlon // 2, nlat // 2
    core, z = lax.rem(lat, 2), lax.rem(lon, nz)
    plane = 2 * ny * nens
    place = (ens * 2 + lon // nz) * ny + lat // 2

    def remote(src, dst, send, recv, **device):
        return pltpu.make_async_remote_copy(
            src_ref=src, dst_ref=dst, send_sem=send, recv_sem=recv, device_id=device, device_id_type=MESH
        )

    loads = [
        (temp.at[0], trac.at[0, :, 8:24, :]),
        (height.at[0], surf.at[0, 0, 16:32, :]),
        (flow.at[0], surf.at[0, 1:3, 16:32, :]),
        (land_sea, wet_i),
        (fold, fold_s),
        (w_first, w1_raw),
        (w_second, w2_raw),
        (w_third, w3_raw),
        (temp_bar.at[0], bar_t),
        (height_bar.at[0], bar_h),
        (flow_bar.at[0], bar_f),
    ]
    loads = [pltpu.make_async_copy(src, dst, load_sem.at[k]) for k, (src, dst) in enumerate(loads)]
    for load in loads:
        load.start()

    barrier = pltpu.get_barrier_semaphore()

    def greet(**device):
        pl.semaphore_signal(barrier, inc=1, device_id=device, device_id_type=MESH)

    def bits(value, size):
        return [lax.rem(value // 2**k, 2) for k in range(size.bit_length() - 1)]

    def flip(value, digits, mask):
        return value + sum((1 - 2 * digit) * 2**k for k, digit in enumerate(digits) if mask >> k & 1)

    def reach(mask):
        return (0, 1, 2, 3, 4, 3, 2, 3)[mask] if mask < 8 else 1 + reach(mask - 8)

    def plane_reach(mask):
        return sum((0, 1, 2, 1)[part] for part in (mask // ny, mask % ny))

    x, y = ens * 2 + lon // nz, lat // 2
    x_bits, y_bits, lon_bits = bits(x, 2 * nens), bits(y, ny), bits(lon, nlon)
    plane_masks = sorted(range(1, plane), key=plane_reach, reverse=True)
    column_masks = sorted(range(1, nz), key=reach, reverse=True)
    lon_masks = sorted(range(1, nlon), key=reach, reverse=True)

    def plane_peer(mask):
        px, py = flip(x, x_bits, mask // ny), flip(y, y_bits, mask % ny)
        device = dict(lon=lax.rem(px, 2) * nz + z, lat=py * 2 + core, ens=px // 2)
        return px * ny + py, device

    def lon_peer(mask):
        return flip(lon, lon_bits, mask)

    for mask in plane_masks:
        greet(**plane_peer(mask)[1])
    for mask in column_masks:
        greet(lon=lon_peer(mask))
    greet(lon=left)
    greet(lon=right)

    @pl.when(lat > 0)
    def _():
        greet(lat=lat - 1)
        greet(lon=left, lat=lat - 1)
        greet(lon=right, lat=lat - 1)

    @pl.when(lat < top)
    def _():
        greet(lat=lat + 1)
        greet(lon=left, lat=lat + 1)
        greet(lon=right, lat=lat + 1)

    @pl.when(lat == top)
    def _():
        for mask in lon_masks:
            greet(lon=lon_peer(mask))

    inputs[:, 32 * (HCH + 1) :, :] = jnp.zeros((2, 32 * (15 - HCH), LANES), F32)
    for ref, rows in ((gs3, 20), (gs2, 22), (gs1, 24)):
        for tile in range(2):
            for row in (0, 1, rows - 2, rows - 1):
                ref[tile, row] = jnp.zeros((48, LANES), BF16)
    back[...] = jnp.zeros_like(back)
    for ref in (unfold_surf, unfold_trac):
        ref[lon, 24:32, :] = jnp.zeros((8, LANES), F32)
    unfold_edge[:, 24:32, :] = jnp.zeros((2, 8, LANES), F32)

    @pl.when(lat == 0)
    def _():
        surf[:, :, 0:16, :] = jnp.zeros((2, 4, 16, LANES), F32)
        trac[:, :, 0:8, :] = jnp.zeros((2, LEV, 8, LANES), F32)
        back_in[:, 0] = jnp.zeros((2, 2, 16, LANES), F32)
        back_surf[0] = jnp.zeros((3, 16, LANES), F32)
        back_trac[0] = jnp.zeros((LEV, 8, LANES), F32)

    @pl.when(lat == top)
    def _():
        surf[:, :, 32:48, :] = jnp.zeros((2, 4, 16, LANES), F32)
        trac[:, :, 24:32, :] = jnp.zeros((2, LEV, 8, LANES), F32)
        back_in[:, 2] = jnp.zeros((2, 2, 16, LANES), F32)
        back_surf[1] = jnp.zeros((3, 16, LANES), F32)
        back_trac[1] = jnp.zeros((LEV, 8, LANES), F32)

    for k in (1, 2, 3, 0):
        loads[k].wait()
    surf[0, 3, 16:32, :] = wet_i[...].astype(F32)
    msg_out[0] = pack_edges([surf[0, f, 16:32, :] for f in range(4)], RIM)
    msg_out[1] = pack_edges([trac[0, c, 8:24, :] for c in range(LEV)], TRIM)

    def lat_copies(up):
        to = 1 if up else -1
        rows_s = slice(0, 16) if up else slice(32, 48)
        rows_t = (slice(16, 24), slice(0, 8)) if up else (slice(8, 16), slice(24, 32))
        slot = 0 if up else 2
        return (
            remote(surf.at[0, :, 16:32, :], surf.at[0, :, rows_s, :], f_send.at[slot], f_recv.at[slot], lat=lat + to),
            remote(
                trac.at[0, :, rows_t[0], :],
                trac.at[0, :, rows_t[1], :],
                f_send.at[slot + 1],
                f_recv.at[slot + 1],
                lat=lat + to,
            ),
        )

    def edge_copy(side, shift):
        slot = 3 * side + 1 - shift
        return remote(
            msg_out, msg_in.at[side, 1 - shift], m_send.at[slot], m_recv.at[slot], lon=(right, left)[side], lat=lat + shift
        )

    def lon_copy(ref, mask, send, recv, arrival=False):
        peer = lon_peer(mask)
        return remote(ref.at[lon], ref.at[peer if arrival else lon], send.at[mask], recv.at[mask], lon=peer)

    def ghost_rows(width, count):
        full = [(f, m) for f in range(min(count, CL)) for m in range(width)]
        return full + [(f, 0) for f in range(CL, count)]

    @pl.when(lat == top)
    def _():
        for row, (f, m) in enumerate(ghost_rows(RIM, 4)):
            fold_surf[lon, row : row + 1, :] = surf[0, f, 31 - m : 32 - m, :]
        for row, (c, m) in enumerate(ghost_rows(TRIM, LEV)):
            fold_trac[lon, row : row + 1, :] = trac[0, c, 23 - m : 24 - m, :]

    pl.semaphore_wait(
        barrier,
        (plane - 1)
        + (nz - 1)
        + 2
        + 3 * (lat > 0).astype(jnp.int32)
        + 3 * (lat < top).astype(jnp.int32)
        + (nlon - 1) * (lat == top).astype(jnp.int32),
    )

    def for_lat(fn):
        pl.when(lat > 0)(functools.partial(fn, -1))
        fn(0)
        pl.when(lat < top)(functools.partial(fn, 1))

    @pl.when(lat == top)
    def _():
        for mask in lon_masks:
            lon_copy(fold_surf, mask, fold_send.at[0], fold_recv.at[0]).start()

    def start_forward(shift):
        if shift:
            for copy in lat_copies(shift > 0):
                copy.start()
        for side in range(2):
            edge_copy(side, shift).start()

    for_lat(start_forward)

    @pl.when(lat == top)
    def _():
        for mask in lon_masks:
            lon_copy(fold_trac, mask, fold_send.at[1], fold_recv.at[1]).start()

    for k in range(4, 11):
        loads[k].wait()
    raw1 = w1_raw[...].astype(F32)
    w_rows[...] = jnp.zeros_like(w_rows)
    for tap in range(9):
        w_rows[0, :, 16 * tap : 16 * tap + CL] = raw1[:, 11 * tap : 11 * tap + CL]
        w_rows[0, :, 16 * tap + HCH : 16 * tap + HCH + 1] = raw1[:, 11 * tap + CL : 11 * tap + CL + 1]
    w_rows[1, :, 0:144] = w2_raw[...].astype(F32)
    w_rows[2, 0:CL, 0:144] = w3_raw[...].astype(F32)
    for layer in range(3):
        first = jnp.transpose(w_rows[layer, :, 0:128])
        second = jnp.transpose(w_rows[layer, :, 128:256])
        for tap in range(9):
            block = second[0:16, :] if tap == 8 else first[16 * tap : 16 * tap + 16, :]
            w_flip[layer, :, 16 * (8 - tap) : 16 * (8 - tap) + 16] = block
    weight1 = w_rows[0, :, 0:144].astype(BF16)
    weight2 = w_rows[1, :, 0:144].astype(BF16)
    flip1, flip2, flip3 = (w_flip[layer].astype(BF16) for layer in range(3))

    wet_own = surf[0, 3, 16:32, :]
    g3_rows[16 * CL :, :] = jnp.zeros((16 * (16 - CL), LANES), F32)
    for c in range(CL):
        g3_rows[16 * c : 16 * c + 16, :] = closure_gain * wet_own * bar_t[c]
    for row in range(16):
        own = g3_rows[pl.ds(row, 16, stride=16), :]
        store_shifted(gs3, row + 2, (own, jnp.zeros_like(own)))

    shift_s = fold_s[0] + 1
    base = shift_s - (LANES + RIM) - LANES * lon + LANES * (2 * nlon)
    tile0 = base // LANES
    offset = shift_s - 1 - LANES * lon + LANES * (2 * nlon) - LANES * tile0

    def mirrored(ref):
        return jnp.concatenate([ref[lax.rem(tile0 + j, nlon)] for j in range(3)], axis=1)

    @pl.when(lat == top)
    def _():
        source = lax.broadcasted_iota(jnp.int32, (3 * LANES, 2 * LANES), 0)
        column = lax.broadcasted_iota(jnp.int32, (3 * LANES, 2 * LANES), 1)
        column = jnp.where(column < LANES + LANES // 2, column, column - 2 * LANES)
        select_in[...] = jnp.where(source + column == offset, 1.0, 0.0).astype(BF16)
        lane = lax.broadcasted_iota(jnp.int32, (LANES, LANES), 0)
        column = lax.broadcasted_iota(jnp.int32, (LANES, LANES), 1)
        halo = jnp.where(lane < LANES // 2, lane + LANES, lane - LANES)
        for k, at in enumerate((lane, halo)):
            for j in range(3):
                first = LANES * (3 * k + j)
                select_out[first : first + LANES, :] = jnp.where(at + LANES * j + column == offset, 1.0, 0.0).astype(
                    BF16
                )

    left_s = slot_mask(16, RIM, 4, 0)
    left_t = slot_mask(16, TRIM, LEV, 0)

    def wait_forward(shift):
        k = shift + 1
        if shift:
            for copy in lat_copies(shift < 0):
                copy.wait_recv()
        for side in range(2):
            edge_copy(side, -shift).wait_recv()
        packed = jnp.where(left_s, msg_in[0, k, 0], msg_in[1, k, 0])
        for f in range(4):
            surf[1, f, 16 * k : 16 * k + 16, :] = unpack_edge(packed, RIM, f)
        packed = jnp.where(left_t, msg_in[0, k, 1], msg_in[1, k, 1])
        rows, at = ((slice(8, 16), 0), (slice(0, 16), 8), (slice(0, 8), 24))[k]
        packed = packed[rows]
        for c in range(LEV):
            trac[1, c, at : at + packed.shape[0], :] = unpack_edge(packed, TRIM, c)

    for_lat(wait_forward)

    @pl.when(lat == top)
    def _():
        for mask in lon_masks:
            lon_copy(fold_surf, mask, fold_send.at[0], fold_recv.at[0], True).wait_recv()
        window = jnp.concatenate([mirrored(fold_surf), jnp.zeros((8, 3 * LANES), F32)], axis=0)
        ghost = permute_columns(window, select_in[...])
        for f in range(4):
            rows = ghost[RIM * f : RIM * f + RIM]
            rows = -rows if f in (1, 2) else rows
            for tile in range(2):
                surf[tile, f, 32 : 32 + RIM, :] = rows[:, LANES * tile : LANES * tile + LANES]

    h, e, n, wet = (tuple(surf[tile, f] for tile in range(2)) for f in range(4))
    for _ in range(SUB):
        h, e, n = step_forward(h, e, n, wet)
    new_e, new_n = e[0][16:32], n[0][16:32]

    @pl.when(lat == top)
    def _():
        for mask in lon_masks:
            lon_copy(fold_trac, mask, fold_send.at[1], fold_recv.at[1], True).wait_recv()
        ghost = permute_columns(mirrored(fold_trac), select_in[...])
        for c in range(LEV):
            first, count = (TRIM * c, TRIM) if c < CL else (TRIM * CL + c - CL, 1)
            for tile in range(2):
                trac[tile, c, 24 : 24 + count, :] = ghost[first : first + count, LANES * tile : LANES * tile + LANES]

    for tile in range(2):
        for c in range(LEV):
            inputs[tile, 32 * c : 32 * c + 32, :] = trac[tile, c]
        inputs[tile, 32 * HCH : 32 * HCH + 32, :] = h[tile][8:40]
    for row in range(22):
        store_shifted(xs1, row, tuple(inputs[tile, pl.ds(5 + row, 16, stride=32), :] for tile in range(2)))
    for row in range(20):
        act = lift(jnp.tanh)(conv_row(weight1, xs1, row))
        for tile in range(2):
            act1[tile, row] = act[tile]
        store_shifted(xs2, row, act)
    for row in range(18):
        act = lift(jnp.tanh)(conv_row(weight2, xs2, row))
        for tile in range(2):
            act2[tile, row] = act[tile]
        store_shifted(xs3, row, act)

    def weight_sum(gs, xs, rows):
        total = jnp.zeros((16, 144), F32)
        for row in range(rows):
            grad = jnp.concatenate([gs[tile, row + 2, 16:32, :] for tile in range(2)], axis=1)
            total = total + contract(grad, patch(xs, row))
        return total

    def back_layer(weight, gs, act_ref, out, rows):
        for row in range(rows):
            grad = conv_row(weight, gs, row)
            act = tuple(act_ref[tile, row] for tile in range(2))
            store_shifted(out, row + 2, lift(lambda g, a: g * (1.0 - a * a))(grad, act))

    sum3 = weight_sum(gs3, xs3, 16)
    back_layer(flip3, gs3, act2, gs2, 18)
    sum2 = weight_sum(gs2, xs2, 18)
    back_layer(flip2, gs2, act1, gs1, 20)
    sum1 = weight_sum(gs1, xs1, 20)

    tail = jnp.concatenate([sum1[:, 128:144], sum2[:, 128:144], sum3[:, 128:144], jnp.zeros((16, 80), F32)], axis=1)
    tail = jnp.concatenate([tail[0:6, 0:48], tail[6:12, 0:48], tail[10:16, 0:32]], axis=1)
    rows = jnp.concatenate([sum1[:, :128], sum2[:, :128], sum3[0:CL, :128], tail], axis=0)
    halves[0] = rows[0:24]
    halves[1] = rows[24:48]

    def half_copy():
        return remote(halves.at[1 - core], half_in, pair_send.at[0], pair_recv.at[0], lat=lat + 1 - 2 * core)

    def plane_copy(mask, arrival=False):
        other, device = plane_peer(mask)
        slot = other if arrival else place
        return remote(plane_in.at[place], plane_in.at[slot], plane_send.at[mask], plane_recv.at[mask], **device)

    def column_copy(mask, arrival=False):
        peer = lon_peer(mask)
        slot = lax.rem(peer, nz) if arrival else z
        return remote(column_in.at[z], column_in.at[slot], column_send.at[mask], column_recv.at[mask], lon=peer)

    def total_copy(arrival=False):
        slot = 1 - core if arrival else core
        return remote(totals.at[core], totals.at[slot], pair_send.at[1], pair_recv.at[1], lat=lat + 1 - 2 * core)

    def sum_slots(ref, count):
        total = ref[0]
        for k in range(1, count):
            total = total + ref[k]
        return total

    half_copy().start()

    for row in range(22):
        grad = conv_row(flip1, gs1, row)
        for tile in range(2):
            back[tile, pl.ds(5 + row, 16, stride=32), :] = grad[tile]

    lane16 = lane_iota(16)
    zero8 = jnp.zeros((8, LANES), F32)
    sum_e = jnp.zeros((16, LANES), F32)
    sum_n = jnp.zeros((16, LANES), F32)
    for c in range(LEV):
        bar = bar_t[c]
        wb = wet_own * bar
        own, halo = trac[0, c, 8:24, :], trac[1, c, 8:24, :]
        ahead = jnp.where(lane16 == LANES - 1, pltpu.roll(halo, LANES - 1, 1), pltpu.roll(own, LANES - 1, 1))
        behind = jnp.where(lane16 == 0, pltpu.roll(halo, 1, 1), pltpu.roll(own, 1, 1))
        sum_e = sum_e + wb * (ahead - behind)
        sum_n = sum_n + wb * (trac[0, c, 9:25, :] - trac[0, c, 7:23, :])
        qe = (0.5 * advection) * new_e * wb
        qn = (0.5 * advection) * new_n * wb
        wd = diffusion * wb
        up = pltpu.roll(wd + qe, LANES - 1, 1)
        down = pltpu.roll(wd - qe, 1, 1)
        middle = (
            bar - 4.0 * wd + jnp.where(lane16 < LANES - 1, up, 0.0) + jnp.where(lane16 > 0, down, 0.0)
        )
        side = jnp.where(lane16 == LANES - 1, up, jnp.where(lane16 == 0, down, 0.0))
        above = pltpu.roll(jnp.concatenate([zero8, wd + qn, zero8], axis=0), 31, 0)
        below = pltpu.roll(jnp.concatenate([zero8, wd - qn, zero8], axis=0), 1, 0)
        main = jnp.concatenate([zero8, middle, zero8], axis=0) + above + below
        side = jnp.concatenate([zero8, side, zero8], axis=0)
        if c < CL:
            main = main + back[0, 32 * c : 32 * c + 32, :]
            side = side + back[1, 32 * c : 32 * c + 32, :]
        tg[0, c] = main
        tg[1, c] = side

    def lat_back(up):
        to = 1 if up else -1
        rows_s = slice(32, 48) if up else slice(0, 16)
        rows_t = slice(24, 32) if up else slice(0, 8)
        slot = 0 if up else 1
        return (
            remote(sg.at[0, :, rows_s, :], back_surf.at[slot], b_send.at[0, slot], b_recv.at[0, slot], lat=lat + to),
            remote(tg.at[0, :, rows_t, :], back_trac.at[slot], b_send.at[1, slot], b_recv.at[1, slot], lat=lat + to),
        )

    def pack_ghosts(grads, first, count, width, out, edge):
        for row, (f, m) in enumerate(ghost_rows(width, count)):
            out[lon, row : row + 1, :] = grads[0, f, first + m : first + m + 1, :]
            edge[row : row + 1, :] = grads[1, f, first + m : first + m + 1, :]
        out[lon, 32:40, :] = pack_edges([edge[8 * g : 8 * g + 8, :] for g in range(4)], width)

    @pl.when(lat == top)
    def _():
        pack_ghosts(tg, 24, LEV, TRIM, unfold_trac, unfold_edge.at[0])
        for mask in lon_masks:
            lon_copy(unfold_trac, mask, unfold_send.at[1], unfold_recv.at[1]).start()

    pl.when(lat > 0)(lambda: lat_back(False)[1].start())
    pl.when(lat < top)(lambda: lat_back(True)[1].start())

    half_copy().wait_recv()
    plane_in[place] = halves[core] + half_in[...]
    for mask in plane_masks:
        plane_copy(mask).start()

    def own_rows(x):
        zero16 = jnp.zeros((16, LANES), F32)
        return (jnp.concatenate([zero16, x, zero16], axis=0), jnp.zeros((48, LANES), F32))

    e = own_rows(bar_f[0] - (0.5 * advection) * sum_e)
    n = own_rows(bar_f[1] - (0.5 * advection) * sum_n)
    rim = tuple(jnp.concatenate([zero8, back[tile, 32 * HCH : 32 * HCH + 32, :], zero8], axis=0) for tile in range(2))
    h = lift(lambda a, b: a + b)(rim, own_rows(bar_h[...]))
    wet = tuple(surf[tile, 3] for tile in range(2))
    for index in range(SUB):
        h, e, n = step_adjoint(h, e, n, wet)
    for f, pair in enumerate((h, e, n)):
        for tile in range(2):
            sg[tile, f] = pair[tile]

    for block in range(3):
        back_out[block, 0] = pack_edges([sg[1, f, 16 * block : 16 * block + 16, :] for f in range(3)], RIM)
        if block == 1:
            fields = [tg[1, c, 8:24, :] for c in range(LEV)]
        elif block == 0:
            fields = [jnp.concatenate([zero8, tg[1, c, 0:8, :]], axis=0) for c in range(LEV)]
        else:
            fields = [jnp.concatenate([tg[1, c, 24:32, :], zero8], axis=0) for c in range(LEV)]
        back_out[block, 1] = pack_edges(fields, TRIM)

    def edge_back(side, block):
        return remote(
            back_out.at[block],
            back_in.at[side, 2 - block],
            bm_send.at[side, 2 - block],
            bm_recv.at[side, 2 - block],
            lon=(right, left)[side],
            lat=lat + block - 1,
        )

    @pl.when(lat == top)
    def _():
        pack_ghosts(sg, 32, 3, RIM, unfold_surf, unfold_edge.at[1])
        for mask in lon_masks:
            lon_copy(unfold_surf, mask, unfold_send.at[0], unfold_recv.at[0]).start()

    def start_back(shift):
        if shift:
            lat_back(shift > 0)[0].start()
        for side in range(2):
            edge_back(side, shift + 1).start()

    for_lat(start_back)

    right_s = slot_mask(16, RIM, 3, RIM)
    right_t = slot_mask(16, TRIM, LEV, TRIM)

    def sent_forward(shift):
        if shift:
            for copy in lat_copies(shift > 0):
                copy.wait_send()
        for side in range(2):
            edge_copy(side, shift).wait_send()

    for_lat(sent_forward)

    @pl.when(lat == top)
    def _():
        for mask in lon_masks:
            for part, ref in enumerate((fold_surf, fold_trac)):
                lon_copy(ref, mask, fold_send.at[part], fold_recv.at[part]).wait_send()

    half_copy().wait_send()
    for mask in plane_masks:
        plane_copy(mask).wait_send()

    for mask in plane_masks:
        plane_copy(mask, True).wait_recv()
    column_in[z] = sum_slots(plane_in, plane)
    for mask in column_masks:
        column_copy(mask).start()

    def wait_back(shift):
        if shift:
            for copy in lat_back(shift < 0):
                copy.wait_recv()
        for side in range(2):
            edge_back(side, 1 - shift).wait_recv()

    for_lat(wait_back)

    from_left = back_in[0, 0] + back_in[0, 1] + back_in[0, 2]
    from_right = back_in[1, 0] + back_in[1, 1] + back_in[1, 2]
    packed = jnp.where(right_s, from_left[0], from_right[0])
    for f in range(3):
        total = sg[0, f, 16:32, :] + back_surf[0, f] + back_surf[1, f] + unpack_edge(packed, RIM, f)
        if f == 0:
            height_out[0] = total
        else:
            flow_out[0, f - 1] = total
    packed = jnp.where(right_t, from_left[1], from_right[1])
    for c in range(LEV):
        ghosts = jnp.concatenate([back_trac[0, c], back_trac[1, c]], axis=0)
        temp_out[0, c] = tg[0, c, 8:24, :] + ghosts + unpack_edge(packed, TRIM, c)

    def sent_back(shift):
        if shift:
            for copy in lat_back(shift > 0):
                copy.wait_send()
        for side in range(2):
            edge_back(side, shift + 1).wait_send()

    for_lat(sent_back)

    for mask in column_masks:
        column_copy(mask, True).wait_recv()
    totals[core] = sum_slots(column_in, nz)
    total_copy().start()

    @pl.when(lat == top)
    def _():
        def unfold(ref, width):
            tiles = [ref[lax.rem(tile0 + j, nlon)] for j in range(3)]
            edges = [
                jnp.concatenate([unpack_edge(tile[32:40], width, g) for g in range(4)], axis=0) for tile in tiles
            ]
            return permute_columns(jnp.concatenate([tile[0:32] for tile in tiles] + edges, axis=1), select_out[...])

        for mask in lon_masks:
            lon_copy(unfold_trac, mask, unfold_send.at[1], unfold_recv.at[1], True).wait_recv()
        ghost = unfold(unfold_trac, TRIM)
        for row, (c, m) in enumerate(ghost_rows(TRIM, LEV)):
            temp_out[0, c, 15 - m : 16 - m, :] = temp_out[0, c, 15 - m : 16 - m, :] + ghost[row : row + 1]
        for mask in lon_masks:
            lon_copy(unfold_surf, mask, unfold_send.at[0], unfold_recv.at[0], True).wait_recv()
        ghost = unfold(unfold_surf, RIM)
        for row, (f, m) in enumerate(ghost_rows(RIM, 3)):
            if f == 0:
                height_out[0, 15 - m : 16 - m, :] = height_out[0, 15 - m : 16 - m, :] + ghost[row : row + 1]
            else:
                flow_out[0, f - 1, 15 - m : 16 - m, :] = flow_out[0, f - 1, 15 - m : 16 - m, :] - ghost[row : row + 1]

    total_copy(True).wait_recv()
    scale = 1.0 / math.sqrt(nens * nlat * 16 * nlon * LANES)
    rows = jnp.concatenate([totals[0], totals[1]], axis=0) * scale
    tail = rows[32 + CL : 48]
    tail = jnp.concatenate(
        [tail[:, 0:48], tail[:, 48:96], jnp.concatenate([tail[2:6, 96:128], jnp.zeros((4, 16), F32)], axis=1)], axis=0
    )
    for layer, out in ((1, second_out), (2, third_out)):
        count = out.shape[0]
        out[:, 0:128] = rows[16 * layer : 16 * layer + count]
        out[:, 128:144] = tail[0:count, 16 * layer : 16 * layer + 16]
    for tap in range(9):
        block = tail[:, 0:16] if tap == 8 else rows[0:16, 16 * tap : 16 * tap + 16]
        first_out[:, 11 * tap : 11 * tap + CL] = block[:, 0:CL]
        first_out[:, 11 * tap + CL : 11 * tap + CL + 1] = block[:, HCH : HCH + 1]

    for mask in column_masks:
        column_copy(mask).wait_send()
    total_copy().wait_send()

    @pl.when(lat == top)
    def _():
        for mask in lon_masks:
            for part, ref in enumerate((unfold_surf, unfold_trac)):
                lon_copy(ref, mask, unfold_send.at[part], unfold_recv.at[part]).wait_send()


def hand_over(*refs):
    sources, targets, sem = refs[:6], refs[6:12], refs[12]
    copies = [pltpu.make_async_copy(src, dst, sem.at[k]) for k, (src, dst) in enumerate(zip(sources, targets))]
    for copy in copies:
        copy.start()
    for copy in copies:
        copy.wait()


def solution(mesh):
    nlon, nlat, nens = (mesh.shape[axis] for axis in ("lon", "lat", "ens"))
    plane = nlat * nens

    def local(temp, height, flow, land_sea, fold, w_first, w_second, w_third, temp_bar, height_bar, flow_bar):
        vmem = pltpu.VMEM
        dma = pltpu.SemaphoreType.DMA
        scratch = [
            vmem((2, 4, 48, LANES), F32),
            vmem((2, LEV, 32, LANES), F32),
            vmem((2, 16 * 32, LANES), F32),
            vmem((16, LANES), jnp.int32),
            vmem((LEV, 16, LANES), F32),
            vmem((16, LANES), F32),
            vmem((2, 16, LANES), F32),
            pltpu.SMEM(fold.shape, jnp.int32),
            vmem(w_first.shape, BF16),
            vmem(w_second.shape, BF16),
            vmem(w_third.shape, BF16),
            vmem((3, 16, 256), F32),
            vmem((3, 16, 144), F32),
            vmem((2, 16, LANES), F32),
            vmem((2, 3, 2, 16, LANES), F32),
            vmem((nlon, 40, LANES), F32),
            vmem((nlon, 32, LANES), F32),
            vmem((3 * LANES, 2 * LANES), BF16),
            vmem((6 * LANES, LANES), BF16),
            vmem((16 * 16, LANES), F32),
            vmem((2, 22, 48, LANES), BF16),
            vmem((2, 20, 48, LANES), BF16),
            vmem((2, 18, 48, LANES), BF16),
            vmem((2, 24, 48, LANES), BF16),
            vmem((2, 22, 48, LANES), BF16),
            vmem((2, 20, 48, LANES), BF16),
            vmem((2, 20, 16, LANES), F32),
            vmem((2, 18, 16, LANES), F32),
            vmem((2, 16 * 32, LANES), F32),
            vmem((2, 3, 48, LANES), F32),
            vmem((2, LEV, 32, LANES), F32),
            vmem((3, 2, 16, LANES), F32),
            vmem((2, 3, 2, 16, LANES), F32),
            vmem((2, 3, 16, LANES), F32),
            vmem((2, LEV, 8, LANES), F32),
            vmem((nlon, 40, LANES), F32),
            vmem((nlon, 40, LANES), F32),
            vmem((2, 32, LANES), F32),
            vmem((2, 24, LANES), F32),
            vmem((24, LANES), F32),
            vmem((plane, 24, LANES), F32),
            vmem((nlon // 2, 24, LANES), F32),
            vmem((2, 24, LANES), F32),
            dma((11,)),
            dma((4,)),
            dma((4,)),
            dma((6,)),
            dma((6,)),
            dma((2, nlon)),
            dma((2, nlon)),
            dma((2, 2)),
            dma((2, 2)),
            dma((2, 4)),
            dma((2, 4)),
            dma((2, nlon)),
            dma((2, nlon)),
            dma((2,)),
            dma((2,)),
            dma((plane,)),
            dma((plane,)),
            dma((nlon // 2,)),
            dma((nlon // 2,)),
        ]
        out_shape = (
            jax.ShapeDtypeStruct(temp.shape, F32),
            jax.ShapeDtypeStruct(height.shape, F32),
            jax.ShapeDtypeStruct(flow.shape, F32),
            jax.ShapeDtypeStruct(w_first.shape, F32),
            jax.ShapeDtypeStruct(w_second.shape, F32),
            jax.ShapeDtypeStruct(w_third.shape, F32),
        )
        results = pl.pallas_call(
            functools.partial(kernel, (nlon, nlat, nens)),
            out_shape=tuple(pltpu.VMEM(o.shape, F32) for o in out_shape),
            in_specs=[pl.BlockSpec(memory_space=pltpu.HBM)] * 11,
            out_specs=[pl.BlockSpec(memory_space=pltpu.VMEM)] * 6,
            scratch_shapes=scratch,
            compiler_params=pltpu.CompilerParams(
                collective_id=0, has_side_effects=True, vmem_limit_bytes=60 * 1024 * 1024
            ),
        )(temp, height, flow, land_sea, fold, w_first, w_second, w_third, temp_bar, height_bar, flow_bar)
        return pl.pallas_call(
            hand_over,
            out_shape=out_shape,
            in_specs=[pl.BlockSpec(memory_space=pl.ANY)] * 6,
            out_specs=[pl.BlockSpec(memory_space=pltpu.HBM)] * 6,
            scratch_shapes=[dma((6,))],
            compiler_params=pltpu.CompilerParams(vmem_limit_bytes=1024 * 1024),
        )(*results)

    field = P("ens", None, "lat", "lon")
    surface = P("ens", "lat", "lon")
    return jax.shard_map(
        local,
        mesh=mesh,
        in_specs=(field, surface, field, P("lat", "lon"), P(), P(), P(), P(), field, surface, field),
        out_specs=(field, surface, field, P(), P(), P()),
        check_vma=False,
    )
```

```python
import functools
import math

import jax
import jax.numpy as jnp
from jax import lax
from jax.experimental import pallas as pl
from jax.experimental.pallas import tpu as pltpu
from jax.sharding import PartitionSpec as P

MESH = pl.DeviceIdType.MESH
F32 = jnp.float32
BF16 = jnp.bfloat16

SUB = 4
LEV = 12
CL = 10
RIM = 10
TRIM = 3
HCH = 12
LANES = 128

gravity = 0.3
drag_rate = 0.05
coriolis = 0.2
diffusion = 0.1
advection = 0.1
closure_gain = 0.5


def lane_iota(rows):
    return lax.broadcasted_iota(jnp.int32, (rows, LANES), 1)


def east_of(x):
    a, b = (pltpu.roll(v, LANES - 1, 1) for v in x)
    edge = lane_iota(a.shape[0]) == LANES - 1
    return (jnp.where(edge, b, a), jnp.where(edge, a, b))


def west_of(x):
    a, b = (pltpu.roll(v, 1, 1) for v in x)
    edge = lane_iota(a.shape[0]) == 0
    return (jnp.where(edge, b, a), jnp.where(edge, a, b))


def north_of(x):
    return tuple(pltpu.roll(v, v.shape[0] - 1, 0) for v in x)


def south_of(x):
    return tuple(pltpu.roll(v, 1, 0) for v in x)


def lift(fn):
    return lambda *pairs: tuple(fn(*vs) for vs in zip(*pairs))


sub2 = lift(lambda u, v: u - v)


def step_forward(h, e, n, w):
    de = sub2(east_of(e), west_of(e))
    dn = sub2(north_of(n), south_of(n))
    h = lift(lambda w_, h_, a, b: w_ * (h_ - (0.5 * gravity) * (a + b)))(w, h, de, dn)
    se = sub2(east_of(h), west_of(h))
    sn = sub2(north_of(h), south_of(h))
    keep = 1.0 - drag_rate
    e_new = lift(lambda w_, e_, n_, s: w_ * (keep * e_ - (0.5 * gravity) * s + coriolis * n_))(w, e, n, se)
    n_new = lift(lambda w_, e_, n_, s: w_ * (keep * n_ - (0.5 * gravity) * s - coriolis * e_))(w, e, n, sn)
    return h, e_new, n_new


def step_adjoint(h, e, n, w):
    we = lift(lambda a, b: a * b)(w, e)
    wn = lift(lambda a, b: a * b)(w, n)
    de = sub2(east_of(we), west_of(we))
    dn = sub2(north_of(wn), south_of(wn))
    hw = lift(lambda w_, h_, a, b: w_ * (h_ + (0.5 * gravity) * (a + b)))(w, h, de, dn)
    se = sub2(east_of(hw), west_of(hw))
    sn = sub2(north_of(hw), south_of(hw))
    keep = 1.0 - drag_rate
    e_new = lift(lambda a, b, s: keep * a - coriolis * b + (0.5 * gravity) * s)(we, wn, se)
    n_new = lift(lambda a, b, s: keep * b + coriolis * a + (0.5 * gravity) * s)(we, wn, sn)
    return hw, e_new, n_new


def slot_mask(rows, width, count, offset):
    lane = lane_iota(rows)
    mask = None
    for slot in range(count):
        start = 2 * width * slot + offset
        here = (lane >= start) & (lane < start + width)
        mask = here if mask is None else mask | here
    return mask


def pack_edges(fields, width):
    lane = lane_iota(fields[0].shape[0])
    out = jnp.zeros_like(fields[0])
    for slot, field in enumerate(fields):
        start = 2 * width * slot
        rolled = pltpu.roll(field, (start + width) % LANES, 1)
        out = jnp.where((lane >= start) & (lane < start + 2 * width), rolled, out)
    return out


def unpack_edge(packed, width, slot):
    lane = lane_iota(packed.shape[0])
    rolled = pltpu.roll(packed, (-width - 2 * width * slot) % LANES, 1)
    return jnp.where((lane < width) | (lane >= LANES - width), rolled, 0.0)


def split_bf16(x):
    high = x.astype(BF16)
    rest = x - high.astype(F32)
    middle = rest.astype(BF16)
    low = (rest - middle.astype(F32)).astype(BF16)
    return jnp.concatenate([high, middle, low], axis=0)


def permute_columns(x, select):
    rows = x.shape[0]
    y = jnp.dot(split_bf16(x), select, preferred_element_type=F32)
    return (y[2 * rows :] + y[rows : 2 * rows]) + y[:rows]


def store_shifted(ref, row, pair):
    for dx, shifted in enumerate((west_of(pair), pair, east_of(pair))):
        for tile in range(2):
            ref[tile, row, 16 * dx : 16 * dx + 16, :] = shifted[tile].astype(BF16)


def patch(ref, row):
    return jnp.concatenate([ref[tile, row : row + 3].reshape(144, LANES) for tile in range(2)], axis=1)


def conv_row(weight, ref, row):
    y = jnp.dot(weight, patch(ref, row), preferred_element_type=F32)
    return (y[:, :LANES], y[:, LANES:])


def contract(left, right):
    return lax.dot_general(left, right, (((1,), (1,)), ((), ())), preferred_element_type=F32)


def kernel(
    sizes,
    temp,
    height,
    flow,
    land_sea,
    fold,
    w_first,
    w_second,
    w_third,
    temp_bar,
    height_bar,
    flow_bar,
    temp_out,
    height_out,
    flow_out,
    first_out,
    second_out,
    third_out,
    surf,
    trac,
    inputs,
    wet_i,
    bar_t,
    bar_h,
    bar_f,
    fold_s,
    w1_raw,
    w2_raw,
    w3_raw,
    w_rows,
    w_flip,
    msg_out,
    msg_in,
    fold_surf,
    fold_trac,
    select_in,
    select_out,
    g3_rows,
    xs1,
    xs2,
    xs3,
    gs1,
    gs2,
    gs3,
    act1,
    act2,
    back,
    sg,
    tg,
    back_out,
    back_in,
    back_surf,
    back_trac,
    unfold_surf,
    unfold_trac,
    unfold_edge,
    halves,
    half_in,
    plane_in,
    column_in,
    totals,
    load_sem,
    f_send,
    f_recv,
    m_send,
    m_recv,
    fold_send,
    fold_recv,
    b_send,
    b_recv,
    bm_send,
    bm_recv,
    unfold_send,
    unfold_recv,
    pair_send,
    pair_recv,
    plane_send,
    plane_recv,
    column_send,
    column_recv,
):
    nlon, nlat, nens = sizes
    lon, lat, ens = lax.axis_index("lon"), lax.axis_index("lat"), lax.axis_index("ens")
    top = nlat - 1
    left, right = lax.rem(lon + nlon - 1, nlon), lax.rem(lon + 1, nlon)
    nz, ny = nlon // 2, nlat // 2
    core, z = lax.rem(lat, 2), lax.rem(lon, nz)
    plane = 2 * ny * nens
    place = (ens * 2 + lon // nz) * ny + lat // 2

    def remote(src, dst, send, recv, **device):
        return pltpu.make_async_remote_copy(
            src_ref=src, dst_ref=dst, send_sem=send, recv_sem=recv, device_id=device, device_id_type=MESH
        )

    loads = [
        (temp.at[0], trac.at[0, :, 8:24, :]),
        (height.at[0], surf.at[0, 0, 16:32, :]),
        (flow.at[0], surf.at[0, 1:3, 16:32, :]),
        (land_sea, wet_i),
        (fold, fold_s),
        (w_first, w1_raw),
        (w_second, w2_raw),
        (w_third, w3_raw),
        (temp_bar.at[0], bar_t),
        (height_bar.at[0], bar_h),
        (flow_bar.at[0], bar_f),
    ]
    loads = [pltpu.make_async_copy(src, dst, load_sem.at[k]) for k, (src, dst) in enumerate(loads)]
    for load in loads:
        load.start()

    barrier = pltpu.get_barrier_semaphore()

    def greet(**device):
        pl.semaphore_signal(barrier, inc=1, device_id=device, device_id_type=MESH)

    def bits(value, size):
        return [lax.rem(value // 2**k, 2) for k in range(size.bit_length() - 1)]

    def flip(value, digits, mask):
        return value + sum((1 - 2 * digit) * 2**k for k, digit in enumerate(digits) if mask >> k & 1)

    def reach(mask):
        return (0, 1, 2, 3, 4, 3, 2, 3)[mask] if mask < 8 else 1 + reach(mask - 8)

    def plane_reach(mask):
        return sum((0, 1, 2, 1)[part] for part in (mask // ny, mask % ny))

    x, y = ens * 2 + lon // nz, lat // 2
    x_bits, y_bits, lon_bits = bits(x, 2 * nens), bits(y, ny), bits(lon, nlon)
    plane_masks = sorted(range(1, plane), key=plane_reach, reverse=True)
    column_masks = sorted(range(1, nz), key=reach, reverse=True)
    lon_masks = sorted(range(1, nlon), key=reach, reverse=True)

    def plane_peer(mask):
        px, py = flip(x, x_bits, mask // ny), flip(y, y_bits, mask % ny)
        device = dict(lon=lax.rem(px, 2) * nz + z, lat=py * 2 + core, ens=px // 2)
        return px * ny + py, device

    def lon_peer(mask):
        return flip(lon, lon_bits, mask)

    for mask in plane_masks:
        greet(**plane_peer(mask)[1])
    for mask in column_masks:
        greet(lon=lon_peer(mask))
    greet(lon=left)
    greet(lon=right)

    @pl.when(lat > 0)
    def _():
        greet(lat=lat - 1)
        greet(lon=left, lat=lat - 1)
        greet(lon=right, lat=lat - 1)

    @pl.when(lat < top)
    def _():
        greet(lat=lat + 1)
        greet(lon=left, lat=lat + 1)
        greet(lon=right, lat=lat + 1)

    @pl.when(lat == top)
    def _():
        for mask in lon_masks:
            greet(lon=lon_peer(mask))

    inputs[:, 32 * (HCH + 1) :, :] = jnp.zeros((2, 32 * (15 - HCH), LANES), F32)
    for ref, rows in ((gs3, 20), (gs2, 22), (gs1, 24)):
        for tile in range(2):
            for row in (0, 1, rows - 2, rows - 1):
                ref[tile, row] = jnp.zeros((48, LANES), BF16)
    back[...] = jnp.zeros_like(back)
    for ref in (unfold_surf, unfold_trac):
        ref[lon, 24:32, :] = jnp.zeros((8, LANES), F32)
    unfold_edge[:, 24:32, :] = jnp.zeros((2, 8, LANES), F32)

    @pl.when(lat == 0)
    def _():
        surf[:, :, 0:16, :] = jnp.zeros((2, 4, 16, LANES), F32)
        trac[:, :, 0:8, :] = jnp.zeros((2, LEV, 8, LANES), F32)
        back_in[:, 0] = jnp.zeros((2, 2, 16, LANES), F32)
        back_surf[0] = jnp.zeros((3, 16, LANES), F32)
        back_trac[0] = jnp.zeros((LEV, 8, LANES), F32)

    @pl.when(lat == top)
    def _():
        surf[:, :, 32:48, :] = jnp.zeros((2, 4, 16, LANES), F32)
        trac[:, :, 24:32, :] = jnp.zeros((2, LEV, 8, LANES), F32)
        back_in[:, 2] = jnp.zeros((2, 2, 16, LANES), F32)
        back_surf[1] = jnp.zeros((3, 16, LANES), F32)
        back_trac[1] = jnp.zeros((LEV, 8, LANES), F32)

    for k in (1, 2, 3, 0):
        loads[k].wait()
    surf[0, 3, 16:32, :] = wet_i[...].astype(F32)
    msg_out[0] = pack_edges([surf[0, f, 16:32, :] for f in range(4)], RIM)
    msg_out[1] = pack_edges([trac[0, c, 8:24, :] for c in range(LEV)], TRIM)

    def lat_copies(up):
        to = 1 if up else -1
        rows_s = slice(0, 16) if up else slice(32, 48)
        rows_t = (slice(16, 24), slice(0, 8)) if up else (slice(8, 16), slice(24, 32))
        slot = 0 if up else 2
        return (
            remote(surf.at[0, :, 16:32, :], surf.at[0, :, rows_s, :], f_send.at[slot], f_recv.at[slot], lat=lat + to),
            remote(
                trac.at[0, :, rows_t[0], :],
                trac.at[0, :, rows_t[1], :],
                f_send.at[slot + 1],
                f_recv.at[slot + 1],
                lat=lat + to,
            ),
        )

    def edge_copy(side, shift):
        slot = 3 * side + 1 - shift
        return remote(
            msg_out, msg_in.at[side, 1 - shift], m_send.at[slot], m_recv.at[slot], lon=(right, left)[side], lat=lat + shift
        )

    def lon_copy(ref, mask, send, recv, arrival=False):
        peer = lon_peer(mask)
        return remote(ref.at[lon], ref.at[peer if arrival else lon], send.at[mask], recv.at[mask], lon=peer)

    def ghost_rows(width, count):
        full = [(f, m) for f in range(min(count, CL)) for m in range(width)]
        return full + [(f, 0) for f in range(CL, count)]

    @pl.when(lat == top)
    def _():
        for row, (f, m) in enumerate(ghost_rows(RIM, 4)):
            fold_surf[lon, row : row + 1, :] = surf[0, f, 31 - m : 32 - m, :]
        for row, (c, m) in enumerate(ghost_rows(TRIM, LEV)):
            fold_trac[lon, row : row + 1, :] = trac[0, c, 23 - m : 24 - m, :]

    pl.semaphore_wait(
        barrier,
        (plane - 1)
        + (nz - 1)
        + 2
        + 3 * (lat > 0).astype(jnp.int32)
        + 3 * (lat < top).astype(jnp.int32)
        + (nlon - 1) * (lat == top).astype(jnp.int32),
    )

    def for_lat(fn):
        pl.when(lat > 0)(functools.partial(fn, -1))
        fn(0)
        pl.when(lat < top)(functools.partial(fn, 1))

    def start_forward(shift):
        if shift:
            for copy in lat_copies(shift > 0):
                copy.start()
        for side in range(2):
            edge_copy(side, shift).start()

    for_lat(start_forward)

    @pl.when(lat == top)
    def _():
        for mask in lon_masks:
            lon_copy(fold_surf, mask, fold_send.at[0], fold_recv.at[0]).start()

    @pl.when(lat == top)
    def _():
        for mask in lon_masks:
            lon_copy(fold_trac, mask, fold_send.at[1], fold_recv.at[1]).start()

    for k in range(4, 11):
        loads[k].wait()
    raw1 = w1_raw[...].astype(F32)
    w_rows[...] = jnp.zeros_like(w_rows)
    for tap in range(9):
        w_rows[0, :, 16 * tap : 16 * tap + CL] = raw1[:, 11 * tap : 11 * tap + CL]
        w_rows[0, :, 16 * tap + HCH : 16 * tap + HCH + 1] = raw1[:, 11 * tap + CL : 11 * tap + CL + 1]
    w_rows[1, :, 0:144] = w2_raw[...].astype(F32)
    w_rows[2, 0:CL, 0:144] = w3_raw[...].astype(F32)
    for layer in range(3):
        first = jnp.transpose(w_rows[layer, :, 0:128])
        second = jnp.transpose(w_rows[layer, :, 128:256])
        for tap in range(9):
            block = second[0:16, :] if tap == 8 else first[16 * tap : 16 * tap + 16, :]
            w_flip[layer, :, 16 * (8 - tap) : 16 * (8 - tap) + 16] = block
    weight1 = w_rows[0, :, 0:144].astype(BF16)
    weight2 = w_rows[1, :, 0:144].astype(BF16)
    flip1, flip2, flip3 = (w_flip[layer].astype(BF16) for layer in range(3))

    wet_own = surf[0, 3, 16:32, :]
    g3_rows[16 * CL :, :] = jnp.zeros((16 * (16 - CL), LANES), F32)
    for c in range(CL):
        g3_rows[16 * c : 16 * c + 16, :] = closure_gain * wet_own * bar_t[c]
    for row in range(16):
        own = g3_rows[pl.ds(row, 16, stride=16), :]
        store_shifted(gs3, row + 2, (own, jnp.zeros_like(own)))

    shift_s = fold_s[0] + 1
    base = shift_s - (LANES + RIM) - LANES * lon + LANES * (2 * nlon)
    tile0 = base // LANES
    offset = shift_s - 1 - LANES * lon + LANES * (2 * nlon) - LANES * tile0

    def mirrored(ref):
        return jnp.concatenate([ref[lax.rem(tile0 + j, nlon)] for j in range(3)], axis=1)

    @pl.when(lat == top)
    def _():
        source = lax.broadcasted_iota(jnp.int32, (3 * LANES, 2 * LANES), 0)
        column = lax.broadcasted_iota(jnp.int32, (3 * LANES, 2 * LANES), 1)
        column = jnp.where(column < LANES + LANES // 2, column, column - 2 * LANES)
        select_in[...] = jnp.where(source + column == offset, 1.0, 0.0).astype(BF16)
        lane = lax.broadcasted_iota(jnp.int32, (LANES, LANES), 0)
        column = lax.broadcasted_iota(jnp.int32, (LANES, LANES), 1)
        halo = jnp.where(lane < LANES // 2, lane + LANES, lane - LANES)
        for k, at in enumerate((lane, halo)):
            for j in range(3):
                first = LANES * (3 * k + j)
                select_out[first : first + LANES, :] = jnp.where(at + LANES * j + column == offset, 1.0, 0.0).astype(
                    BF16
                )

    left_s = slot_mask(16, RIM, 4, 0)
    left_t = slot_mask(16, TRIM, LEV, 0)

    def wait_forward(shift):
        k = shift + 1
        if shift:
            for copy in lat_copies(shift < 0):
                copy.wait_recv()
        for side in range(2):
            edge_copy(side, -shift).wait_recv()
        packed = jnp.where(left_s, msg_in[0, k, 0], msg_in[1, k, 0])
        for f in range(4):
            surf[1, f, 16 * k : 16 * k + 16, :] = unpack_edge(packed, RIM, f)
        packed = jnp.where(left_t, msg_in[0, k, 1], msg_in[1, k, 1])
        rows, at = ((slice(8, 16), 0), (slice(0, 16), 8), (slice(0, 8), 24))[k]
        packed = packed[rows]
        for c in range(LEV):
            trac[1, c, at : at + packed.shape[0], :] = unpack_edge(packed, TRIM, c)

    for_lat(wait_forward)

    @pl.when(lat == top)
    def _():
        for mask in lon_masks:
            lon_copy(fold_surf, mask, fold_send.at[0], fold_recv.at[0], True).wait_recv()
        window = jnp.concatenate([mirrored(fold_surf), jnp.zeros((8, 3 * LANES), F32)], axis=0)
        ghost = permute_columns(window, select_in[...])
        for f in range(4):
            rows = ghost[RIM * f : RIM * f + RIM]
            rows = -rows if f in (1, 2) else rows
            for tile in range(2):
                surf[tile, f, 32 : 32 + RIM, :] = rows[:, LANES * tile : LANES * tile + LANES]

    h, e, n, wet = (tuple(surf[tile, f] for tile in range(2)) for f in range(4))
    for _ in range(SUB):
        h, e, n = step_forward(h, e, n, wet)
    new_e, new_n = e[0][16:32], n[0][16:32]

    for tile in range(2):
        for c in range(LEV):
            inputs[tile, 32 * c : 32 * c + 32, :] = trac[tile, c]
        inputs[tile, 32 * HCH : 32 * HCH + 32, :] = h[tile][8:40]

    def activate(weight, xs, act_ref, out, rows):
        for row in rows:
            act = lift(jnp.tanh)(conv_row(weight, xs, row))
            for tile in range(2):
                act_ref[tile, row] = act[tile]
            store_shifted(out, row, act)

    def weight_sum(total, gs, xs, rows):
        for row in rows:
            grad = jnp.concatenate([gs[tile, row + 2, 16:32, :] for tile in range(2)], axis=1)
            total = total + contract(grad, patch(xs, row))
        return total

    def back_layer(weight, gs, act_ref, out, rows):
        for row in rows:
            grad = conv_row(weight, gs, row)
            act = tuple(act_ref[tile, row] for tile in range(2))
            store_shifted(out, row + 2, lift(lambda g, a: g * (1.0 - a * a))(grad, act))

    def closure(ends, sums):
        rows = [range(*pair) for pair in ends]
        for row in rows[0]:
            store_shifted(xs1, row, tuple(inputs[tile, pl.ds(5 + row, 16, stride=32), :] for tile in range(2)))
        activate(weight1, xs1, act1, xs2, rows[1])
        activate(weight2, xs2, act2, xs3, rows[2])
        back_layer(flip3, gs3, act2, gs2, rows[2])
        sum3 = weight_sum(sums[2], gs3, xs3, rows[3])
        back_layer(flip2, gs2, act1, gs1, rows[4])
        sum2 = weight_sum(sums[1], gs2, xs2, rows[2])
        sum1 = weight_sum(sums[0], gs1, xs1, rows[4])
        return sum1, sum2, sum3

    split = (19, 17, 15, 13, 15)
    sums = closure([(0, at) for at in split], (jnp.zeros((16, 144), F32),) * 3)

    @pl.when(lat == top)
    def _():
        for mask in lon_masks:
            lon_copy(fold_trac, mask, fold_send.at[1], fold_recv.at[1], True).wait_recv()
        ghost = permute_columns(mirrored(fold_trac), select_in[...])
        for c in range(LEV):
            first, count = (TRIM * c, TRIM) if c < CL else (TRIM * CL + c - CL, 1)
            for tile in range(2):
                rows = ghost[first : first + count, LANES * tile : LANES * tile + LANES]
                trac[tile, c, 24 : 24 + count, :] = rows
                inputs[tile, 32 * c + 24 : 32 * c + 24 + count, :] = rows

    sum1, sum2, sum3 = closure(list(zip(split, (22, 20, 18, 16, 20))), sums)

    tail = jnp.concatenate([sum1[:, 128:144], sum2[:, 128:144], sum3[:, 128:144], jnp.zeros((16, 80), F32)], axis=1)
    tail = jnp.concatenate([tail[0:6, 0:48], tail[6:12, 0:48], tail[10:16, 0:32]], axis=1)
    rows = jnp.concatenate([sum1[:, :128], sum2[:, :128], sum3[0:CL, :128], tail], axis=0)
    halves[0] = rows[0:24]
    halves[1] = rows[24:48]

    def half_copy():
        return remote(halves.at[1 - core], half_in, pair_send.at[0], pair_recv.at[0], lat=lat + 1 - 2 * core)

    def plane_copy(mask, arrival=False):
        other, device = plane_peer(mask)
        slot = other if arrival else place
        return remote(plane_in.at[place], plane_in.at[slot], plane_send.at[mask], plane_recv.at[mask], **device)

    def column_copy(mask, arrival=False):
        peer = lon_peer(mask)
        slot = lax.rem(peer, nz) if arrival else z
        return remote(column_in.at[z], column_in.at[slot], column_send.at[mask], column_recv.at[mask], lon=peer)

    def total_copy(arrival=False):
        slot = 1 - core if arrival else core
        return remote(totals.at[core], totals.at[slot], pair_send.at[1], pair_recv.at[1], lat=lat + 1 - 2 * core)

    def sum_slots(ref, count):
        total = ref[0]
        for k in range(1, count):
            total = total + ref[k]
        return total

    half_copy().start()

    for row in range(22):
        grad = conv_row(flip1, gs1, row)
        for tile in range(2):
            back[tile, pl.ds(5 + row, 16, stride=32), :] = grad[tile]

    lane16 = lane_iota(16)
    zero8 = jnp.zeros((8, LANES), F32)
    sum_e = jnp.zeros((16, LANES), F32)
    sum_n = jnp.zeros((16, LANES), F32)
    for c in range(LEV):
        bar = bar_t[c]
        wb = wet_own * bar
        own, halo = trac[0, c, 8:24, :], trac[1, c, 8:24, :]
        ahead = jnp.where(lane16 == LANES - 1, pltpu.roll(halo, LANES - 1, 1), pltpu.roll(own, LANES - 1, 1))
        behind = jnp.where(lane16 == 0, pltpu.roll(halo, 1, 1), pltpu.roll(own, 1, 1))
        sum_e = sum_e + wb * (ahead - behind)
        sum_n = sum_n + wb * (trac[0, c, 9:25, :] - trac[0, c, 7:23, :])
        qe = (0.5 * advection) * new_e * wb
        qn = (0.5 * advection) * new_n * wb
        wd = diffusion * wb
        up = pltpu.roll(wd + qe, LANES - 1, 1)
        down = pltpu.roll(wd - qe, 1, 1)
        middle = (
            bar - 4.0 * wd + jnp.where(lane16 < LANES - 1, up, 0.0) + jnp.where(lane16 > 0, down, 0.0)
        )
        side = jnp.where(lane16 == LANES - 1, up, jnp.where(lane16 == 0, down, 0.0))
        above = pltpu.roll(jnp.concatenate([zero8, wd + qn, zero8], axis=0), 31, 0)
        below = pltpu.roll(jnp.concatenate([zero8, wd - qn, zero8], axis=0), 1, 0)
        main = jnp.concatenate([zero8, middle, zero8], axis=0) + above + below
        side = jnp.concatenate([zero8, side, zero8], axis=0)
        if c < CL:
            main = main + back[0, 32 * c : 32 * c + 32, :]
            side = side + back[1, 32 * c : 32 * c + 32, :]
        tg[0, c] = main
        tg[1, c] = side

    def lat_back(up):
        to = 1 if up else -1
        rows_s = slice(32, 48) if up else slice(0, 16)
        rows_t = slice(24, 32) if up else slice(0, 8)
        slot = 0 if up else 1
        return (
            remote(sg.at[0, :, rows_s, :], back_surf.at[slot], b_send.at[0, slot], b_recv.at[0, slot], lat=lat + to),
            remote(tg.at[0, :, rows_t, :], back_trac.at[slot], b_send.at[1, slot], b_recv.at[1, slot], lat=lat + to),
        )

    def pack_ghosts(grads, first, count, width, out, edge):
        for row, (f, m) in enumerate(ghost_rows(width, count)):
            out[lon, row : row + 1, :] = grads[0, f, first + m : first + m + 1, :]
            edge[row : row + 1, :] = grads[1, f, first + m : first + m + 1, :]
        out[lon, 32:40, :] = pack_edges([edge[8 * g : 8 * g + 8, :] for g in range(4)], width)

    half_copy().wait_recv()
    column_in[z] = halves[core] + half_in[...]
    for mask in column_masks:
        column_copy(mask).start()

    @pl.when(lat == top)
    def _():
        pack_ghosts(tg, 24, LEV, TRIM, unfold_trac, unfold_edge.at[0])

    pl.when(lat > 0)(lambda: lat_back(False)[1].start())
    pl.when(lat < top)(lambda: lat_back(True)[1].start())

    def own_rows(x):
        zero16 = jnp.zeros((16, LANES), F32)
        return (jnp.concatenate([zero16, x, zero16], axis=0), jnp.zeros((48, LANES), F32))

    e = own_rows(bar_f[0] - (0.5 * advection) * sum_e)
    n = own_rows(bar_f[1] - (0.5 * advection) * sum_n)
    rim = tuple(jnp.concatenate([zero8, back[tile, 32 * HCH : 32 * HCH + 32, :], zero8], axis=0) for tile in range(2))
    h = lift(lambda a, b: a + b)(rim, own_rows(bar_h[...]))
    wet = tuple(surf[tile, 3] for tile in range(2))
    for index in range(SUB):
        h, e, n = step_adjoint(h, e, n, wet)
    for f, pair in enumerate((h, e, n)):
        for tile in range(2):
            sg[tile, f] = pair[tile]

    for block in range(3):
        back_out[block, 0] = pack_edges([sg[1, f, 16 * block : 16 * block + 16, :] for f in range(3)], RIM)
        if block == 1:
            fields = [tg[1, c, 8:24, :] for c in range(LEV)]
        elif block == 0:
            fields = [jnp.concatenate([zero8, tg[1, c, 0:8, :]], axis=0) for c in range(LEV)]
        else:
            fields = [jnp.concatenate([tg[1, c, 24:32, :], zero8], axis=0) for c in range(LEV)]
        back_out[block, 1] = pack_edges(fields, TRIM)

    def edge_back(side, block):
        return remote(
            back_out.at[block],
            back_in.at[side, 2 - block],
            bm_send.at[side, 2 - block],
            bm_recv.at[side, 2 - block],
            lon=(right, left)[side],
            lat=lat + block - 1,
        )

    @pl.when(lat == top)
    def _():
        pack_ghosts(sg, 32, 3, RIM, unfold_surf, unfold_edge.at[1])
        for mask in lon_masks:
            lon_copy(unfold_surf, mask, unfold_send.at[0], unfold_recv.at[0]).start()
        for mask in lon_masks:
            lon_copy(unfold_trac, mask, unfold_send.at[1], unfold_recv.at[1]).start()

    def start_back(shift):
        if shift:
            lat_back(shift > 0)[0].start()
        for side in range(2):
            edge_back(side, shift + 1).start()

    for_lat(start_back)

    right_s = slot_mask(16, RIM, 3, RIM)
    right_t = slot_mask(16, TRIM, LEV, TRIM)

    def sent_forward(shift):
        if shift:
            for copy in lat_copies(shift > 0):
                copy.wait_send()
        for side in range(2):
            edge_copy(side, shift).wait_send()

    for_lat(sent_forward)

    @pl.when(lat == top)
    def _():
        for mask in lon_masks:
            for part, ref in enumerate((fold_surf, fold_trac)):
                lon_copy(ref, mask, fold_send.at[part], fold_recv.at[part]).wait_send()

    half_copy().wait_send()
    for mask in column_masks:
        column_copy(mask).wait_send()

    for mask in column_masks:
        column_copy(mask, True).wait_recv()
    plane_in[place] = sum_slots(column_in, nz)
    for mask in plane_masks:
        plane_copy(mask).start()

    def wait_back(shift):
        if shift:
            for copy in lat_back(shift < 0):
                copy.wait_recv()
        for side in range(2):
            edge_back(side, 1 - shift).wait_recv()

    for_lat(wait_back)

    from_left = back_in[0, 0] + back_in[0, 1] + back_in[0, 2]
    from_right = back_in[1, 0] + back_in[1, 1] + back_in[1, 2]
    packed = jnp.where(right_s, from_left[0], from_right[0])
    for f in range(3):
        total = sg[0, f, 16:32, :] + back_surf[0, f] + back_surf[1, f] + unpack_edge(packed, RIM, f)
        if f == 0:
            height_out[0] = total
        else:
            flow_out[0, f - 1] = total
    packed = jnp.where(right_t, from_left[1], from_right[1])
    for c in range(LEV):
        ghosts = jnp.concatenate([back_trac[0, c], back_trac[1, c]], axis=0)
        temp_out[0, c] = tg[0, c, 8:24, :] + ghosts + unpack_edge(packed, TRIM, c)

    def sent_back(shift):
        if shift:
            for copy in lat_back(shift > 0):
                copy.wait_send()
        for side in range(2):
            edge_back(side, shift + 1).wait_send()

    for_lat(sent_back)

    for mask in plane_masks:
        plane_copy(mask, True).wait_recv()
    totals[core] = sum_slots(plane_in, plane)
    total_copy().start()

    @pl.when(lat == top)
    def _():
        def unfold(ref, width):
            tiles = [ref[lax.rem(tile0 + j, nlon)] for j in range(3)]
            edges = [
                jnp.concatenate([unpack_edge(tile[32:40], width, g) for g in range(4)], axis=0) for tile in tiles
            ]
            return permute_columns(jnp.concatenate([tile[0:32] for tile in tiles] + edges, axis=1), select_out[...])

        for mask in lon_masks:
            lon_copy(unfold_trac, mask, unfold_send.at[1], unfold_recv.at[1], True).wait_recv()
        ghost = unfold(unfold_trac, TRIM)
        for row, (c, m) in enumerate(ghost_rows(TRIM, LEV)):
            temp_out[0, c, 15 - m : 16 - m, :] = temp_out[0, c, 15 - m : 16 - m, :] + ghost[row : row + 1]
        for mask in lon_masks:
            lon_copy(unfold_surf, mask, unfold_send.at[0], unfold_recv.at[0], True).wait_recv()
        ghost = unfold(unfold_surf, RIM)
        for row, (f, m) in enumerate(ghost_rows(RIM, 3)):
            if f == 0:
                height_out[0, 15 - m : 16 - m, :] = height_out[0, 15 - m : 16 - m, :] + ghost[row : row + 1]
            else:
                flow_out[0, f - 1, 15 - m : 16 - m, :] = flow_out[0, f - 1, 15 - m : 16 - m, :] - ghost[row : row + 1]

    total_copy(True).wait_recv()
    scale = 1.0 / math.sqrt(nens * nlat * 16 * nlon * LANES)
    rows = jnp.concatenate([totals[0], totals[1]], axis=0) * scale
    tail = rows[32 + CL : 48]
    tail = jnp.concatenate(
        [tail[:, 0:48], tail[:, 48:96], jnp.concatenate([tail[2:6, 96:128], jnp.zeros((4, 16), F32)], axis=1)], axis=0
    )
    for layer, out in ((1, second_out), (2, third_out)):
        count = out.shape[0]
        out[:, 0:128] = rows[16 * layer : 16 * layer + count]
        out[:, 128:144] = tail[0:count, 16 * layer : 16 * layer + 16]
    for tap in range(9):
        block = tail[:, 0:16] if tap == 8 else rows[0:16, 16 * tap : 16 * tap + 16]
        first_out[:, 11 * tap : 11 * tap + CL] = block[:, 0:CL]
        first_out[:, 11 * tap + CL : 11 * tap + CL + 1] = block[:, HCH : HCH + 1]

    for mask in plane_masks:
        plane_copy(mask).wait_send()
    total_copy().wait_send()

    @pl.when(lat == top)
    def _():
        for mask in lon_masks:
            for part, ref in enumerate((unfold_surf, unfold_trac)):
                lon_copy(ref, mask, unfold_send.at[part], unfold_recv.at[part]).wait_send()


def hand_over(*refs):
    sources, targets, sem = refs[:6], refs[6:12], refs[12]
    copies = [pltpu.make_async_copy(src, dst, sem.at[k]) for k, (src, dst) in enumerate(zip(sources, targets))]
    for copy in copies:
        copy.start()
    for copy in copies:
        copy.wait()


def solution(mesh):
    nlon, nlat, nens = (mesh.shape[axis] for axis in ("lon", "lat", "ens"))
    plane = nlat * nens

    def local(temp, height, flow, land_sea, fold, w_first, w_second, w_third, temp_bar, height_bar, flow_bar):
        vmem = pltpu.VMEM
        dma = pltpu.SemaphoreType.DMA
        scratch = [
            vmem((2, 4, 48, LANES), F32),
            vmem((2, LEV, 32, LANES), F32),
            vmem((2, 16 * 32, LANES), F32),
            vmem((16, LANES), jnp.int32),
            vmem((LEV, 16, LANES), F32),
            vmem((16, LANES), F32),
            vmem((2, 16, LANES), F32),
            pltpu.SMEM(fold.shape, jnp.int32),
            vmem(w_first.shape, BF16),
            vmem(w_second.shape, BF16),
            vmem(w_third.shape, BF16),
            vmem((3, 16, 256), F32),
            vmem((3, 16, 144), F32),
            vmem((2, 16, LANES), F32),
            vmem((2, 3, 2, 16, LANES), F32),
            vmem((nlon, 40, LANES), F32),
            vmem((nlon, 32, LANES), F32),
            vmem((3 * LANES, 2 * LANES), BF16),
            vmem((6 * LANES, LANES), BF16),
            vmem((16 * 16, LANES), F32),
            vmem((2, 22, 48, LANES), BF16),
            vmem((2, 20, 48, LANES), BF16),
            vmem((2, 18, 48, LANES), BF16),
            vmem((2, 24, 48, LANES), BF16),
            vmem((2, 22, 48, LANES), BF16),
            vmem((2, 20, 48, LANES), BF16),
            vmem((2, 20, 16, LANES), F32),
            vmem((2, 18, 16, LANES), F32),
            vmem((2, 16 * 32, LANES), F32),
            vmem((2, 3, 48, LANES), F32),
            vmem((2, LEV, 32, LANES), F32),
            vmem((3, 2, 16, LANES), F32),
            vmem((2, 3, 2, 16, LANES), F32),
            vmem((2, 3, 16, LANES), F32),
            vmem((2, LEV, 8, LANES), F32),
            vmem((nlon, 40, LANES), F32),
            vmem((nlon, 40, LANES), F32),
            vmem((2, 32, LANES), F32),
            vmem((2, 24, LANES), F32),
            vmem((24, LANES), F32),
            vmem((plane, 24, LANES), F32),
            vmem((nlon // 2, 24, LANES), F32),
            vmem((2, 24, LANES), F32),
            dma((11,)),
            dma((4,)),
            dma((4,)),
            dma((6,)),
            dma((6,)),
            dma((2, nlon)),
            dma((2, nlon)),
            dma((2, 2)),
            dma((2, 2)),
            dma((2, 4)),
            dma((2, 4)),
            dma((2, nlon)),
            dma((2, nlon)),
            dma((2,)),
            dma((2,)),
            dma((plane,)),
            dma((plane,)),
            dma((nlon // 2,)),
            dma((nlon // 2,)),
        ]
        out_shape = (
            jax.ShapeDtypeStruct(temp.shape, F32),
            jax.ShapeDtypeStruct(height.shape, F32),
            jax.ShapeDtypeStruct(flow.shape, F32),
            jax.ShapeDtypeStruct(w_first.shape, F32),
            jax.ShapeDtypeStruct(w_second.shape, F32),
            jax.ShapeDtypeStruct(w_third.shape, F32),
        )
        results = pl.pallas_call(
            functools.partial(kernel, (nlon, nlat, nens)),
            out_shape=tuple(pltpu.VMEM(o.shape, F32) for o in out_shape),
            in_specs=[pl.BlockSpec(memory_space=pltpu.HBM)] * 11,
            out_specs=[pl.BlockSpec(memory_space=pltpu.VMEM)] * 6,
            scratch_shapes=scratch,
            compiler_params=pltpu.CompilerParams(
                collective_id=0, has_side_effects=True, vmem_limit_bytes=60 * 1024 * 1024
            ),
        )(temp, height, flow, land_sea, fold, w_first, w_second, w_third, temp_bar, height_bar, flow_bar)
        return pl.pallas_call(
            hand_over,
            out_shape=out_shape,
            in_specs=[pl.BlockSpec(memory_space=pl.ANY)] * 6,
            out_specs=[pl.BlockSpec(memory_space=pltpu.HBM)] * 6,
            scratch_shapes=[dma((6,))],
            compiler_params=pltpu.CompilerParams(vmem_limit_bytes=1024 * 1024),
        )(*results)

    field = P("ens", None, "lat", "lon")
    surface = P("ens", "lat", "lon")
    return jax.shard_map(
        local,
        mesh=mesh,
        in_specs=(field, surface, field, P("lat", "lon"), P(), P(), P(), P(), field, surface, field),
        out_specs=(field, surface, field, P(), P(), P()),
        check_vma=False,
    )
```

```python
import functools
import math

import jax
import jax.numpy as jnp
from jax import lax
from jax.experimental import pallas as pl
from jax.experimental.pallas import tpu as pltpu
from jax.sharding import PartitionSpec as P

MESH = pl.DeviceIdType.MESH
F32 = jnp.float32
BF16 = jnp.bfloat16

SUB = 4
LEV = 12
CL = 10
RIM = 10
TRIM = 3
HCH = 12
LANES = 128

gravity = 0.3
drag_rate = 0.05
coriolis = 0.2
diffusion = 0.1
advection = 0.1
closure_gain = 0.5


def lane_iota(rows):
    return lax.broadcasted_iota(jnp.int32, (rows, LANES), 1)


def east_of(x):
    a, b = (pltpu.roll(v, LANES - 1, 1) for v in x)
    edge = lane_iota(a.shape[0]) == LANES - 1
    return (jnp.where(edge, b, a), jnp.where(edge, a, b))


def west_of(x):
    a, b = (pltpu.roll(v, 1, 1) for v in x)
    edge = lane_iota(a.shape[0]) == 0
    return (jnp.where(edge, b, a), jnp.where(edge, a, b))


def north_of(x):
    return tuple(pltpu.roll(v, v.shape[0] - 1, 0) for v in x)


def south_of(x):
    return tuple(pltpu.roll(v, 1, 0) for v in x)


def lift(fn):
    return lambda *pairs: tuple(fn(*vs) for vs in zip(*pairs))


sub2 = lift(lambda u, v: u - v)


def step_forward(h, e, n, w):
    de = sub2(east_of(e), west_of(e))
    dn = sub2(north_of(n), south_of(n))
    h = lift(lambda w_, h_, a, b: w_ * (h_ - (0.5 * gravity) * (a + b)))(w, h, de, dn)
    se = sub2(east_of(h), west_of(h))
    sn = sub2(north_of(h), south_of(h))
    keep = 1.0 - drag_rate
    e_new = lift(lambda w_, e_, n_, s: w_ * (keep * e_ - (0.5 * gravity) * s + coriolis * n_))(w, e, n, se)
    n_new = lift(lambda w_, e_, n_, s: w_ * (keep * n_ - (0.5 * gravity) * s - coriolis * e_))(w, e, n, sn)
    return h, e_new, n_new


def step_adjoint(h, e, n, w):
    we = lift(lambda a, b: a * b)(w, e)
    wn = lift(lambda a, b: a * b)(w, n)
    de = sub2(east_of(we), west_of(we))
    dn = sub2(north_of(wn), south_of(wn))
    hw = lift(lambda w_, h_, a, b: w_ * (h_ + (0.5 * gravity) * (a + b)))(w, h, de, dn)
    se = sub2(east_of(hw), west_of(hw))
    sn = sub2(north_of(hw), south_of(hw))
    keep = 1.0 - drag_rate
    e_new = lift(lambda a, b, s: keep * a - coriolis * b + (0.5 * gravity) * s)(we, wn, se)
    n_new = lift(lambda a, b, s: keep * b + coriolis * a + (0.5 * gravity) * s)(we, wn, sn)
    return hw, e_new, n_new


def slot_mask(rows, width, count, offset):
    lane = lane_iota(rows)
    mask = None
    for slot in range(count):
        start = 2 * width * slot + offset
        here = (lane >= start) & (lane < start + width)
        mask = here if mask is None else mask | here
    return mask


def pack_edges(fields, width):
    lane = lane_iota(fields[0].shape[0])
    out = jnp.zeros_like(fields[0])
    for slot, field in enumerate(fields):
        start = 2 * width * slot
        rolled = pltpu.roll(field, (start + width) % LANES, 1)
        out = jnp.where((lane >= start) & (lane < start + 2 * width), rolled, out)
    return out


def unpack_edge(packed, width, slot):
    lane = lane_iota(packed.shape[0])
    rolled = pltpu.roll(packed, (-width - 2 * width * slot) % LANES, 1)
    return jnp.where((lane < width) | (lane >= LANES - width), rolled, 0.0)


def split_bf16(x):
    high = x.astype(BF16)
    rest = x - high.astype(F32)
    middle = rest.astype(BF16)
    low = (rest - middle.astype(F32)).astype(BF16)
    return jnp.concatenate([high, middle, low], axis=0)


def permute_columns(x, select):
    rows = x.shape[0]
    y = jnp.dot(split_bf16(x), select, preferred_element_type=F32)
    return (y[2 * rows :] + y[rows : 2 * rows]) + y[:rows]


def store_shifted(ref, row, pair):
    for dx, shifted in enumerate((west_of(pair), pair, east_of(pair))):
        for tile in range(2):
            ref[tile, row, 16 * dx : 16 * dx + 16, :] = shifted[tile].astype(BF16)


def patch(ref, row):
    return jnp.concatenate([ref[tile, row : row + 3].reshape(144, LANES) for tile in range(2)], axis=1)


def conv_row(weight, ref, row):
    y = jnp.dot(weight, patch(ref, row), preferred_element_type=F32)
    return (y[:, :LANES], y[:, LANES:])


def contract(left, right):
    return lax.dot_general(left, right, (((1,), (1,)), ((), ())), preferred_element_type=F32)


def kernel(
    sizes,
    temp,
    height,
    flow,
    land_sea,
    fold,
    w_first,
    w_second,
    w_third,
    temp_bar,
    height_bar,
    flow_bar,
    temp_out,
    height_out,
    flow_out,
    first_out,
    second_out,
    third_out,
    surf,
    trac,
    inputs,
    wet_i,
    bar_t,
    bar_h,
    bar_f,
    fold_s,
    w1_raw,
    w2_raw,
    w3_raw,
    w_rows,
    w_flip,
    msg_out,
    msg_in,
    fold_surf,
    fold_trac,
    select_in,
    select_out,
    g3_rows,
    xs1,
    xs2,
    xs3,
    gs1,
    gs2,
    gs3,
    act1,
    act2,
    back,
    sg,
    tg,
    back_out,
    back_in,
    back_surf,
    back_trac,
    unfold_surf,
    unfold_trac,
    unfold_edge,
    halves,
    half_in,
    plane_in,
    column_in,
    totals,
    load_sem,
    f_send,
    f_recv,
    m_send,
    m_recv,
    fold_send,
    fold_recv,
    b_send,
    b_recv,
    bm_send,
    bm_recv,
    unfold_send,
    unfold_recv,
    pair_send,
    pair_recv,
    plane_send,
    plane_recv,
    column_send,
    column_recv,
):
    nlon, nlat, nens = sizes
    lon, lat, ens = lax.axis_index("lon"), lax.axis_index("lat"), lax.axis_index("ens")
    top = nlat - 1
    left, right = lax.rem(lon + nlon - 1, nlon), lax.rem(lon + 1, nlon)
    nz, ny = nlon // 2, nlat // 2
    core, z = lax.rem(lat, 2), lax.rem(lon, nz)
    plane = 2 * ny * nens
    place = (ens * 2 + lon // nz) * ny + lat // 2

    def remote(src, dst, send, recv, **device):
        return pltpu.make_async_remote_copy(
            src_ref=src, dst_ref=dst, send_sem=send, recv_sem=recv, device_id=device, device_id_type=MESH
        )

    barrier = pltpu.get_barrier_semaphore()

    def greet(**device):
        pl.semaphore_signal(barrier, inc=1, device_id=device, device_id_type=MESH)

    def bits(value, size):
        return [lax.rem(value // 2**k, 2) for k in range(size.bit_length() - 1)]

    def flip(value, digits, mask):
        return value + sum((1 - 2 * digit) * 2**k for k, digit in enumerate(digits) if mask >> k & 1)

    def reach(mask):
        return (0, 1, 2, 3, 4, 3, 2, 3)[mask] if mask < 8 else 1 + reach(mask - 8)

    def plane_reach(mask):
        return sum((0, 1, 2, 1)[part] for part in (mask // ny, mask % ny))

    x, y = ens * 2 + lon // nz, lat // 2
    x_bits, y_bits, lon_bits = bits(x, 2 * nens), bits(y, ny), bits(lon, nlon)
    plane_masks = sorted(range(1, plane), key=plane_reach, reverse=True)
    column_masks = sorted(range(1, nz), key=reach, reverse=True)
    lon_masks = sorted(range(1, nlon), key=reach, reverse=True)

    def plane_peer(mask):
        px, py = flip(x, x_bits, mask // ny), flip(y, y_bits, mask % ny)
        device = dict(lon=lax.rem(px, 2) * nz + z, lat=py * 2 + core, ens=px // 2)
        return px * ny + py, device

    def lon_peer(mask):
        return flip(lon, lon_bits, mask)


    @pl.when(lat == top)
    def _():
        for mask in lon_masks:
            greet(lon=lon_peer(mask))

    for mask in plane_masks:
        greet(**plane_peer(mask)[1])
    for mask in column_masks:
        greet(lon=lon_peer(mask))
    greet(lon=left)
    greet(lon=right)

    @pl.when(lat > 0)
    def _():
        greet(lat=lat - 1)
        greet(lon=left, lat=lat - 1)
        greet(lon=right, lat=lat - 1)

    @pl.when(lat < top)
    def _():
        greet(lat=lat + 1)
        greet(lon=left, lat=lat + 1)
        greet(lon=right, lat=lat + 1)

    loads = [
        (temp.at[0], trac.at[0, :, 8:24, :]),
        (height.at[0], surf.at[0, 0, 16:32, :]),
        (flow.at[0], surf.at[0, 1:3, 16:32, :]),
        (land_sea, wet_i),
        (fold, fold_s),
        (w_first, w1_raw),
        (w_second, w2_raw),
        (w_third, w3_raw),
        (temp_bar.at[0], bar_t),
        (height_bar.at[0], bar_h),
        (flow_bar.at[0], bar_f),
    ]
    loads = [pltpu.make_async_copy(src, dst, load_sem.at[k]) for k, (src, dst) in enumerate(loads)]
    for load in loads:
        load.start()

    inputs[:, 32 * (HCH + 1) :, :] = jnp.zeros((2, 32 * (15 - HCH), LANES), F32)
    for ref, rows in ((gs3, 20), (gs2, 22), (gs1, 24)):
        for tile in range(2):
            for row in (0, 1, rows - 2, rows - 1):
                ref[tile, row] = jnp.zeros((48, LANES), BF16)
    back[...] = jnp.zeros_like(back)
    for ref in (unfold_surf, unfold_trac):
        ref[lon, 24:32, :] = jnp.zeros((8, LANES), F32)
    unfold_edge[:, 24:32, :] = jnp.zeros((2, 8, LANES), F32)

    @pl.when(lat == 0)
    def _():
        surf[:, :, 0:16, :] = jnp.zeros((2, 4, 16, LANES), F32)
        trac[:, :, 0:8, :] = jnp.zeros((2, LEV, 8, LANES), F32)
        back_in[:, 0] = jnp.zeros((2, 2, 16, LANES), F32)
        back_surf[0] = jnp.zeros((3, 16, LANES), F32)
        back_trac[0] = jnp.zeros((LEV, 8, LANES), F32)

    @pl.when(lat == top)
    def _():
        surf[:, :, 32:48, :] = jnp.zeros((2, 4, 16, LANES), F32)
        trac[:, :, 24:32, :] = jnp.zeros((2, LEV, 8, LANES), F32)
        back_in[:, 2] = jnp.zeros((2, 2, 16, LANES), F32)
        back_surf[1] = jnp.zeros((3, 16, LANES), F32)
        back_trac[1] = jnp.zeros((LEV, 8, LANES), F32)

    for k in (1, 2, 3, 0):
        loads[k].wait()
    surf[0, 3, 16:32, :] = wet_i[...].astype(F32)
    msg_out[0] = pack_edges([surf[0, f, 16:32, :] for f in range(4)], RIM)
    msg_out[1] = pack_edges([trac[0, c, 8:24, :] for c in range(LEV)], TRIM)

    def lat_copies(up):
        to = 1 if up else -1
        rows_s = slice(0, 16) if up else slice(32, 48)
        rows_t = (slice(16, 24), slice(0, 8)) if up else (slice(8, 16), slice(24, 32))
        slot = 0 if up else 2
        return (
            remote(surf.at[0, :, 16:32, :], surf.at[0, :, rows_s, :], f_send.at[slot], f_recv.at[slot], lat=lat + to),
            remote(
                trac.at[0, :, rows_t[0], :],
                trac.at[0, :, rows_t[1], :],
                f_send.at[slot + 1],
                f_recv.at[slot + 1],
                lat=lat + to,
            ),
        )

    def edge_copy(side, shift):
        slot = 3 * side + 1 - shift
        return remote(
            msg_out, msg_in.at[side, 1 - shift], m_send.at[slot], m_recv.at[slot], lon=(right, left)[side], lat=lat + shift
        )

    def lon_copy(ref, mask, send, recv, arrival=False):
        peer = lon_peer(mask)
        return remote(ref.at[lon], ref.at[peer if arrival else lon], send.at[mask], recv.at[mask], lon=peer)

    def ghost_rows(width, count):
        full = [(f, m) for f in range(min(count, CL)) for m in range(width)]
        return full + [(f, 0) for f in range(CL, count)]

    @pl.when(lat == top)
    def _():
        for row, (f, m) in enumerate(ghost_rows(RIM, 4)):
            fold_surf[lon, row : row + 1, :] = surf[0, f, 31 - m : 32 - m, :]
        for row, (c, m) in enumerate(ghost_rows(TRIM, LEV)):
            fold_trac[lon, row : row + 1, :] = trac[0, c, 23 - m : 24 - m, :]

    pl.semaphore_wait(
        barrier,
        (plane - 1)
        + (nz - 1)
        + 2
        + 3 * (lat > 0).astype(jnp.int32)
        + 3 * (lat < top).astype(jnp.int32)
        + (nlon - 1) * (lat == top).astype(jnp.int32),
    )

    def for_lat(fn):
        pl.when(lat > 0)(functools.partial(fn, -1))
        fn(0)
        pl.when(lat < top)(functools.partial(fn, 1))

    def start_forward(shift):
        if shift:
            for copy in lat_copies(shift > 0):
                copy.start()
        for side in range(2):
            edge_copy(side, shift).start()

    for_lat(start_forward)

    @pl.when(lat == top)
    def _():
        for mask in lon_masks:
            lon_copy(fold_surf, mask, fold_send.at[0], fold_recv.at[0]).start()

    @pl.when(lat == top)
    def _():
        for mask in lon_masks:
            lon_copy(fold_trac, mask, fold_send.at[1], fold_recv.at[1]).start()

    for k in range(4, 11):
        loads[k].wait()
    raw1 = w1_raw[...].astype(F32)
    w_rows[...] = jnp.zeros_like(w_rows)
    for tap in range(9):
        w_rows[0, :, 16 * tap : 16 * tap + CL] = raw1[:, 11 * tap : 11 * tap + CL]
        w_rows[0, :, 16 * tap + HCH : 16 * tap + HCH + 1] = raw1[:, 11 * tap + CL : 11 * tap + CL + 1]
    w_rows[1, :, 0:144] = w2_raw[...].astype(F32)
    w_rows[2, 0:CL, 0:144] = w3_raw[...].astype(F32)
    for layer in range(3):
        first = jnp.transpose(w_rows[layer, :, 0:128])
        second = jnp.transpose(w_rows[layer, :, 128:256])
        for tap in range(9):
            block = second[0:16, :] if tap == 8 else first[16 * tap : 16 * tap + 16, :]
            w_flip[layer, :, 16 * (8 - tap) : 16 * (8 - tap) + 16] = block
    weight1 = w_rows[0, :, 0:144].astype(BF16)
    weight2 = w_rows[1, :, 0:144].astype(BF16)
    flip1, flip2, flip3 = (w_flip[layer].astype(BF16) for layer in range(3))

    wet_own = surf[0, 3, 16:32, :]
    g3_rows[16 * CL :, :] = jnp.zeros((16 * (16 - CL), LANES), F32)
    for c in range(CL):
        g3_rows[16 * c : 16 * c + 16, :] = closure_gain * wet_own * bar_t[c]
    for row in range(16):
        own = g3_rows[pl.ds(row, 16, stride=16), :]
        store_shifted(gs3, row + 2, (own, jnp.zeros_like(own)))

    shift_s = fold_s[0] + 1
    base = shift_s - (LANES + RIM) - LANES * lon + LANES * (2 * nlon)
    tile0 = base // LANES
    offset = shift_s - 1 - LANES * lon + LANES * (2 * nlon) - LANES * tile0

    def mirrored(ref):
        return jnp.concatenate([ref[lax.rem(tile0 + j, nlon)] for j in range(3)], axis=1)

    @pl.when(lat == top)
    def _():
        source = lax.broadcasted_iota(jnp.int32, (3 * LANES, 2 * LANES), 0)
        column = lax.broadcasted_iota(jnp.int32, (3 * LANES, 2 * LANES), 1)
        column = jnp.where(column < LANES + LANES // 2, column, column - 2 * LANES)
        select_in[...] = jnp.where(source + column == offset, 1.0, 0.0).astype(BF16)
        lane = lax.broadcasted_iota(jnp.int32, (LANES, LANES), 0)
        column = lax.broadcasted_iota(jnp.int32, (LANES, LANES), 1)
        halo = jnp.where(lane < LANES // 2, lane + LANES, lane - LANES)
        for k, at in enumerate((lane, halo)):
            for j in range(3):
                first = LANES * (3 * k + j)
                select_out[first : first + LANES, :] = jnp.where(at + LANES * j + column == offset, 1.0, 0.0).astype(
                    BF16
                )

    left_s = slot_mask(16, RIM, 4, 0)
    left_t = slot_mask(16, TRIM, LEV, 0)

    def wait_forward(shift):
        k = shift + 1
        if shift:
            for copy in lat_copies(shift < 0):
                copy.wait_recv()
        for side in range(2):
            edge_copy(side, -shift).wait_recv()
        packed = jnp.where(left_s, msg_in[0, k, 0], msg_in[1, k, 0])
        for f in range(4):
            surf[1, f, 16 * k : 16 * k + 16, :] = unpack_edge(packed, RIM, f)
        packed = jnp.where(left_t, msg_in[0, k, 1], msg_in[1, k, 1])
        rows, at = ((slice(8, 16), 0), (slice(0, 16), 8), (slice(0, 8), 24))[k]
        packed = packed[rows]
        for c in range(LEV):
            trac[1, c, at : at + packed.shape[0], :] = unpack_edge(packed, TRIM, c)

    for_lat(wait_forward)

    @pl.when(lat == top)
    def _():
        for mask in lon_masks:
            lon_copy(fold_surf, mask, fold_send.at[0], fold_recv.at[0], True).wait_recv()
        window = jnp.concatenate([mirrored(fold_surf), jnp.zeros((8, 3 * LANES), F32)], axis=0)
        ghost = permute_columns(window, select_in[...])
        for f in range(4):
            rows = ghost[RIM * f : RIM * f + RIM]
            rows = -rows if f in (1, 2) else rows
            for tile in range(2):
                surf[tile, f, 32 : 32 + RIM, :] = rows[:, LANES * tile : LANES * tile + LANES]

    h, e, n, wet = (tuple(surf[tile, f] for tile in range(2)) for f in range(4))
    for _ in range(SUB):
        h, e, n = step_forward(h, e, n, wet)
    new_e, new_n = e[0][16:32], n[0][16:32]

    for tile in range(2):
        for c in range(LEV):
            inputs[tile, 32 * c : 32 * c + 32, :] = trac[tile, c]
        inputs[tile, 32 * HCH : 32 * HCH + 32, :] = h[tile][8:40]

    def activate(weight, xs, act_ref, out, rows):
        for row in rows:
            act = lift(jnp.tanh)(conv_row(weight, xs, row))
            for tile in range(2):
                act_ref[tile, row] = act[tile]
            store_shifted(out, row, act)

    def weight_sum(total, gs, xs, rows):
        for row in rows:
            grad = jnp.concatenate([gs[tile, row + 2, 16:32, :] for tile in range(2)], axis=1)
            total = total + contract(grad, patch(xs, row))
        return total

    def back_layer(weight, gs, act_ref, out, rows):
        for row in rows:
            grad = conv_row(weight, gs, row)
            act = tuple(act_ref[tile, row] for tile in range(2))
            store_shifted(out, row + 2, lift(lambda g, a: g * (1.0 - a * a))(grad, act))

    def closure(ends, sums):
        rows = [range(*pair) for pair in ends]
        for row in rows[0]:
            store_shifted(xs1, row, tuple(inputs[tile, pl.ds(5 + row, 16, stride=32), :] for tile in range(2)))
        activate(weight1, xs1, act1, xs2, rows[1])
        activate(weight2, xs2, act2, xs3, rows[2])
        back_layer(flip3, gs3, act2, gs2, rows[2])
        sum3 = weight_sum(sums[2], gs3, xs3, rows[3])
        back_layer(flip2, gs2, act1, gs1, rows[4])
        sum2 = weight_sum(sums[1], gs2, xs2, rows[2])
        sum1 = weight_sum(sums[0], gs1, xs1, rows[4])
        return sum1, sum2, sum3

    split = (19, 17, 15, 13, 15)
    sums = closure([(0, at) for at in split], (jnp.zeros((16, 144), F32),) * 3)

    @pl.when(lat == top)
    def _():
        for mask in lon_masks:
            lon_copy(fold_trac, mask, fold_send.at[1], fold_recv.at[1], True).wait_recv()
        ghost = permute_columns(mirrored(fold_trac), select_in[...])
        for c in range(LEV):
            first, count = (TRIM * c, TRIM) if c < CL else (TRIM * CL + c - CL, 1)
            for tile in range(2):
                rows = ghost[first : first + count, LANES * tile : LANES * tile + LANES]
                trac[tile, c, 24 : 24 + count, :] = rows
                inputs[tile, 32 * c + 24 : 32 * c + 24 + count, :] = rows

    sum1, sum2, sum3 = closure(list(zip(split, (22, 20, 18, 16, 20))), sums)

    tail = jnp.concatenate([sum1[:, 128:144], sum2[:, 128:144], sum3[:, 128:144], jnp.zeros((16, 80), F32)], axis=1)
    tail = jnp.concatenate([tail[0:6, 0:48], tail[6:12, 0:48], tail[10:16, 0:32]], axis=1)
    rows = jnp.concatenate([sum1[:, :128], sum2[:, :128], sum3[0:CL, :128], tail], axis=0)
    halves[0] = rows[0:24]
    halves[1] = rows[24:48]

    def half_copy():
        return remote(halves.at[1 - core], half_in, pair_send.at[0], pair_recv.at[0], lat=lat + 1 - 2 * core)

    def plane_copy(mask, arrival=False):
        other, device = plane_peer(mask)
        slot = other if arrival else place
        return remote(plane_in.at[place], plane_in.at[slot], plane_send.at[mask], plane_recv.at[mask], **device)

    def column_copy(mask, arrival=False):
        peer = lon_peer(mask)
        slot = lax.rem(peer, nz) if arrival else z
        return remote(column_in.at[z], column_in.at[slot], column_send.at[mask], column_recv.at[mask], lon=peer)

    def total_copy(arrival=False):
        slot = 1 - core if arrival else core
        return remote(totals.at[core], totals.at[slot], pair_send.at[1], pair_recv.at[1], lat=lat + 1 - 2 * core)

    def sum_slots(ref, count):
        total = ref[0]
        for k in range(1, count):
            total = total + ref[k]
        return total

    half_copy().start()

    for row in range(22):
        grad = conv_row(flip1, gs1, row)
        for tile in range(2):
            back[tile, pl.ds(5 + row, 16, stride=32), :] = grad[tile]

    lane16 = lane_iota(16)
    zero8 = jnp.zeros((8, LANES), F32)
    sum_e = jnp.zeros((16, LANES), F32)
    sum_n = jnp.zeros((16, LANES), F32)
    for c in range(LEV):
        bar = bar_t[c]
        wb = wet_own * bar
        own, halo = trac[0, c, 8:24, :], trac[1, c, 8:24, :]
        ahead = jnp.where(lane16 == LANES - 1, pltpu.roll(halo, LANES - 1, 1), pltpu.roll(own, LANES - 1, 1))
        behind = jnp.where(lane16 == 0, pltpu.roll(halo, 1, 1), pltpu.roll(own, 1, 1))
        sum_e = sum_e + wb * (ahead - behind)
        sum_n = sum_n + wb * (trac[0, c, 9:25, :] - trac[0, c, 7:23, :])
        qe = (0.5 * advection) * new_e * wb
        qn = (0.5 * advection) * new_n * wb
        wd = diffusion * wb
        up = pltpu.roll(wd + qe, LANES - 1, 1)
        down = pltpu.roll(wd - qe, 1, 1)
        middle = (
            bar - 4.0 * wd + jnp.where(lane16 < LANES - 1, up, 0.0) + jnp.where(lane16 > 0, down, 0.0)
        )
        side = jnp.where(lane16 == LANES - 1, up, jnp.where(lane16 == 0, down, 0.0))
        above = pltpu.roll(jnp.concatenate([zero8, wd + qn, zero8], axis=0), 31, 0)
        below = pltpu.roll(jnp.concatenate([zero8, wd - qn, zero8], axis=0), 1, 0)
        main = jnp.concatenate([zero8, middle, zero8], axis=0) + above + below
        side = jnp.concatenate([zero8, side, zero8], axis=0)
        if c < CL:
            main = main + back[0, 32 * c : 32 * c + 32, :]
            side = side + back[1, 32 * c : 32 * c + 32, :]
        tg[0, c] = main
        tg[1, c] = side

    def lat_back(up):
        to = 1 if up else -1
        rows_s = slice(32, 48) if up else slice(0, 16)
        rows_t = slice(24, 32) if up else slice(0, 8)
        slot = 0 if up else 1
        return (
            remote(sg.at[0, :, rows_s, :], back_surf.at[slot], b_send.at[0, slot], b_recv.at[0, slot], lat=lat + to),
            remote(tg.at[0, :, rows_t, :], back_trac.at[slot], b_send.at[1, slot], b_recv.at[1, slot], lat=lat + to),
        )

    def pack_ghosts(grads, first, count, width, out, edge):
        for row, (f, m) in enumerate(ghost_rows(width, count)):
            out[lon, row : row + 1, :] = grads[0, f, first + m : first + m + 1, :]
            edge[row : row + 1, :] = grads[1, f, first + m : first + m + 1, :]
        out[lon, 32:40, :] = pack_edges([edge[8 * g : 8 * g + 8, :] for g in range(4)], width)

    half_copy().wait_recv()
    column_in[z] = halves[core] + half_in[...]
    for mask in column_masks:
        column_copy(mask).start()

    @pl.when(lat == top)
    def _():
        pack_ghosts(tg, 24, LEV, TRIM, unfold_trac, unfold_edge.at[0])

    pl.when(lat > 0)(lambda: lat_back(False)[1].start())
    pl.when(lat < top)(lambda: lat_back(True)[1].start())

    def own_rows(x):
        zero16 = jnp.zeros((16, LANES), F32)
        return (jnp.concatenate([zero16, x, zero16], axis=0), jnp.zeros((48, LANES), F32))

    e = own_rows(bar_f[0] - (0.5 * advection) * sum_e)
    n = own_rows(bar_f[1] - (0.5 * advection) * sum_n)
    rim = tuple(jnp.concatenate([zero8, back[tile, 32 * HCH : 32 * HCH + 32, :], zero8], axis=0) for tile in range(2))
    h = lift(lambda a, b: a + b)(rim, own_rows(bar_h[...]))
    wet = tuple(surf[tile, 3] for tile in range(2))
    for index in range(SUB):
        h, e, n = step_adjoint(h, e, n, wet)
    for f, pair in enumerate((h, e, n)):
        for tile in range(2):
            sg[tile, f] = pair[tile]

    for block in range(3):
        back_out[block, 0] = pack_edges([sg[1, f, 16 * block : 16 * block + 16, :] for f in range(3)], RIM)
        if block == 1:
            fields = [tg[1, c, 8:24, :] for c in range(LEV)]
        elif block == 0:
            fields = [jnp.concatenate([zero8, tg[1, c, 0:8, :]], axis=0) for c in range(LEV)]
        else:
            fields = [jnp.concatenate([tg[1, c, 24:32, :], zero8], axis=0) for c in range(LEV)]
        back_out[block, 1] = pack_edges(fields, TRIM)

    def edge_back(side, block):
        return remote(
            back_out.at[block],
            back_in.at[side, 2 - block],
            bm_send.at[side, 2 - block],
            bm_recv.at[side, 2 - block],
            lon=(right, left)[side],
            lat=lat + block - 1,
        )

    @pl.when(lat == top)
    def _():
        pack_ghosts(sg, 32, 3, RIM, unfold_surf, unfold_edge.at[1])
        for mask in lon_masks:
            lon_copy(unfold_surf, mask, unfold_send.at[0], unfold_recv.at[0]).start()
        for mask in lon_masks:
            lon_copy(unfold_trac, mask, unfold_send.at[1], unfold_recv.at[1]).start()

    def start_back(shift):
        if shift:
            lat_back(shift > 0)[0].start()
        for side in range(2):
            edge_back(side, shift + 1).start()

    for_lat(start_back)

    right_s = slot_mask(16, RIM, 3, RIM)
    right_t = slot_mask(16, TRIM, LEV, TRIM)

    def sent_forward(shift):
        if shift:
            for copy in lat_copies(shift > 0):
                copy.wait_send()
        for side in range(2):
            edge_copy(side, shift).wait_send()

    for_lat(sent_forward)

    @pl.when(lat == top)
    def _():
        for mask in lon_masks:
            for part, ref in enumerate((fold_surf, fold_trac)):
                lon_copy(ref, mask, fold_send.at[part], fold_recv.at[part]).wait_send()

    half_copy().wait_send()
    for mask in column_masks:
        column_copy(mask).wait_send()

    for mask in column_masks:
        column_copy(mask, True).wait_recv()
    plane_in[place] = sum_slots(column_in, nz)
    for mask in plane_masks:
        plane_copy(mask).start()

    def wait_back(shift):
        if shift:
            for copy in lat_back(shift < 0):
                copy.wait_recv()
        for side in range(2):
            edge_back(side, 1 - shift).wait_recv()

    for_lat(wait_back)

    from_left = back_in[0, 0] + back_in[0, 1] + back_in[0, 2]
    from_right = back_in[1, 0] + back_in[1, 1] + back_in[1, 2]
    packed = jnp.where(right_s, from_left[0], from_right[0])
    for f in range(3):
        total = sg[0, f, 16:32, :] + back_surf[0, f] + back_surf[1, f] + unpack_edge(packed, RIM, f)
        if f == 0:
            height_out[0] = total
        else:
            flow_out[0, f - 1] = total
    packed = jnp.where(right_t, from_left[1], from_right[1])
    for c in range(LEV):
        ghosts = jnp.concatenate([back_trac[0, c], back_trac[1, c]], axis=0)
        temp_out[0, c] = tg[0, c, 8:24, :] + ghosts + unpack_edge(packed, TRIM, c)

    def sent_back(shift):
        if shift:
            for copy in lat_back(shift > 0):
                copy.wait_send()
        for side in range(2):
            edge_back(side, shift + 1).wait_send()

    for_lat(sent_back)

    @pl.when(lat == top)
    def _():
        for mask in lon_masks:
            for part, ref in enumerate((unfold_surf, unfold_trac)):
                lon_copy(ref, mask, unfold_send.at[part], unfold_recv.at[part]).wait_send()

    for mask in plane_masks:
        plane_copy(mask, True).wait_recv()
    totals[core] = sum_slots(plane_in, plane)
    total_copy().start()
    for mask in plane_masks:
        plane_copy(mask).wait_send()

    @pl.when(lat == top)
    def _():
        def unfold(ref, width):
            tiles = [ref[lax.rem(tile0 + j, nlon)] for j in range(3)]
            edges = [
                jnp.concatenate([unpack_edge(tile[32:40], width, g) for g in range(4)], axis=0) for tile in tiles
            ]
            return permute_columns(jnp.concatenate([tile[0:32] for tile in tiles] + edges, axis=1), select_out[...])

        for mask in lon_masks:
            lon_copy(unfold_trac, mask, unfold_send.at[1], unfold_recv.at[1], True).wait_recv()
        ghost = unfold(unfold_trac, TRIM)
        for row, (c, m) in enumerate(ghost_rows(TRIM, LEV)):
            temp_out[0, c, 15 - m : 16 - m, :] = temp_out[0, c, 15 - m : 16 - m, :] + ghost[row : row + 1]
        for mask in lon_masks:
            lon_copy(unfold_surf, mask, unfold_send.at[0], unfold_recv.at[0], True).wait_recv()
        ghost = unfold(unfold_surf, RIM)
        for row, (f, m) in enumerate(ghost_rows(RIM, 3)):
            if f == 0:
                height_out[0, 15 - m : 16 - m, :] = height_out[0, 15 - m : 16 - m, :] + ghost[row : row + 1]
            else:
                flow_out[0, f - 1, 15 - m : 16 - m, :] = flow_out[0, f - 1, 15 - m : 16 - m, :] - ghost[row : row + 1]

    total_copy(True).wait_recv()
    scale = 1.0 / math.sqrt(nens * nlat * 16 * nlon * LANES)
    rows = jnp.concatenate([totals[0], totals[1]], axis=0) * scale
    tail = rows[32 + CL : 48]
    tail = jnp.concatenate(
        [tail[:, 0:48], tail[:, 48:96], jnp.concatenate([tail[2:6, 96:128], jnp.zeros((4, 16), F32)], axis=1)], axis=0
    )
    for layer, out in ((1, second_out), (2, third_out)):
        count = out.shape[0]
        out[:, 0:128] = rows[16 * layer : 16 * layer + count]
        out[:, 128:144] = tail[0:count, 16 * layer : 16 * layer + 16]
    for tap in range(9):
        block = tail[:, 0:16] if tap == 8 else rows[0:16, 16 * tap : 16 * tap + 16]
        first_out[:, 11 * tap : 11 * tap + CL] = block[:, 0:CL]
        first_out[:, 11 * tap + CL : 11 * tap + CL + 1] = block[:, HCH : HCH + 1]

    total_copy().wait_send()


def hand_over(*refs):
    sources, targets, sem = refs[:6], refs[6:12], refs[12]
    copies = [pltpu.make_async_copy(src, dst, sem.at[k]) for k, (src, dst) in enumerate(zip(sources, targets))]
    for copy in copies:
        copy.start()
    for copy in copies:
        copy.wait()


def solution(mesh):
    nlon, nlat, nens = (mesh.shape[axis] for axis in ("lon", "lat", "ens"))
    plane = nlat * nens

    def local(temp, height, flow, land_sea, fold, w_first, w_second, w_third, temp_bar, height_bar, flow_bar):
        vmem = pltpu.VMEM
        dma = pltpu.SemaphoreType.DMA
        scratch = [
            vmem((2, 4, 48, LANES), F32),
            vmem((2, LEV, 32, LANES), F32),
            vmem((2, 16 * 32, LANES), F32),
            vmem((16, LANES), jnp.int32),
            vmem((LEV, 16, LANES), F32),
            vmem((16, LANES), F32),
            vmem((2, 16, LANES), F32),
            pltpu.SMEM(fold.shape, jnp.int32),
            vmem(w_first.shape, BF16),
            vmem(w_second.shape, BF16),
            vmem(w_third.shape, BF16),
            vmem((3, 16, 256), F32),
            vmem((3, 16, 144), F32),
            vmem((2, 16, LANES), F32),
            vmem((2, 3, 2, 16, LANES), F32),
            vmem((nlon, 40, LANES), F32),
            vmem((nlon, 32, LANES), F32),
            vmem((3 * LANES, 2 * LANES), BF16),
            vmem((6 * LANES, LANES), BF16),
            vmem((16 * 16, LANES), F32),
            vmem((2, 22, 48, LANES), BF16),
            vmem((2, 20, 48, LANES), BF16),
            vmem((2, 18, 48, LANES), BF16),
            vmem((2, 24, 48, LANES), BF16),
            vmem((2, 22, 48, LANES), BF16),
            vmem((2, 20, 48, LANES), BF16),
            vmem((2, 20, 16, LANES), F32),
            vmem((2, 18, 16, LANES), F32),
            vmem((2, 16 * 32, LANES), F32),
            vmem((2, 3, 48, LANES), F32),
            vmem((2, LEV, 32, LANES), F32),
            vmem((3, 2, 16, LANES), F32),
            vmem((2, 3, 2, 16, LANES), F32),
            vmem((2, 3, 16, LANES), F32),
            vmem((2, LEV, 8, LANES), F32),
            vmem((nlon, 40, LANES), F32),
            vmem((nlon, 40, LANES), F32),
            vmem((2, 32, LANES), F32),
            vmem((2, 24, LANES), F32),
            vmem((24, LANES), F32),
            vmem((plane, 24, LANES), F32),
            vmem((nlon // 2, 24, LANES), F32),
            vmem((2, 24, LANES), F32),
            dma((11,)),
            dma((4,)),
            dma((4,)),
            dma((6,)),
            dma((6,)),
            dma((2, nlon)),
            dma((2, nlon)),
            dma((2, 2)),
            dma((2, 2)),
            dma((2, 4)),
            dma((2, 4)),
            dma((2, nlon)),
            dma((2, nlon)),
            dma((2,)),
            dma((2,)),
            dma((plane,)),
            dma((plane,)),
            dma((nlon // 2,)),
            dma((nlon // 2,)),
        ]
        out_shape = (
            jax.ShapeDtypeStruct(temp.shape, F32),
            jax.ShapeDtypeStruct(height.shape, F32),
            jax.ShapeDtypeStruct(flow.shape, F32),
            jax.ShapeDtypeStruct(w_first.shape, F32),
            jax.ShapeDtypeStruct(w_second.shape, F32),
            jax.ShapeDtypeStruct(w_third.shape, F32),
        )
        results = pl.pallas_call(
            functools.partial(kernel, (nlon, nlat, nens)),
            out_shape=tuple(pltpu.VMEM(o.shape, F32) for o in out_shape),
            in_specs=[pl.BlockSpec(memory_space=pltpu.HBM)] * 11,
            out_specs=[pl.BlockSpec(memory_space=pltpu.VMEM)] * 6,
            scratch_shapes=scratch,
            compiler_params=pltpu.CompilerParams(
                collective_id=0, has_side_effects=True, vmem_limit_bytes=60 * 1024 * 1024
            ),
        )(temp, height, flow, land_sea, fold, w_first, w_second, w_third, temp_bar, height_bar, flow_bar)
        return pl.pallas_call(
            hand_over,
            out_shape=out_shape,
            in_specs=[pl.BlockSpec(memory_space=pl.ANY)] * 6,
            out_specs=[pl.BlockSpec(memory_space=pltpu.HBM)] * 6,
            scratch_shapes=[dma((6,))],
            compiler_params=pltpu.CompilerParams(vmem_limit_bytes=1024 * 1024),
        )(*results)

    field = P("ens", None, "lat", "lon")
    surface = P("ens", "lat", "lon")
    return jax.shard_map(
        local,
        mesh=mesh,
        in_specs=(field, surface, field, P("lat", "lon"), P(), P(), P(), P(), field, surface, field),
        out_specs=(field, surface, field, P(), P(), P()),
        check_vma=False,
    )
```

```python
import functools
import math

import jax
import jax.numpy as jnp
from jax import lax
from jax.experimental import pallas as pl
from jax.experimental.pallas import tpu as pltpu
from jax.sharding import PartitionSpec as P

MESH = pl.DeviceIdType.MESH
F32 = jnp.float32
BF16 = jnp.bfloat16

SUB = 4
LEV = 12
CL = 10
RIM = 10
TRIM = 3
HCH = 12
LANES = 128

gravity = 0.3
drag_rate = 0.05
coriolis = 0.2
diffusion = 0.1
advection = 0.1
closure_gain = 0.5


def lane_iota(rows):
    return lax.broadcasted_iota(jnp.int32, (rows, LANES), 1)


def east_of(x):
    a, b = (pltpu.roll(v, LANES - 1, 1) for v in x)
    edge = lane_iota(a.shape[0]) == LANES - 1
    return (jnp.where(edge, b, a), jnp.where(edge, a, b))


def west_of(x):
    a, b = (pltpu.roll(v, 1, 1) for v in x)
    edge = lane_iota(a.shape[0]) == 0
    return (jnp.where(edge, b, a), jnp.where(edge, a, b))


def north_of(x):
    return tuple(pltpu.roll(v, v.shape[0] - 1, 0) for v in x)


def south_of(x):
    return tuple(pltpu.roll(v, 1, 0) for v in x)


def lift(fn):
    return lambda *pairs: tuple(fn(*vs) for vs in zip(*pairs))


sub2 = lift(lambda u, v: u - v)


def step_forward(h, e, n, w):
    de = sub2(east_of(e), west_of(e))
    dn = sub2(north_of(n), south_of(n))
    h = lift(lambda w_, h_, a, b: w_ * (h_ - (0.5 * gravity) * (a + b)))(w, h, de, dn)
    se = sub2(east_of(h), west_of(h))
    sn = sub2(north_of(h), south_of(h))
    keep = 1.0 - drag_rate
    e_new = lift(lambda w_, e_, n_, s: w_ * (keep * e_ - (0.5 * gravity) * s + coriolis * n_))(w, e, n, se)
    n_new = lift(lambda w_, e_, n_, s: w_ * (keep * n_ - (0.5 * gravity) * s - coriolis * e_))(w, e, n, sn)
    return h, e_new, n_new


def step_adjoint(h, e, n, w):
    we = lift(lambda a, b: a * b)(w, e)
    wn = lift(lambda a, b: a * b)(w, n)
    de = sub2(east_of(we), west_of(we))
    dn = sub2(north_of(wn), south_of(wn))
    hw = lift(lambda w_, h_, a, b: w_ * (h_ + (0.5 * gravity) * (a + b)))(w, h, de, dn)
    se = sub2(east_of(hw), west_of(hw))
    sn = sub2(north_of(hw), south_of(hw))
    keep = 1.0 - drag_rate
    e_new = lift(lambda a, b, s: keep * a - coriolis * b + (0.5 * gravity) * s)(we, wn, se)
    n_new = lift(lambda a, b, s: keep * b + coriolis * a + (0.5 * gravity) * s)(we, wn, sn)
    return hw, e_new, n_new


def slot_mask(rows, width, count, offset):
    lane = lane_iota(rows)
    mask = None
    for slot in range(count):
        start = 2 * width * slot + offset
        here = (lane >= start) & (lane < start + width)
        mask = here if mask is None else mask | here
    return mask


def pack_edges(fields, width):
    lane = lane_iota(fields[0].shape[0])
    out = jnp.zeros_like(fields[0])
    for slot, field in enumerate(fields):
        start = 2 * width * slot
        rolled = pltpu.roll(field, (start + width) % LANES, 1)
        out = jnp.where((lane >= start) & (lane < start + 2 * width), rolled, out)
    return out


def unpack_edge(packed, width, slot):
    lane = lane_iota(packed.shape[0])
    rolled = pltpu.roll(packed, (-width - 2 * width * slot) % LANES, 1)
    return jnp.where((lane < width) | (lane >= LANES - width), rolled, 0.0)


def split_bf16(x):
    high = x.astype(BF16)
    rest = x - high.astype(F32)
    middle = rest.astype(BF16)
    low = (rest - middle.astype(F32)).astype(BF16)
    return jnp.concatenate([high, middle, low], axis=0)


def permute_columns(x, select):
    rows = x.shape[0]
    y = jnp.dot(split_bf16(x), select, preferred_element_type=F32)
    return (y[2 * rows :] + y[rows : 2 * rows]) + y[:rows]


def store_shifted(ref, row, pair):
    for dx, shifted in enumerate((west_of(pair), pair, east_of(pair))):
        for tile in range(2):
            ref[tile, row, 16 * dx : 16 * dx + 16, :] = shifted[tile].astype(BF16)


def patch(ref, row):
    return jnp.concatenate([ref[tile, row : row + 3].reshape(144, LANES) for tile in range(2)], axis=1)


def conv_row(weight, ref, row):
    y = jnp.dot(weight, patch(ref, row), preferred_element_type=F32)
    return (y[:, :LANES], y[:, LANES:])


def contract(left, right):
    return lax.dot_general(left, right, (((1,), (1,)), ((), ())), preferred_element_type=F32)


def kernel(
    sizes,
    temp,
    height,
    flow,
    land_sea,
    fold,
    w_first,
    w_second,
    w_third,
    temp_bar,
    height_bar,
    flow_bar,
    temp_out,
    height_out,
    flow_out,
    first_out,
    second_out,
    third_out,
    surf,
    trac,
    inputs,
    wet_i,
    bar_t,
    bar_h,
    bar_f,
    fold_s,
    w1_raw,
    w2_raw,
    w3_raw,
    w_rows,
    w_flip,
    msg_out,
    msg_in,
    fold_surf,
    fold_trac,
    select_in,
    select_out,
    g3_rows,
    xs1,
    xs2,
    xs3,
    gs1,
    gs2,
    gs3,
    act1,
    act2,
    back,
    sg,
    tg,
    back_out,
    back_in,
    back_surf,
    back_trac,
    unfold_surf,
    unfold_trac,
    unfold_edge,
    halves,
    half_in,
    plane_in,
    column_in,
    totals,
    load_sem,
    f_send,
    f_recv,
    m_send,
    m_recv,
    fold_send,
    fold_recv,
    b_send,
    b_recv,
    bm_send,
    bm_recv,
    unfold_send,
    unfold_recv,
    pair_send,
    pair_recv,
    plane_send,
    plane_recv,
    column_send,
    column_recv,
):
    nlon, nlat, nens = sizes
    lon, lat, ens = lax.axis_index("lon"), lax.axis_index("lat"), lax.axis_index("ens")
    top = nlat - 1
    left, right = lax.rem(lon + nlon - 1, nlon), lax.rem(lon + 1, nlon)
    nz, ny = nlon // 2, nlat // 2
    core, z = lax.rem(lat, 2), lax.rem(lon, nz)
    plane = 2 * ny * nens
    place = (ens * 2 + lon // nz) * ny + lat // 2

    def remote(src, dst, send, recv, **device):
        return pltpu.make_async_remote_copy(
            src_ref=src, dst_ref=dst, send_sem=send, recv_sem=recv, device_id=device, device_id_type=MESH
        )

    barrier = pltpu.get_barrier_semaphore()

    def greet(**device):
        pl.semaphore_signal(barrier, inc=1, device_id=device, device_id_type=MESH)

    def bits(value, size):
        return [lax.rem(value // 2**k, 2) for k in range(size.bit_length() - 1)]

    def flip(value, digits, mask):
        return value + sum((1 - 2 * digit) * 2**k for k, digit in enumerate(digits) if mask >> k & 1)

    def reach(mask):
        return (0, 1, 2, 3, 4, 3, 2, 3)[mask] if mask < 8 else 1 + reach(mask - 8)

    def plane_reach(mask):
        return sum((0, 1, 2, 1)[part] for part in (mask // ny, mask % ny))

    x, y = ens * 2 + lon // nz, lat // 2
    x_bits, y_bits, lon_bits = bits(x, 2 * nens), bits(y, ny), bits(lon, nlon)
    plane_masks = sorted(range(1, plane), key=plane_reach, reverse=True)
    column_masks = sorted(range(1, nz), key=reach, reverse=True)
    lon_masks = sorted(range(1, nlon), key=reach, reverse=True)

    def plane_peer(mask):
        px, py = flip(x, x_bits, mask // ny), flip(y, y_bits, mask % ny)
        device = dict(lon=lax.rem(px, 2) * nz + z, lat=py * 2 + core, ens=px // 2)
        return px * ny + py, device

    def lon_peer(mask):
        return flip(lon, lon_bits, mask)


    @pl.when(lat == top)
    def _():
        for mask in lon_masks:
            greet(lon=lon_peer(mask))

    for mask in plane_masks:
        greet(**plane_peer(mask)[1])
    for mask in column_masks:
        greet(lon=lon_peer(mask))
    greet(lon=left)
    greet(lon=right)

    @pl.when(lat > 0)
    def _():
        greet(lat=lat - 1)
        greet(lon=left, lat=lat - 1)
        greet(lon=right, lat=lat - 1)

    @pl.when(lat < top)
    def _():
        greet(lat=lat + 1)
        greet(lon=left, lat=lat + 1)
        greet(lon=right, lat=lat + 1)

    loads = [
        (temp.at[0], trac.at[0, :, 8:24, :]),
        (height.at[0], surf.at[0, 0, 16:32, :]),
        (flow.at[0], surf.at[0, 1:3, 16:32, :]),
        (land_sea, wet_i),
        (fold, fold_s),
        (w_first, w1_raw),
        (w_second, w2_raw),
        (w_third, w3_raw),
        (temp_bar.at[0], bar_t),
        (height_bar.at[0], bar_h),
        (flow_bar.at[0], bar_f),
    ]
    loads = [pltpu.make_async_copy(src, dst, load_sem.at[k]) for k, (src, dst) in enumerate(loads)]
    for load in loads:
        load.start()

    inputs[:, 32 * (HCH + 1) :, :] = jnp.zeros((2, 32 * (15 - HCH), LANES), F32)
    for ref, rows in ((gs3, 20), (gs2, 22), (gs1, 24)):
        for tile in range(2):
            for row in (0, 1, rows - 2, rows - 1):
                ref[tile, row] = jnp.zeros((48, LANES), BF16)
    back[...] = jnp.zeros_like(back)
    for ref in (unfold_surf, unfold_trac):
        ref[lon, 24:32, :] = jnp.zeros((8, LANES), F32)
    unfold_edge[:, 24:32, :] = jnp.zeros((2, 8, LANES), F32)

    @pl.when(lat == 0)
    def _():
        surf[:, :, 0:16, :] = jnp.zeros((2, 4, 16, LANES), F32)
        trac[:, :, 0:8, :] = jnp.zeros((2, LEV, 8, LANES), F32)
        back_in[:, 0] = jnp.zeros((2, 2, 16, LANES), F32)
        back_surf[0] = jnp.zeros((3, 16, LANES), F32)
        back_trac[0] = jnp.zeros((LEV, 8, LANES), F32)

    @pl.when(lat == top)
    def _():
        surf[:, :, 32:48, :] = jnp.zeros((2, 4, 16, LANES), F32)
        trac[:, :, 24:32, :] = jnp.zeros((2, LEV, 8, LANES), F32)
        back_in[:, 2] = jnp.zeros((2, 2, 16, LANES), F32)
        back_surf[1] = jnp.zeros((3, 16, LANES), F32)
        back_trac[1] = jnp.zeros((LEV, 8, LANES), F32)

    for k in (1, 2, 3, 0):
        loads[k].wait()
    surf[0, 3, 16:32, :] = wet_i[...].astype(F32)
    msg_out[0] = pack_edges([surf[0, f, 16:32, :] for f in range(4)], RIM)
    msg_out[1] = pack_edges([trac[0, c, 8:24, :] for c in range(LEV)], TRIM)

    def lat_copies(up):
        to = 1 if up else -1
        rows_s = slice(0, 16) if up else slice(32, 48)
        rows_t = (slice(16, 24), slice(0, 8)) if up else (slice(8, 16), slice(24, 32))
        slot = 0 if up else 2
        return (
            remote(surf.at[0, :, 16:32, :], surf.at[0, :, rows_s, :], f_send.at[slot], f_recv.at[slot], lat=lat + to),
            remote(
                trac.at[0, :, rows_t[0], :],
                trac.at[0, :, rows_t[1], :],
                f_send.at[slot + 1],
                f_recv.at[slot + 1],
                lat=lat + to,
            ),
        )

    def edge_copy(side, shift):
        slot = 3 * side + 1 - shift
        return remote(
            msg_out, msg_in.at[side, 1 - shift], m_send.at[slot], m_recv.at[slot], lon=(right, left)[side], lat=lat + shift
        )

    def lon_copy(ref, mask, send, recv, arrival=False):
        peer = lon_peer(mask)
        return remote(ref.at[lon], ref.at[peer if arrival else lon], send.at[mask], recv.at[mask], lon=peer)

    def ghost_rows(width, count):
        full = [(f, m) for f in range(min(count, CL)) for m in range(width)]
        return full + [(f, 0) for f in range(CL, count)]

    @pl.when(lat == top)
    def _():
        for row, (f, m) in enumerate(ghost_rows(RIM, 4)):
            fold_surf[lon, row : row + 1, :] = surf[0, f, 31 - m : 32 - m, :]
        for row, (c, m) in enumerate(ghost_rows(TRIM, LEV)):
            fold_trac[lon, row : row + 1, :] = trac[0, c, 23 - m : 24 - m, :]

    pl.semaphore_wait(
        barrier,
        (plane - 1)
        + (nz - 1)
        + 2
        + 3 * (lat > 0).astype(jnp.int32)
        + 3 * (lat < top).astype(jnp.int32)
        + (nlon - 1) * (lat == top).astype(jnp.int32),
    )

    def for_lat(fn):
        pl.when(lat > 0)(functools.partial(fn, -1))
        fn(0)
        pl.when(lat < top)(functools.partial(fn, 1))

    def start_forward(shift):
        if shift:
            for copy in lat_copies(shift > 0):
                copy.start()
        for side in range(2):
            edge_copy(side, shift).start()

    for_lat(start_forward)

    @pl.when(lat == top)
    def _():
        for mask in lon_masks:
            lon_copy(fold_surf, mask, fold_send.at[0], fold_recv.at[0]).start()

    @pl.when(lat == top)
    def _():
        for mask in lon_masks:
            lon_copy(fold_trac, mask, fold_send.at[1], fold_recv.at[1]).start()

    for k in range(4, 11):
        loads[k].wait()
    raw1 = w1_raw[...].astype(F32)
    w_rows[...] = jnp.zeros_like(w_rows)
    for tap in range(9):
        w_rows[0, :, 16 * tap : 16 * tap + CL] = raw1[:, 11 * tap : 11 * tap + CL]
        w_rows[0, :, 16 * tap + HCH : 16 * tap + HCH + 1] = raw1[:, 11 * tap + CL : 11 * tap + CL + 1]
    w_rows[1, :, 0:144] = w2_raw[...].astype(F32)
    w_rows[2, 0:CL, 0:144] = w3_raw[...].astype(F32)
    for layer in range(3):
        first = jnp.transpose(w_rows[layer, :, 0:128])
        second = jnp.transpose(w_rows[layer, :, 128:256])
        for tap in range(9):
            block = second[0:16, :] if tap == 8 else first[16 * tap : 16 * tap + 16, :]
            w_flip[layer, :, 16 * (8 - tap) : 16 * (8 - tap) + 16] = block
    weight1 = w_rows[0, :, 0:144].astype(BF16)
    weight2 = w_rows[1, :, 0:144].astype(BF16)
    flip1, flip2, flip3 = (w_flip[layer].astype(BF16) for layer in range(3))

    wet_own = surf[0, 3, 16:32, :]
    g3_rows[16 * CL :, :] = jnp.zeros((16 * (16 - CL), LANES), F32)
    for c in range(CL):
        g3_rows[16 * c : 16 * c + 16, :] = closure_gain * wet_own * bar_t[c]
    for row in range(16):
        own = g3_rows[pl.ds(row, 16, stride=16), :]
        store_shifted(gs3, row + 2, (own, jnp.zeros_like(own)))

    shift_s = fold_s[0] + 1
    base = shift_s - (LANES + RIM) - LANES * lon + LANES * (2 * nlon)
    tile0 = base // LANES
    offset = shift_s - 1 - LANES * lon + LANES * (2 * nlon) - LANES * tile0

    def mirrored(ref):
        return jnp.concatenate([ref[lax.rem(tile0 + j, nlon)] for j in range(3)], axis=1)

    @pl.when(lat == top)
    def _():
        source = lax.broadcasted_iota(jnp.int32, (3 * LANES, 2 * LANES), 0)
        column = lax.broadcasted_iota(jnp.int32, (3 * LANES, 2 * LANES), 1)
        column = jnp.where(column < LANES + LANES // 2, column, column - 2 * LANES)
        select_in[...] = jnp.where(source + column == offset, 1.0, 0.0).astype(BF16)
        lane = lax.broadcasted_iota(jnp.int32, (LANES, LANES), 0)
        column = lax.broadcasted_iota(jnp.int32, (LANES, LANES), 1)
        halo = jnp.where(lane < LANES // 2, lane + LANES, lane - LANES)
        for k, at in enumerate((lane, halo)):
            for j in range(3):
                first = LANES * (3 * k + j)
                select_out[first : first + LANES, :] = jnp.where(at + LANES * j + column == offset, 1.0, 0.0).astype(
                    BF16
                )

    left_s = slot_mask(16, RIM, 4, 0)
    left_t = slot_mask(16, TRIM, LEV, 0)

    def wait_forward(shift):
        k = shift + 1
        if shift:
            for copy in lat_copies(shift < 0):
                copy.wait_recv()
        for side in range(2):
            edge_copy(side, -shift).wait_recv()
        packed = jnp.where(left_s, msg_in[0, k, 0], msg_in[1, k, 0])
        for f in range(4):
            surf[1, f, 16 * k : 16 * k + 16, :] = unpack_edge(packed, RIM, f)
        packed = jnp.where(left_t, msg_in[0, k, 1], msg_in[1, k, 1])
        rows, at = ((slice(8, 16), 0), (slice(0, 16), 8), (slice(0, 8), 24))[k]
        packed = packed[rows]
        for c in range(LEV):
            trac[1, c, at : at + packed.shape[0], :] = unpack_edge(packed, TRIM, c)

    for_lat(wait_forward)

    @pl.when(lat == top)
    def _():
        for mask in lon_masks:
            lon_copy(fold_surf, mask, fold_send.at[0], fold_recv.at[0], True).wait_recv()
        window = jnp.concatenate([mirrored(fold_surf), jnp.zeros((8, 3 * LANES), F32)], axis=0)
        ghost = permute_columns(window, select_in[...])
        for f in range(4):
            rows = ghost[RIM * f : RIM * f + RIM]
            rows = -rows if f in (1, 2) else rows
            for tile in range(2):
                surf[tile, f, 32 : 32 + RIM, :] = rows[:, LANES * tile : LANES * tile + LANES]

    h, e, n, wet = (tuple(surf[tile, f] for tile in range(2)) for f in range(4))
    for _ in range(SUB):
        h, e, n = step_forward(h, e, n, wet)
    new_e, new_n = e[0][16:32], n[0][16:32]

    for tile in range(2):
        for c in range(LEV):
            inputs[tile, 32 * c : 32 * c + 32, :] = trac[tile, c]
        inputs[tile, 32 * HCH : 32 * HCH + 32, :] = h[tile][8:40]

    def activate(weight, xs, act_ref, out, rows):
        for row in rows:
            act = lift(jnp.tanh)(conv_row(weight, xs, row))
            for tile in range(2):
                act_ref[tile, row] = act[tile]
            store_shifted(out, row, act)

    def weight_sum(total, gs, xs, rows):
        for row in rows:
            grad = jnp.concatenate([gs[tile, row + 2, 16:32, :] for tile in range(2)], axis=1)
            total = total + contract(grad, patch(xs, row))
        return total

    def back_layer(weight, gs, act_ref, out, rows):
        for row in rows:
            grad = conv_row(weight, gs, row)
            act = tuple(act_ref[tile, row] for tile in range(2))
            store_shifted(out, row + 2, lift(lambda g, a: g * (1.0 - a * a))(grad, act))

    def closure(ends, sums):
        rows = [range(*pair) for pair in ends]
        for row in rows[0]:
            store_shifted(xs1, row, tuple(inputs[tile, pl.ds(5 + row, 16, stride=32), :] for tile in range(2)))
        activate(weight1, xs1, act1, xs2, rows[1])
        activate(weight2, xs2, act2, xs3, rows[2])
        back_layer(flip3, gs3, act2, gs2, rows[2])
        sum3 = weight_sum(sums[2], gs3, xs3, rows[3])
        back_layer(flip2, gs2, act1, gs1, rows[4])
        sum2 = weight_sum(sums[1], gs2, xs2, rows[2])
        sum1 = weight_sum(sums[0], gs1, xs1, rows[4])
        return sum1, sum2, sum3

    split = (19, 17, 15, 13, 15)
    sums = closure([(0, at) for at in split], (jnp.zeros((16, 144), F32),) * 3)

    @pl.when(lat == top)
    def _():
        for mask in lon_masks:
            lon_copy(fold_trac, mask, fold_send.at[1], fold_recv.at[1], True).wait_recv()
        ghost = permute_columns(mirrored(fold_trac), select_in[...])
        for c in range(LEV):
            first, count = (TRIM * c, TRIM) if c < CL else (TRIM * CL + c - CL, 1)
            for tile in range(2):
                rows = ghost[first : first + count, LANES * tile : LANES * tile + LANES]
                trac[tile, c, 24 : 24 + count, :] = rows
                inputs[tile, 32 * c + 24 : 32 * c + 24 + count, :] = rows

    sum1, sum2, sum3 = closure(list(zip(split, (22, 20, 18, 16, 20))), sums)

    tail = jnp.concatenate([sum1[:, 128:144], sum2[:, 128:144], sum3[:, 128:144], jnp.zeros((16, 80), F32)], axis=1)
    tail = jnp.concatenate([tail[0:6, 0:48], tail[6:12, 0:48], tail[10:16, 0:32]], axis=1)
    rows = jnp.concatenate([sum1[:, :128], sum2[:, :128], sum3[0:CL, :128], tail], axis=0)
    halves[0] = rows[0:24]
    halves[1] = rows[24:48]

    def half_copy():
        return remote(halves.at[1 - core], half_in, pair_send.at[0], pair_recv.at[0], lat=lat + 1 - 2 * core)

    def plane_copy(mask, arrival=False):
        other, device = plane_peer(mask)
        slot = other if arrival else place
        return remote(plane_in.at[place], plane_in.at[slot], plane_send.at[mask], plane_recv.at[mask], **device)

    def column_copy(mask, arrival=False):
        peer = lon_peer(mask)
        slot = lax.rem(peer, nz) if arrival else z
        return remote(column_in.at[z], column_in.at[slot], column_send.at[mask], column_recv.at[mask], lon=peer)

    def total_copy(arrival=False):
        slot = 1 - core if arrival else core
        return remote(totals.at[core], totals.at[slot], pair_send.at[1], pair_recv.at[1], lat=lat + 1 - 2 * core)

    def sum_slots(ref, count):
        total = ref[0]
        for k in range(1, count):
            total = total + ref[k]
        return total

    half_copy().start()

    half_copy().wait_recv()
    column_in[z] = halves[core] + half_in[...]
    for mask in column_masks:
        column_copy(mask).start()

    for row in range(22):
        grad = conv_row(flip1, gs1, row)
        for tile in range(2):
            back[tile, pl.ds(5 + row, 16, stride=32), :] = grad[tile]

    lane16 = lane_iota(16)
    zero8 = jnp.zeros((8, LANES), F32)
    sum_e = jnp.zeros((16, LANES), F32)
    sum_n = jnp.zeros((16, LANES), F32)
    for c in range(LEV):
        bar = bar_t[c]
        wb = wet_own * bar
        own, halo = trac[0, c, 8:24, :], trac[1, c, 8:24, :]
        ahead = jnp.where(lane16 == LANES - 1, pltpu.roll(halo, LANES - 1, 1), pltpu.roll(own, LANES - 1, 1))
        behind = jnp.where(lane16 == 0, pltpu.roll(halo, 1, 1), pltpu.roll(own, 1, 1))
        sum_e = sum_e + wb * (ahead - behind)
        sum_n = sum_n + wb * (trac[0, c, 9:25, :] - trac[0, c, 7:23, :])
        qe = (0.5 * advection) * new_e * wb
        qn = (0.5 * advection) * new_n * wb
        wd = diffusion * wb
        up = pltpu.roll(wd + qe, LANES - 1, 1)
        down = pltpu.roll(wd - qe, 1, 1)
        middle = (
            bar - 4.0 * wd + jnp.where(lane16 < LANES - 1, up, 0.0) + jnp.where(lane16 > 0, down, 0.0)
        )
        side = jnp.where(lane16 == LANES - 1, up, jnp.where(lane16 == 0, down, 0.0))
        above = pltpu.roll(jnp.concatenate([zero8, wd + qn, zero8], axis=0), 31, 0)
        below = pltpu.roll(jnp.concatenate([zero8, wd - qn, zero8], axis=0), 1, 0)
        main = jnp.concatenate([zero8, middle, zero8], axis=0) + above + below
        side = jnp.concatenate([zero8, side, zero8], axis=0)
        if c < CL:
            main = main + back[0, 32 * c : 32 * c + 32, :]
            side = side + back[1, 32 * c : 32 * c + 32, :]
        tg[0, c] = main
        tg[1, c] = side

    def lat_back(up):
        to = 1 if up else -1
        rows_s = slice(32, 48) if up else slice(0, 16)
        rows_t = slice(24, 32) if up else slice(0, 8)
        slot = 0 if up else 1
        return (
            remote(sg.at[0, :, rows_s, :], back_surf.at[slot], b_send.at[0, slot], b_recv.at[0, slot], lat=lat + to),
            remote(tg.at[0, :, rows_t, :], back_trac.at[slot], b_send.at[1, slot], b_recv.at[1, slot], lat=lat + to),
        )

    def pack_ghosts(grads, first, count, width, out, edge):
        for row, (f, m) in enumerate(ghost_rows(width, count)):
            out[lon, row : row + 1, :] = grads[0, f, first + m : first + m + 1, :]
            edge[row : row + 1, :] = grads[1, f, first + m : first + m + 1, :]
        out[lon, 32:40, :] = pack_edges([edge[8 * g : 8 * g + 8, :] for g in range(4)], width)

    @pl.when(lat == top)
    def _():
        pack_ghosts(tg, 24, LEV, TRIM, unfold_trac, unfold_edge.at[0])

    pl.when(lat > 0)(lambda: lat_back(False)[1].start())
    pl.when(lat < top)(lambda: lat_back(True)[1].start())

    def own_rows(x):
        zero16 = jnp.zeros((16, LANES), F32)
        return (jnp.concatenate([zero16, x, zero16], axis=0), jnp.zeros((48, LANES), F32))

    e = own_rows(bar_f[0] - (0.5 * advection) * sum_e)
    n = own_rows(bar_f[1] - (0.5 * advection) * sum_n)
    rim = tuple(jnp.concatenate([zero8, back[tile, 32 * HCH : 32 * HCH + 32, :], zero8], axis=0) for tile in range(2))
    h = lift(lambda a, b: a + b)(rim, own_rows(bar_h[...]))
    wet = tuple(surf[tile, 3] for tile in range(2))
    for index in range(SUB):
        h, e, n = step_adjoint(h, e, n, wet)
    for f, pair in enumerate((h, e, n)):
        for tile in range(2):
            sg[tile, f] = pair[tile]

    for block in range(3):
        back_out[block, 0] = pack_edges([sg[1, f, 16 * block : 16 * block + 16, :] for f in range(3)], RIM)
        if block == 1:
            fields = [tg[1, c, 8:24, :] for c in range(LEV)]
        elif block == 0:
            fields = [jnp.concatenate([zero8, tg[1, c, 0:8, :]], axis=0) for c in range(LEV)]
        else:
            fields = [jnp.concatenate([tg[1, c, 24:32, :], zero8], axis=0) for c in range(LEV)]
        back_out[block, 1] = pack_edges(fields, TRIM)

    def edge_back(side, block):
        return remote(
            back_out.at[block],
            back_in.at[side, 2 - block],
            bm_send.at[side, 2 - block],
            bm_recv.at[side, 2 - block],
            lon=(right, left)[side],
            lat=lat + block - 1,
        )

    @pl.when(lat == top)
    def _():
        pack_ghosts(sg, 32, 3, RIM, unfold_surf, unfold_edge.at[1])
        for mask in lon_masks:
            lon_copy(unfold_surf, mask, unfold_send.at[0], unfold_recv.at[0]).start()
        for mask in lon_masks:
            lon_copy(unfold_trac, mask, unfold_send.at[1], unfold_recv.at[1]).start()

    def start_back(shift):
        if shift:
            lat_back(shift > 0)[0].start()
        for side in range(2):
            edge_back(side, shift + 1).start()

    for_lat(start_back)

    right_s = slot_mask(16, RIM, 3, RIM)
    right_t = slot_mask(16, TRIM, LEV, TRIM)

    def sent_forward(shift):
        if shift:
            for copy in lat_copies(shift > 0):
                copy.wait_send()
        for side in range(2):
            edge_copy(side, shift).wait_send()

    for_lat(sent_forward)

    @pl.when(lat == top)
    def _():
        for mask in lon_masks:
            for part, ref in enumerate((fold_surf, fold_trac)):
                lon_copy(ref, mask, fold_send.at[part], fold_recv.at[part]).wait_send()

    half_copy().wait_send()
    for mask in column_masks:
        column_copy(mask).wait_send()

    for mask in column_masks:
        column_copy(mask, True).wait_recv()
    plane_in[place] = sum_slots(column_in, nz)
    for mask in plane_masks:
        plane_copy(mask).start()

    def wait_back(shift):
        if shift:
            for copy in lat_back(shift < 0):
                copy.wait_recv()
        for side in range(2):
            edge_back(side, 1 - shift).wait_recv()

    for_lat(wait_back)

    from_left = back_in[0, 0] + back_in[0, 1] + back_in[0, 2]
    from_right = back_in[1, 0] + back_in[1, 1] + back_in[1, 2]
    packed = jnp.where(right_s, from_left[0], from_right[0])
    for f in range(3):
        total = sg[0, f, 16:32, :] + back_surf[0, f] + back_surf[1, f] + unpack_edge(packed, RIM, f)
        if f == 0:
            height_out[0] = total
        else:
            flow_out[0, f - 1] = total
    packed = jnp.where(right_t, from_left[1], from_right[1])
    for c in range(LEV):
        ghosts = jnp.concatenate([back_trac[0, c], back_trac[1, c]], axis=0)
        temp_out[0, c] = tg[0, c, 8:24, :] + ghosts + unpack_edge(packed, TRIM, c)

    def sent_back(shift):
        if shift:
            for copy in lat_back(shift > 0):
                copy.wait_send()
        for side in range(2):
            edge_back(side, shift + 1).wait_send()

    for_lat(sent_back)

    @pl.when(lat == top)
    def _():
        for mask in lon_masks:
            for part, ref in enumerate((unfold_surf, unfold_trac)):
                lon_copy(ref, mask, unfold_send.at[part], unfold_recv.at[part]).wait_send()

    for mask in plane_masks:
        plane_copy(mask, True).wait_recv()
    totals[core] = sum_slots(plane_in, plane)
    total_copy().start()
    for mask in plane_masks:
        plane_copy(mask).wait_send()

    @pl.when(lat == top)
    def _():
        def unfold(ref, width):
            tiles = [ref[lax.rem(tile0 + j, nlon)] for j in range(3)]
            edges = [
                jnp.concatenate([unpack_edge(tile[32:40], width, g) for g in range(4)], axis=0) for tile in tiles
            ]
            return permute_columns(jnp.concatenate([tile[0:32] for tile in tiles] + edges, axis=1), select_out[...])

        for mask in lon_masks:
            lon_copy(unfold_trac, mask, unfold_send.at[1], unfold_recv.at[1], True).wait_recv()
        ghost = unfold(unfold_trac, TRIM)
        for row, (c, m) in enumerate(ghost_rows(TRIM, LEV)):
            temp_out[0, c, 15 - m : 16 - m, :] = temp_out[0, c, 15 - m : 16 - m, :] + ghost[row : row + 1]
        for mask in lon_masks:
            lon_copy(unfold_surf, mask, unfold_send.at[0], unfold_recv.at[0], True).wait_recv()
        ghost = unfold(unfold_surf, RIM)
        for row, (f, m) in enumerate(ghost_rows(RIM, 3)):
            if f == 0:
                height_out[0, 15 - m : 16 - m, :] = height_out[0, 15 - m : 16 - m, :] + ghost[row : row + 1]
            else:
                flow_out[0, f - 1, 15 - m : 16 - m, :] = flow_out[0, f - 1, 15 - m : 16 - m, :] - ghost[row : row + 1]

    total_copy(True).wait_recv()
    scale = 1.0 / math.sqrt(nens * nlat * 16 * nlon * LANES)
    rows = jnp.concatenate([totals[0], totals[1]], axis=0) * scale
    tail = rows[32 + CL : 48]
    tail = jnp.concatenate(
        [tail[:, 0:48], tail[:, 48:96], jnp.concatenate([tail[2:6, 96:128], jnp.zeros((4, 16), F32)], axis=1)], axis=0
    )
    for layer, out in ((1, second_out), (2, third_out)):
        count = out.shape[0]
        out[:, 0:128] = rows[16 * layer : 16 * layer + count]
        out[:, 128:144] = tail[0:count, 16 * layer : 16 * layer + 16]
    for tap in range(9):
        block = tail[:, 0:16] if tap == 8 else rows[0:16, 16 * tap : 16 * tap + 16]
        first_out[:, 11 * tap : 11 * tap + CL] = block[:, 0:CL]
        first_out[:, 11 * tap + CL : 11 * tap + CL + 1] = block[:, HCH : HCH + 1]

    total_copy().wait_send()


def hand_over(*refs):
    sources, targets, sem = refs[:6], refs[6:12], refs[12]
    copies = [pltpu.make_async_copy(src, dst, sem.at[k]) for k, (src, dst) in enumerate(zip(sources, targets))]
    for copy in copies:
        copy.start()
    for copy in copies:
        copy.wait()


def solution(mesh):
    nlon, nlat, nens = (mesh.shape[axis] for axis in ("lon", "lat", "ens"))
    plane = nlat * nens

    def local(temp, height, flow, land_sea, fold, w_first, w_second, w_third, temp_bar, height_bar, flow_bar):
        vmem = pltpu.VMEM
        dma = pltpu.SemaphoreType.DMA
        scratch = [
            vmem((2, 4, 48, LANES), F32),
            vmem((2, LEV, 32, LANES), F32),
            vmem((2, 16 * 32, LANES), F32),
            vmem((16, LANES), jnp.int32),
            vmem((LEV, 16, LANES), F32),
            vmem((16, LANES), F32),
            vmem((2, 16, LANES), F32),
            pltpu.SMEM(fold.shape, jnp.int32),
            vmem(w_first.shape, BF16),
            vmem(w_second.shape, BF16),
            vmem(w_third.shape, BF16),
            vmem((3, 16, 256), F32),
            vmem((3, 16, 144), F32),
            vmem((2, 16, LANES), F32),
            vmem((2, 3, 2, 16, LANES), F32),
            vmem((nlon, 40, LANES), F32),
            vmem((nlon, 32, LANES), F32),
            vmem((3 * LANES, 2 * LANES), BF16),
            vmem((6 * LANES, LANES), BF16),
            vmem((16 * 16, LANES), F32),
            vmem((2, 22, 48, LANES), BF16),
            vmem((2, 20, 48, LANES), BF16),
            vmem((2, 18, 48, LANES), BF16),
            vmem((2, 24, 48, LANES), BF16),
            vmem((2, 22, 48, LANES), BF16),
            vmem((2, 20, 48, LANES), BF16),
            vmem((2, 20, 16, LANES), F32),
            vmem((2, 18, 16, LANES), F32),
            vmem((2, 16 * 32, LANES), F32),
            vmem((2, 3, 48, LANES), F32),
            vmem((2, LEV, 32, LANES), F32),
            vmem((3, 2, 16, LANES), F32),
            vmem((2, 3, 2, 16, LANES), F32),
            vmem((2, 3, 16, LANES), F32),
            vmem((2, LEV, 8, LANES), F32),
            vmem((nlon, 40, LANES), F32),
            vmem((nlon, 40, LANES), F32),
            vmem((2, 32, LANES), F32),
            vmem((2, 24, LANES), F32),
            vmem((24, LANES), F32),
            vmem((plane, 24, LANES), F32),
            vmem((nlon // 2, 24, LANES), F32),
            vmem((2, 24, LANES), F32),
            dma((11,)),
            dma((4,)),
            dma((4,)),
            dma((6,)),
            dma((6,)),
            dma((2, nlon)),
            dma((2, nlon)),
            dma((2, 2)),
            dma((2, 2)),
            dma((2, 4)),
            dma((2, 4)),
            dma((2, nlon)),
            dma((2, nlon)),
            dma((2,)),
            dma((2,)),
            dma((plane,)),
            dma((plane,)),
            dma((nlon // 2,)),
            dma((nlon // 2,)),
        ]
        out_shape = (
            jax.ShapeDtypeStruct(temp.shape, F32),
            jax.ShapeDtypeStruct(height.shape, F32),
            jax.ShapeDtypeStruct(flow.shape, F32),
            jax.ShapeDtypeStruct(w_first.shape, F32),
            jax.ShapeDtypeStruct(w_second.shape, F32),
            jax.ShapeDtypeStruct(w_third.shape, F32),
        )
        results = pl.pallas_call(
            functools.partial(kernel, (nlon, nlat, nens)),
            out_shape=tuple(pltpu.VMEM(o.shape, F32) for o in out_shape),
            in_specs=[pl.BlockSpec(memory_space=pltpu.HBM)] * 11,
            out_specs=[pl.BlockSpec(memory_space=pltpu.VMEM)] * 6,
            scratch_shapes=scratch,
            compiler_params=pltpu.CompilerParams(
                collective_id=0, has_side_effects=True, vmem_limit_bytes=60 * 1024 * 1024
            ),
        )(temp, height, flow, land_sea, fold, w_first, w_second, w_third, temp_bar, height_bar, flow_bar)
        return pl.pallas_call(
            hand_over,
            out_shape=out_shape,
            in_specs=[pl.BlockSpec(memory_space=pl.ANY)] * 6,
            out_specs=[pl.BlockSpec(memory_space=pltpu.HBM)] * 6,
            scratch_shapes=[dma((6,))],
            compiler_params=pltpu.CompilerParams(vmem_limit_bytes=1024 * 1024),
        )(*results)

    field = P("ens", None, "lat", "lon")
    surface = P("ens", "lat", "lon")
    return jax.shard_map(
        local,
        mesh=mesh,
        in_specs=(field, surface, field, P("lat", "lon"), P(), P(), P(), P(), field, surface, field),
        out_specs=(field, surface, field, P(), P(), P()),
        check_vma=False,
    )
```
